32 devices in a mesh: dp: 8 (over z, x), shard: 4 (over y, core).
Axes of the slice: x: 2, y: 2, z: 4, core: 2. Of those that a mesh axis runs over, the one named last changes fastest.
Arguments:
- tokens: bfloat16 [4096, 1024], P(('dp', 'shard')), may hold values from -6 to 6
- cotangent: bfloat16 [4096, 1024], P(('dp', 'shard')), may hold values from -6 to 6
- query_key: float32 [2, 1024, 1024], P(None, ('dp', 'shard')), may hold values from -0.1875 to 0.1875
- value_gate: float32 [2, 1024, 2048], P(None, ('dp', 'shard')), may hold values from -0.1875 to 0.1875
- output_weight: float32 [2048, 1024], P(('dp', 'shard')), may hold values from -0.125 to 0.125
- gate_up: float32 [2, 1024, 2816], P(None, ('dp', 'shard')), may hold values from -0.1875 to 0.1875
- down_weight: float32 [2816, 1024], P(('dp', 'shard')), may hold values from -0.109375 to 0.109375
- small_params: float32 [35088], replicated, may hold values from -7 to 3
- momentum_query_key: float32 [2, 1024, 1024], P(None, ('dp', 'shard')), may hold values from -80 to 80
- momentum_value_gate: float32 [2, 1024, 2048], P(None, ('dp', 'shard')), may hold values from -80 to 80
- momentum_output: float32 [2048, 1024], P(('dp', 'shard')), may hold values from -80 to 80
- momentum_gate_up: float32 [2, 1024, 2816], P(None, ('dp', 'shard')), may hold values from -80 to 80
- momentum_down: float32 [2816, 1024], P(('dp', 'shard')), may hold values from -80 to 80
- moment_one: float32 [35088], replicated, may hold values from -40 to 40
- moment_two: float32 [35088], replicated, may hold values from 4.096 to 409.6
- seq_lengths: int32 [8, 4], P('dp'), may hold values from 1 to 256, 512 in all within a row
Outputs:
- block_out: bfloat16 [4096, 1024], P(('dp', 'shard'))
- input_grad: bfloat16 [4096, 1024], P(('dp', 'shard'))
- grad_query_key: float32 [2, 1024, 1024], P(None, ('dp', 'shard'))
- grad_value_gate: float32 [2, 1024, 2048], P(None, ('dp', 'shard'))
- grad_output: float32 [2048, 1024], P(('dp', 'shard'))
- grad_gate_up: float32 [2, 1024, 2816], P(None, ('dp', 'shard'))
- grad_down: float32 [2816, 1024], P(('dp', 'shard'))
- step_query_key: float32 [2, 1024, 1024], P(None, ('dp', 'shard'))
- step_value_gate: float32 [2, 1024, 2048], P(None, ('dp', 'shard'))
- step_output: float32 [2048, 1024], P(('dp', 'shard'))
- step_gate_up: float32 [2, 1024, 2816], P(None, ('dp', 'shard'))
- step_down: float32 [2816, 1024], P(('dp', 'shard'))
- new_momentum_query_key: float32 [2, 1024, 1024], P(None, ('dp', 'shard'))
- new_momentum_value_gate: float32 [2, 1024, 2048], P(None, ('dp', 'shard'))
- new_momentum_output: float32 [2048, 1024], P(('dp', 'shard'))
- new_momentum_gate_up: float32 [2, 1024, 2816], P(None, ('dp', 'shard'))
- new_momentum_down: float32 [2816, 1024], P(('dp', 'shard'))
- small_grad: float32 [35088], replicated
- small_step: float32 [35088], replicated
- new_moment_one: float32 [35088], replicated
- new_moment_two: float32 [35088], replicated
The draws below stay inside these ranges and needn't reach their ends.
Inputs may be any that keep to these rules, and one draw needn't show every extreme that they name: `seq_lengths`: each row sums to 512, and its largest length is exactly 256.
All inputs are finite; a program needn't handle non-finite values.
Results may differ from the reference program's by a relative error of at most 0.015.
The reference program's roundings to bfloat16 on the way count: a program that leaves them out, or rounds other values in their place, can miss the bound.
Values may be sent and summed in bfloat16 or wider, within the bound.
A program may use at most 384 MiB of HBM per device.

```python
import math
import jax
import jax.numpy as jnp
import numpy as np
from jax import lax

D = 1024
H = 8
DK = 128
DV = 256
FF = 2816
KCONV = 4
SPAN = 64
NS_STEPS = 2
STEP_COUNT = 10
TOK_DEV = 128
HK = 1024
HV = 2048
TOKENS = 4096
PS = 35088
N_DP = 8
N_SHARD = 4


def draw_small_params(key, part):
    streams = jax.random.split(key, 5)
    projections = jax.random.normal(streams[0], (2 * D * H,), jnp.float32) * D ** (-0.5)
    taps = jax.random.uniform(streams[1], (KCONV * (2 * H * DK + H * DV),), jnp.float32, -0.6, 0.6)
    gains = 1.0 + 0.2 * jax.random.uniform(streams[2], (2 * D + DV,), jnp.float32, -1.0, 1.0)
    a_log = jnp.log(jax.random.uniform(streams[3], (H,), jnp.float32, 1.0, 16.0))
    rates = jnp.exp(jax.random.uniform(streams[4], (H,), jnp.float32, jnp.log(0.001), jnp.log(0.1)))
    dt_bias = rates + jnp.log(-jnp.expm1(-rates))
    return jnp.concatenate([projections, taps, gains, a_log, dt_bias])


def block_scale(own_key, dims, cuts, low, largest):
    loudness = 1.0
    for axis_at, blocks in cuts:
        steps = jax.random.uniform(jax.random.fold_in(jax.random.fold_in(own_key, 6), axis_at), (blocks,), jnp.float32, low / len(cuts), largest / len(cuts))
        loudness = loudness * jnp.repeat(jnp.exp(steps), dims[axis_at] // blocks).reshape((-1,) + (1,) * (len(dims) - 1 - axis_at))
    return loudness


def profile(count, total, reach, lean):
    loads = [(1 << 20) // math.isqrt(rank ** lean) + 1 for rank in range(2, count + 1)]
    surplus, holding = total - reach - (count - 1), [1] * (count - 1)
    while surplus > 0:
        movable = [i for i in range(count - 1) if holding[i] < reach]
        whole, remaining = sum([loads[i] for i in movable]), surplus
        for i in movable:
            addition = min(reach - holding[i], max(1, remaining * loads[i] // whole), surplus)
            holding[i] = holding[i] + addition
            surplus = surplus - addition
    return np.array([reach] + holding)


def uneven(rng, count, total, reach, lean):
    if count == 2:
        one = jax.random.randint(rng, (), max(1, total - reach), min(reach, total - 1) + 1)
        return jnp.stack([one, total - one])
    sizes = jnp.asarray(profile(count, total, reach, lean), jnp.int32)
    twos = (count - 1) // 2
    source_of, receiver = sizes[1:1 + 2 * twos:2], sizes[2:2 + 2 * twos:2]
    room = jnp.minimum(source_of - 1, reach - receiver)
    moved = jax.random.randint(jax.random.fold_in(rng, 1), (twos,), 0, 1 << 20) % (room + 1)
    sizes = sizes.at[1:1 + 2 * twos:2].set(source_of - moved).at[2:2 + 2 * twos:2].set(receiver + moved)
    return sizes[jax.random.permutation(jax.random.fold_in(rng, 2), count)]


def normal_values(key, dims, spread, most, cuts=(), kind=jnp.bfloat16):
    entries = jax.random.normal(key, dims, jnp.float32) * spread
    if len(cuts) > 0:
        entries = block_scale(key, dims, cuts, -0.22, 0.18) * entries
    return jnp.clip(entries, min=-most, max=most).astype(kind)


def setup_inputs(seed: int = 0) -> dict:
    keys = jax.random.split(jax.random.key(seed), 17)
    tokens = normal_values(keys[0], (TOKENS, D), 1.0, 6.0, ((0, 32),))
    cotangent = normal_values(keys[1], (TOKENS, D), 1.0, 6.0, ((0, 32),))
    query_key = normal_values(keys[2], (2, D, HK), D ** -0.5, 0.1875, ((1, 32),), jnp.float32)
    value_gate = normal_values(keys[3], (2, D, HV), D ** -0.5, 0.1875, ((1, 32),), jnp.float32)
    output_weight = normal_values(keys[4], (HV, D), HV ** -0.5, 0.125, ((0, 32),), jnp.float32)
    gate_up = normal_values(keys[5], (2, D, FF), D ** -0.5, 0.1875, ((1, 32),), jnp.float32)
    down_weight = normal_values(keys[6], (FF, D), FF ** -0.5, 0.109375, ((0, 32),), jnp.float32)
    small_params = draw_small_params(jax.random.fold_in(keys[16], 71), 0)
    momentum_query_key = normal_values(keys[8], (2, D, HK), (0.2 * TOKENS ** 0.5), 80.0, ((1, 32),), jnp.float32)
    momentum_value_gate = normal_values(keys[9], (2, D, HV), (0.2 * TOKENS ** 0.5), 80.0, ((1, 32),), jnp.float32)
    momentum_output = normal_values(keys[10], (HV, D), (0.2 * TOKENS ** 0.5), 80.0, ((0, 32),), jnp.float32)
    momentum_gate_up = normal_values(keys[11], (2, D, FF), (0.2 * TOKENS ** 0.5), 80.0, ((1, 32),), jnp.float32)
    momentum_down = normal_values(keys[12], (FF, D), (0.2 * TOKENS ** 0.5), 80.0, ((0, 32),), jnp.float32)
    moment_one = normal_values(keys[13], (PS,), (0.1 * TOKENS ** 0.5), 40.0, (), jnp.float32)
    moment_two = jnp.clip(jnp.exp(jax.random.uniform(keys[14], (PS,), jnp.float32, math.log(4.096), math.log(409.6))), 4.096, 409.6)
    seq_lengths = jax.vmap(lambda own: uneven(own, N_SHARD, N_SHARD * TOK_DEV, 2 * TOK_DEV, 0))(jax.random.split(keys[15], N_DP)).reshape((N_DP, N_SHARD)).astype(jnp.int32)
    return {"tokens": tokens, "cotangent": cotangent, "query_key": query_key, "value_gate": value_gate, "output_weight": output_weight, "gate_up": gate_up, "down_weight": down_weight, "small_params": small_params, "momentum_query_key": momentum_query_key, "momentum_value_gate": momentum_value_gate, "momentum_output": momentum_output, "momentum_gate_up": momentum_gate_up, "momentum_down": momentum_down, "moment_one": moment_one, "moment_two": moment_two, "seq_lengths": seq_lengths}


PRECISION_LEVEL = lax.Precision.HIGHEST
NORM_EPS = 1e-06
GATE_EPS = 1e-05
UNIT_EPS = 1e-06
COEF_A = 3.4445
COEF_B = -4.775
COEF_C = 2.0315
MOMENTUM = 0.95
MUON_RATE = 0.1
MUON_DECAY = 0.01
ADAM_RATE = 0.05
BETA_ONE = 0.9
BETA_TWO = 0.95
ADAM_EPS = 1e-08

@jax.custom_vjp
def low(v):
    return lax.optimization_barrier(v.astype(jnp.bfloat16)).astype(jnp.float32)

@jax.custom_vjp
def low_back(v):
    return v

def low_keep(v):
    return (low(v), None)

def low_pass(kept, grad):
    return (grad,)

def back_keep(v):
    return (v, None)

def back_low(kept, grad):
    return (low(grad),)
low.defvjp(low_keep, low_pass)
low_back.defvjp(back_keep, back_low)

def unpack(packed):
    amounts = [D * H, D * H, KCONV * H * DK, KCONV * H * DK, KCONV * H * DV, D, D, DV, H, H]
    layouts = [(D, H), (D, H), (KCONV, H * DK), (KCONV, H * DK), (KCONV, H * DV), (D,), (D,), (DV,), (H,), (H,)]
    pieces = []
    offset = 0
    for amount, layout in zip(amounts, layouts):
        pieces.append(packed[offset:offset + amount].reshape(layout))
        offset = offset + amount
    return pieces

def rms_norm(values, norm_gain, epsilon):
    return values * lax.rsqrt(lax.optimization_barrier(jnp.mean(values * values, axis=-1, keepdims=True)) + epsilon) * norm_gain

def unit_norm(values):
    return values * lax.rsqrt(lax.optimization_barrier(jnp.sum(values * values, axis=-1, keepdims=True)) + UNIT_EPS)

def product(left_side, right_side):
    return jnp.dot(left_side, right_side, precision=PRECISION_LEVEL, preferred_element_type=jnp.float32)

def short_conv(values, weight, segment):
    summed = weight[KCONV - 1] * values
    for delay in range(1, KCONV):
        shifted = jnp.concatenate([jnp.zeros((delay, values.shape[1]), jnp.float32), values[:-delay]], axis=0)
        shifted_seg = jnp.concatenate([jnp.full((delay,), -1, jnp.int32), segment[:-delay]])
        summed = summed + weight[KCONV - 1 - delay] * jnp.where((shifted_seg == segment)[:, None], shifted, 0.0)
    return jax.nn.silu(summed)

def token_step(memory_state, inputs):
    query_single_row, key_single_row, value_row, decay_row, beta_row, keep_row = inputs
    memory_state = memory_state * (decay_row * keep_row)[:, None, None]
    retrieved_values = jnp.einsum('dx,dxl->dl', key_single_row, memory_state, precision=PRECISION_LEVEL)
    state_update = beta_row[:, None] * (value_row - retrieved_values)
    memory_state = memory_state + key_single_row[:, :, None] * state_update[:, None, :]
    return (memory_state, jnp.einsum('dx,dxl->dl', query_single_row, memory_state, precision=PRECISION_LEVEL))

def block_scan(memory_state, inputs):
    return lax.scan(token_step, memory_state, inputs)

def delta_rule(queries, key_rows, value_rows, decays, beta_gate, keep_mask):
    blocks = queries.shape[0] // SPAN

    def blocked(array):
        return array.reshape((blocks, SPAN) + array.shape[1:])
    initial = jnp.zeros((H, DK, DV), jnp.float32)
    operands = (blocked(queries), blocked(key_rows), blocked(value_rows), blocked(decays), blocked(beta_gate), blocked(keep_mask))
    _, outputs = lax.scan(jax.checkpoint(block_scan), initial, operands)
    return outputs.reshape(queries.shape[0], H, DV)

def mixer(raw_query, raw_keys, raw_value, raw_gate, raw_decay, raw_beta, conv_query, conv_keys, conv_value, gain_out, a_log, dt_bias, segment, keep_mask):
    row_count = raw_query.shape[0]
    queries = unit_norm(short_conv(raw_query, conv_query, segment).reshape(row_count, H, DK)) * DK ** (-0.5)
    key_rows = unit_norm(short_conv(raw_keys, conv_keys, segment).reshape(row_count, H, DK))
    value_rows = short_conv(raw_value, conv_value, segment).reshape(row_count, H, DV)
    beta_gate = jax.nn.sigmoid(raw_beta)
    decays = jnp.exp(-jnp.exp(a_log) * jax.nn.softplus(raw_decay + dt_bias))
    mixed = delta_rule(queries, key_rows, value_rows, decays, beta_gate, keep_mask)
    gated = rms_norm(mixed, gain_out, GATE_EPS) * jax.nn.silu(raw_gate).reshape(row_count, H, DV)
    return gated.reshape(row_count, H * DV)

def group_forward(inputs_x, weights, packed, segment, keep_mask):
    query_key, value_gate, output_weight, gate_up, down_weight = weights
    w_decay, w_beta, conv_query, conv_keys, conv_value, gain_one, gain_two, gain_out, a_log, dt_bias = unpack(packed)
    normed = low(rms_norm(inputs_x, gain_one, NORM_EPS))
    raw_query = low_back(product(normed, low(query_key[0])))
    raw_keys = low_back(product(normed, low(query_key[1])))
    raw_value = low_back(product(normed, low(value_gate[0])))
    raw_gate = low_back(product(normed, low(value_gate[1])))
    raw_decay = low_back(product(normed, low(w_decay)))
    raw_beta = low_back(product(normed, low(w_beta)))
    gated = mixer(raw_query, raw_keys, raw_value, raw_gate, raw_decay, raw_beta, conv_query, conv_keys, conv_value, gain_out, a_log, dt_bias, segment, keep_mask)
    branch = low_back(product(low(gated), low(output_weight)))
    middle = inputs_x + branch
    normed_two = low(rms_norm(middle, gain_two, NORM_EPS))
    gate_proj = low_back(product(normed_two, low(gate_up[0])))
    upper_proj = low_back(product(normed_two, low(gate_up[1])))
    hidden_act = low(jax.nn.silu(gate_proj) * upper_proj)
    return middle + product(hidden_act, low(down_weight))

def orthogonalize(matrix):
    tall = matrix.shape[0] > matrix.shape[1]
    current = matrix.T if tall else matrix
    scaled = low(current / (jnp.sqrt(jnp.sum(current * current)) + 1e-07))
    for iteration in range(NS_STEPS):
        gram = low(product(scaled, scaled.T))
        poly = low(COEF_B * gram + COEF_C * product(gram, gram))
        scaled = low(COEF_A * scaled + product(poly, scaled))
    return scaled.T if tall else scaled

def muon_member(grad_part, momentum_part, master_part):
    new_momentum = MOMENTUM * momentum_part + grad_part
    look_ahead = low(grad_part + MOMENTUM * new_momentum)
    ortho = orthogonalize(look_ahead)
    scale = 0.2 * max(grad_part.shape[0], grad_part.shape[1]) ** 0.5
    return (-MUON_RATE * (scale * ortho + MUON_DECAY * master_part), new_momentum)

def muon_weight(grad_full, momentum_full, master_full):
    if grad_full.ndim == 3:
        first_step, first_mom = muon_member(grad_full[0], momentum_full[0], master_full[0])
        second_step, second_mom = muon_member(grad_full[1], momentum_full[1], master_full[1])
        return (jnp.stack([first_step, second_step]), jnp.stack([first_mom, second_mom]))
    return muon_member(grad_full, momentum_full, master_full)

def reference(tokens, cotangent, query_key, value_gate, output_weight, gate_up, down_weight, small_params, momentum_query_key, momentum_value_gate, momentum_output, momentum_gate_up, momentum_down, moment_one, moment_two, seq_lengths):
    group_rows = N_SHARD * TOK_DEV
    weights = (query_key, value_gate, output_weight, gate_up, down_weight)
    token_groups = tokens.astype(jnp.float32).reshape(N_DP, group_rows, D)
    grad_groups = cotangent.astype(jnp.float32).reshape(N_DP, group_rows, D)
    positions = jnp.arange(group_rows, dtype=jnp.int32)

    def one_group(carry, inputs):
        grads_big, grad_small = carry
        group_x, group_dy, lengths = inputs
        ends = jnp.cumsum(lengths).astype(jnp.int32)
        starts = (ends - lengths).astype(jnp.int32)
        segment = lax.optimization_barrier(jnp.sum((positions[:, None] >= ends[None, :]).astype(jnp.int32), axis=1)).astype(jnp.int32)
        keep_mask = 1.0 - lax.optimization_barrier(jnp.sum((positions[:, None] == starts[None, :]).astype(jnp.float32), axis=1))

        def forward(inputs_x, weight_set, packed):
            return group_forward(inputs_x, weight_set, packed, segment, keep_mask)
        result, pull = jax.vjp(forward, group_x, weights, small_params)
        d_input, d_weights, d_small = pull(group_dy)
        grads_big = jax.tree.map(jnp.add, grads_big, d_weights)
        return ((grads_big, grad_small + d_small), (result.astype(jnp.bfloat16), d_input.astype(jnp.bfloat16)))
    zero_big = jax.tree.map(jnp.zeros_like, weights)
    carry_out, stacked = lax.scan(one_group, (zero_big, jnp.zeros_like(small_params)), (token_groups, grad_groups, seq_lengths))
    grads_big, grad_small = carry_out
    block_out = stacked[0].reshape(N_DP * group_rows, D)
    input_grad = stacked[1].reshape(N_DP * group_rows, D)
    grad_qk, grad_vg, grad_out, grad_gu, grad_dn = grads_big
    step_qk, mom_qk = muon_weight(grad_qk, momentum_query_key, query_key)
    step_vg, mom_vg = muon_weight(grad_vg, momentum_value_gate, value_gate)
    step_out, mom_out = muon_weight(grad_out, momentum_output, output_weight)
    step_gu, mom_gu = muon_weight(grad_gu, momentum_gate_up, gate_up)
    step_dn, mom_dn = muon_weight(grad_dn, momentum_down, down_weight)
    new_one = BETA_ONE * moment_one + (1.0 - BETA_ONE) * grad_small
    new_two = BETA_TWO * moment_two + (1.0 - BETA_TWO) * grad_small * grad_small
    small_step = -ADAM_RATE * (new_one / (1.0 - BETA_ONE ** STEP_COUNT)) / (jnp.sqrt(new_two / (1.0 - BETA_TWO ** STEP_COUNT)) + ADAM_EPS)
    return (block_out, input_grad, grad_qk, grad_vg, grad_out, grad_gu, grad_dn, step_qk, step_vg, step_out, step_gu, step_dn, mom_qk, mom_vg, mom_out, mom_gu, mom_dn, grad_small, small_step, new_one, new_two)
```

```python
import functools
import math

import jax
import jax.numpy as jnp
from jax import lax
from jax.experimental import pallas as pl
from jax.experimental.pallas import tpu as pltpu
from jax.sharding import PartitionSpec as P

DK=128; DV=256; KCONV=4; CH=128
f32=jnp.float32; bf16=jnp.bfloat16
HI=lax.Precision.HIGHEST
GATE_EPS=1e-5; UNIT_EPS=1e-6

def _split(a):
    h=a.astype(bf16)
    return h,(a-h.astype(f32)).astype(bf16)

def dot(a,b,ca,cb,passes=3):
    dn=(((ca,),(cb,)),((),()))
    if passes==6:
        return lax.dot_general(a,b,dn,precision=HI,preferred_element_type=f32)
    if passes==1:
        return lax.dot_general(a.astype(bf16),b.astype(bf16),dn,preferred_element_type=f32)
    ah,al=_split(a); bh,bl=_split(b)
    g=functools.partial(lax.dot_general,dimension_numbers=dn,preferred_element_type=f32)
    return g(ah,bh)+(g(ah,bl)+g(al,bh))

def softplus(x): return jnp.maximum(x,0.0)+jnp.log1p(jnp.exp(-jnp.abs(x)))
def sigmoid(x): return lax.logistic(x)

def iota2(n,ax): return lax.broadcasted_iota(jnp.int32,(n,n),ax)

def inverse(A,p):
    n=A[0].shape[0]
    ri=iota2(n,0); ci=iota2(n,1)
    eye=(ri==ci).astype(f32)
    same=lambda b:(ri//b)==(ci//b)
    pw=[jnp.where(same(16),a,0.0) for a in A]
    X=[eye-q for q in pw]
    for _ in range(3):
        pw=[dot(q,q,1,0,p) for q in pw]
        X=[x+dot(x,q,1,0,p) for x,q in zip(X,pw)]
    b=16
    while b<n:
        m=jnp.logical_and(same(2*b),jnp.logical_not(same(b)))
        off=[jnp.where(m,a,0.0) for a in A]
        t=[dot(o,x,1,0,p) for o,x in zip(off,X)]
        X=[x-dot(x,q,1,0,p) for x,q in zip(X,t)]
        b*=2
    return X

def conv_pre(u,taps,info):
    s=taps[3:4]*u
    for k in (1,2,3):
        s=s+taps[3-k:4-k]*(pltpu.roll(u,k,0)*info[:,k:k+1])
    return s

def l2(u):
    return lax.rsqrt(jnp.sum(u*u,axis=-1,keepdims=True)+UNIT_EPS)

def acts(raw,taps,info,nh):
    out=[]
    kq=nh*DK
    for h in range(nh):
        d={}
        for nm,off,w in (("q",h*DK,DK),("k",kq+h*DK,DK),("v",2*kq+h*DV,DV)):
            pre=conv_pre(raw[:,off:off+w],taps[:,off:off+w],info)
            act=pre*sigmoid(pre)
            d[nm+"pre"]=pre; d[nm]=act
        rq=l2(d["q"])*(DK**-0.5); rk=l2(d["k"])
        d["rq"]=rq; d["rk"]=rk
        d["qn"]=d["q"]*rq; d["kn"]=d["k"]*rk
        out.append(d)
    return out

def decays(small,vec,nh):
    z=small+vec[1:2]
    ld=-vec[0:1]*softplus(z)
    beta=sigmoid(small)
    return z,ld,beta

def chunk_terms(ld,segc,segr,R,nh):
    n=CH
    ri=iota2(n,0); ci=iota2(n,1)
    low=(ri>=ci)
    L=low.astype(f32)
    out=[]
    for c in range(R//n):
        sl=slice(c*n,(c+1)*n)
        ldc=ld[sl]
        cc=dot(L,ldc,1,0,6)
        cr=dot(ldc,L,0,1,6)
        sc=segc[sl]; sr=segr[:,sl]
        M=jnp.logical_and(low,sc==sr)
        prev=segc[c*n-1:c*n] if c else None
        last=segc[(c+1)*n-1:(c+1)*n]
        heads=[]
        for h in range(nh):
            col=cc[:,h:h+1]; row=cr[h:h+1,:]
            R_=jnp.where(M,jnp.exp(jnp.where(M,col-row,0.0)),0.0)
            end=cc[n-1:n,h:h+1]
            t=jnp.where(sc==last,jnp.exp(end-col),0.0)
            if c:
                e=jnp.where(sc==prev,jnp.exp(col),0.0)
                g=jnp.where(last==prev,jnp.exp(end),0.0)
            else:
                e=jnp.zeros_like(col); g=jnp.zeros_like(end)
            heads.append((R_,e,t,g))
        out.append(heads)
    return out

def mixer_fwd(raw,small,taps,vec,gain,info,segr,nh,P):
    R=raw.shape[0]; nc=R//CH; n=CH
    segc=info[:,0:1]
    a=acts(raw,taps,info,nh)
    z,ld,beta=decays(small,vec,nh)
    terms=chunk_terms(ld,segc,segr,R,nh)
    ri=iota2(n,0); ci=iota2(n,1)
    strict=ri>ci
    idx=[(h,c) for c in range(nc) for h in range(nh)]
    sl=lambda c:slice(c*n,(c+1)*n)
    A=[];Pm=[]
    for h,c in idx:
        K=a[h]["kn"][sl(c)]; Q=a[h]["qn"][sl(c)]
        R_=terms[c][h][0]
        b=beta[sl(c),nh+h:nh+h+1]
        A.append(jnp.where(strict,b*R_*dot(K,K,1,1,P["kk"]),0.0))
        Pm.append(dot(Q,K,1,1,P["qk"])*R_)
    X=inverse(A,P["inv"])
    U0=[];W=[]
    for i,(h,c) in enumerate(idx):
        b=beta[sl(c),nh+h:nh+h+1]; e=terms[c][h][1]
        U0.append(dot(X[i],b*a[h]["v"][sl(c)],1,0,P["u"]))
        W.append(dot(X[i],(b*e)*a[h]["kn"][sl(c)],1,0,P["u"]) if c else None)
    S=[None]*nh
    S0s={};Us={};O={}
    for i,(h,c) in enumerate(idx):
        R_,e,t,g=terms[c][h]
        K=a[h]["kn"][sl(c)]; Q=a[h]["qn"][sl(c)]
        S0=S[h]
        U=U0[i] if c==0 else U0[i]-dot(W[i],S0,1,0,P["s"])
        o=dot(Pm[i],U,1,0,P["o"])
        if c: o=o+dot(e*Q,S0,1,0,P["o"])
        up=dot(t*K,U,0,0,P["s"])
        S[h]=up if c==0 else g*S0+up
        S0s[h,c]=S0; Us[h,c]=U; O[h,c]=o
    off=2*nh*DK+nh*DV
    gated={}
    for h,c in idx:
        o=O[h,c]
        r=lax.rsqrt(jnp.mean(o*o,axis=-1,keepdims=True)+GATE_EPS)
        gt=raw[sl(c),off+h*DV:off+(h+1)*DV]
        gated[h,c]=o*r*gain*(gt*sigmoid(gt))
    return gated,O,Us,S0s,{(h,c):X[i] for i,(h,c) in enumerate(idx)}

def mixer_bwd(raw,small,taps,vec,gain,info,segr,dgated,O,Us,S0s,X,nh,P):
    R=raw.shape[0]; nc=R//CH; n=CH
    segc=info[:,0:1]
    a=acts(raw,taps,info,nh)
    z,ld,beta=decays(small,vec,nh)
    terms=chunk_terms(ld,segc,segr,R,nh)
    ri=iota2(n,0); ci=iota2(n,1)
    strict=ri>ci
    U_=(ri<=ci).astype(f32)
    idx=[(h,c) for c in range(nc) for h in range(nh)]
    sl=lambda c:slice(c*n,(c+1)*n)
    off=2*nh*DK+nh*DV
    dO={};dgate={};ggain=None
    for h,c in idx:
        o=O[h,c]
        r=lax.rsqrt(jnp.mean(o*o,axis=-1,keepdims=True)+GATE_EPS)
        gt=raw[sl(c),off+h*DV:off+(h+1)*DV]
        s=sigmoid(gt); sg=gt*s
        dg=dgated[h,c]
        nrm=o*r
        dgate[h,c]=dg*nrm*gain*(s*(1.0+gt*(1.0-s)))
        dsn=dg*sg
        part=jnp.sum(dsn*nrm,axis=0,keepdims=True)
        ggain=part if ggain is None else ggain+part
        dn=dsn*gain
        dO[h,c]=r*dn-nrm*(r*jnp.mean(nrm*dn,axis=-1,keepdims=True))
    Pm={};dU0={};KK={};QK={}
    for h,c in idx:
        K=a[h]["kn"][sl(c)]; Q=a[h]["qn"][sl(c)]
        KK[h,c]=dot(K,K,1,1,P["kk"]); QK[h,c]=dot(Q,K,1,1,P["qk"])
        Pm[h,c]=QK[h,c]*terms[c][h][0]
        dU0[h,c]=dot(Pm[h,c],dO[h,c],0,0,P["u"])
    dS=[None]*nh
    dS1s={};Ys={}
    for c in reversed(range(nc)):
        for h in range(nh):
            R_,e,t,g=terms[c][h]
            K=a[h]["kn"][sl(c)]; Q=a[h]["qn"][sl(c)]
            b=beta[sl(c),nh+h:nh+h+1]
            dS1=dS[h]
            dS1s[h,c]=dS1
            dU=dU0[h,c]
            if dS1 is not None: dU=dU+dot(t*K,dS1,1,0,P["s"])
            Y=dot(X[h,c],dU,0,0,P["s"])
            Ys[h,c]=Y
            if c:
                d0=dot(e*Q,dO[h,c],0,0,P["s"])-dot((b*e)*K,Y,0,0,P["s"])
                dS[h]=d0 if dS1 is None else g*dS1+d0
    dQ={};dK={};dV={};dbeta={};dld={}
    ones_r=jnp.ones((8,n),f32)
    for h,c in idx:
        R_,e,t,g=terms[c][h]
        K=a[h]["kn"][sl(c)]; Q=a[h]["qn"][sl(c)]; V=a[h]["v"][sl(c)]
        b=beta[sl(c),nh+h:nh+h+1]
        Y=Ys[h,c]; U=Us[h,c]; dS1=dS1s[h,c]; S0=S0s[h,c]
        dA=jnp.where(strict,-dot(Y,U,1,1,P["g"]),0.0)
        dP=dot(dO[h,c],U,1,1,P["g"])
        H=dP*R_
        Gr=dA*R_
        G=b*Gr
        dq=dot(H,K,1,0,P["g"])
        dk=dot(G,K,1,0,P["g"])+dot(G,K,0,0,P["g"])+dot(H,Q,0,0,P["g"])
        dV[h,c]=b*Y
        db=jnp.sum(Y*V,axis=-1,keepdims=True)+jnp.sum(Gr*KK[h,c],axis=-1,keepdims=True)
        Z=H*QK[h,c]+G*KK[h,c]
        dc=jnp.sum(Z,axis=-1,keepdims=True)-jnp.sum(Z.T,axis=-1,keepdims=True)
        last=(lax.broadcasted_iota(jnp.int32,(n,1),0)==n-1).astype(f32)
        if c:
            YS=dot(Y,S0,1,1,P["g"]); OS=dot(dO[h,c],S0,1,1,P["g"])
            dq=dq+e*OS
            dk=dk-(b*e)*YS
            ks=jnp.sum(YS*K,axis=-1,keepdims=True)
            qs=jnp.sum(OS*Q,axis=-1,keepdims=True)
            db=db-e*ks
            dc=dc+e*(qs-b*ks)
        if dS1 is not None:
            US=dot(U,dS1,1,1,P["g"])
            dk=dk+t*US
            tt=t*jnp.sum(US*K,axis=-1,keepdims=True)
            dc=dc-tt
            tot=jnp.sum(tt,axis=0,keepdims=True)
            if c:
                tot=tot+g*jnp.sum(jnp.sum(dS1*S0,axis=-1,keepdims=True),axis=0,keepdims=True)
            dc=dc+last*tot
        dQ[h,c]=dq; dK[h,c]=dk; dbeta[h,c]=db
        dld[h,c]=dc
    lane=lax.broadcasted_iota(jnp.int32,(n,128),1)
    dsm=[]
    for c in range(nc):
        acc_d=jnp.zeros((n,128),f32); acc_b=jnp.zeros((n,128),f32)
        for h in range(nh):
            acc_d=acc_d+jnp.where(lane==h,dld[h,c],0.0)
            acc_b=acc_b+jnp.where(lane==nh+h,dbeta[h,c],0.0)
        acc_d=dot(U_,acc_d,1,0,6)
        dsm.append((acc_d,acc_b))
    dldf=jnp.concatenate([x[0] for x in dsm],axis=0)
    dbf=jnp.concatenate([x[1] for x in dsm],axis=0)
    dz=-dldf*vec[0:1]*sigmoid(z)
    dsmall=dz+dbf*beta*(1.0-beta)
    g_dt=jnp.sum(dz,axis=0,keepdims=True)
    g_al=jnp.sum(dldf*ld,axis=0,keepdims=True)
    draw={};gt=[None]*0
    tapg=[[None]*0 for _ in range(4)]
    cols=[]
    for nm in ("q","k","v"):
        for h in range(nh):
            d=a[h]
            w=DV if nm=="v" else DK
            coff={"q":h*DK,"k":nh*DK+h*DK,"v":2*nh*DK+h*DV}[nm]
            dy=jnp.concatenate([{"q":dQ,"k":dK,"v":dV}[nm][h,c] for c in range(nc)],axis=0)
            if nm!="v":
                rho=d["r"+nm]; y=d[nm+"n"]
                if nm=="q":
                    dy=rho*dy-(y*(DK**0.5))*(l2(d["q"])*jnp.sum((y*(DK**0.5))*dy,axis=-1,keepdims=True)*(DK**-0.5))
                else:
                    dy=rho*(dy-y*jnp.sum(y*dy,axis=-1,keepdims=True))
            pre=d[nm+"pre"]; s=sigmoid(pre)
            dp=dy*(s*(1.0+pre*(1.0-s)))
            u=raw[:,coff:coff+w]; tp=taps[:,coff:coff+w]
            du=tp[3:4]*dp
            tg=[None]*4
            tg[3]=jnp.sum(dp*u,axis=0,keepdims=True)
            for k in (1,2,3):
                su=pltpu.roll(dp,dp.shape[0]-k,0)*info[:,3+k:4+k]
                du=du+tp[3-k:4-k]*su
                tg[3-k]=jnp.sum(su*u,axis=0,keepdims=True)
            cols.append((nm,h,du,tg))
    return cols,dgate,dsmall,g_dt,g_al,ggain

def m1_kernel(nh,P,raw_ref,small_ref,taps_ref,vec_ref,gain_ref,info_ref,segr_ref,gated_ref,o_ref,u_ref,s_ref,x_ref):
    gated,O,U,S0,X=mixer_fwd(raw_ref[...],small_ref[...],taps_ref[...],vec_ref[...],gain_ref[0:1],info_ref[...],segr_ref[0:1],nh,P)
    n=CH
    for (h,c) in gated:
        r=slice(c*n,(c+1)*n); co=slice(h*DV,(h+1)*DV)
        gated_ref[r,co]=gated[h,c].astype(bf16)
        o_ref[r,co]=O[h,c]; u_ref[r,co]=U[h,c]
        x_ref[c*nh+h]=X[h,c]
        s_ref[c*nh+h]=S0[h,c] if c else jnp.zeros((DK,DV),f32)

def m1(raw,small,taps,vec,gain,info,segr,P):
    R=raw.shape[0]; nh=raw.shape[1]//(2*DK+2*DV); nb=nh*R//CH
    vm=pl.BlockSpec(memory_space=pltpu.VMEM)
    return pl.pallas_call(functools.partial(m1_kernel,nh,P),
      out_shape=[jax.ShapeDtypeStruct((R,nh*DV),bf16),jax.ShapeDtypeStruct((R,nh*DV),f32),jax.ShapeDtypeStruct((R,nh*DV),f32),
                 jax.ShapeDtypeStruct((nb,DK,DV),f32),jax.ShapeDtypeStruct((nb,CH,CH),f32)],
      in_specs=[vm]*7,out_specs=[vm]*5,
      compiler_params=pltpu.CompilerParams(vmem_limit_bytes=56<<20),name="mixer_forward")(raw,small,taps,vec,gain,info,segr)

def m2_kernel(nh,P,raw_ref,small_ref,taps_ref,vec_ref,gain_ref,info_ref,segr_ref,dg_ref,o_ref,u_ref,s_ref,x_ref,
              draw_ref,dsmall_ref,gt_ref,gv_ref,gg_ref):
    n=CH; R=raw_ref.shape[0]; nc=R//n
    g=lambda ref:{(h,c):ref[c*n:(c+1)*n,h*DV:(h+1)*DV] for h in range(nh) for c in range(nc)}
    b=lambda ref:{(h,c):ref[c*nh+h] for h in range(nh) for c in range(nc)}
    cols,dgate,dsmall,g_dt,g_al,gg=mixer_bwd(raw_ref[...],small_ref[...],taps_ref[...],vec_ref[...],gain_ref[0:1],info_ref[...],segr_ref[0:1],
       g(dg_ref),g(o_ref),g(u_ref),b(s_ref),b(x_ref),nh,P)
    gt_ref[...]=jnp.zeros_like(gt_ref)
    for nm,h,du,tg in cols:
        w=DV if nm=="v" else DK
        co={"q":h*DK,"k":nh*DK+h*DK,"v":2*nh*DK+h*DV}[nm]
        draw_ref[:,co:co+w]=du.astype(bf16)
        for i in range(4): gt_ref[i:i+1,co:co+w]=tg[i]
    off=2*nh*DK+nh*DV
    for h,c in dgate: draw_ref[c*n:(c+1)*n,off+h*DV:off+(h+1)*DV]=dgate[h,c].astype(bf16)
    dsmall_ref[...]=dsmall
    gv_ref[...]=jnp.zeros_like(gv_ref)
    gv_ref[0:1]=g_al; gv_ref[1:2]=g_dt
    gg_ref[...]=jnp.zeros_like(gg_ref)
    gg_ref[0:1]=gg

def m2(raw,small,taps,vec,gain,info,segr,dgated,O,U,S,X,P):
    R=raw.shape[0]; nh=raw.shape[1]//(2*DK+2*DV); nb=nh*R//CH
    vm=pl.BlockSpec(memory_space=pltpu.VMEM)
    return pl.pallas_call(functools.partial(m2_kernel,nh,P),
      out_shape=[jax.ShapeDtypeStruct((R,raw.shape[1]),bf16),jax.ShapeDtypeStruct((R,128),f32),jax.ShapeDtypeStruct((8,nh*(2*DK+DV)),f32),
                 jax.ShapeDtypeStruct((8,128),f32),jax.ShapeDtypeStruct((8,DV),f32)],
      in_specs=[vm]*12,out_specs=[vm]*5,
      compiler_params=pltpu.CompilerParams(vmem_limit_bytes=56<<20),name="mixer_backward")(raw,small,taps,vec,gain,info,segr,dgated,O,U,S,X)


f32=jnp.float32; bf16=jnp.bfloat16
MESH=pl.DeviceIdType.MESH
ANY=pl.BlockSpec(memory_space=pl.ANY)
VM=pl.BlockSpec(memory_space=pltpu.VMEM)

def place():
    d=lax.axis_index("dp"); s=lax.axis_index("shard")
    return d,s,d//2,d%2

def greet(peers):
    bar=pltpu.get_barrier_semaphore()
    for p in peers:
        pl.semaphore_signal(bar,inc=1,device_id=p,device_id_type=MESH)
    pl.semaphore_wait(bar,len(peers))

def remote(src,dst,ss,rs,dev):
    return pltpu.make_async_remote_copy(src_ref=src,dst_ref=dst,send_sem=ss,recv_sem=rs,device_id=dev,device_id_type=MESH)

def gather_kernel(n_dp,n_s,ncol,nrow,nact,order,W,*refs):
    n=ncol+nrow+nact
    ins=refs[:n]; outs=refs[n:2*n]
    s0,r0,s1,r1,sa,ra,lsem=refs[2*n:]
    d,s,hi,lo=place()
    n_hi=n_dp//2
    np_=ncol+nrow
    me=d*n_s+s
    td=me%n_dp; ts=me//n_dp
    fd=(s*n_dp+d)//n_s; fs=(s*n_dp+d)%n_s
    zs=[((hi+j)%n_hi)*2+lo for j in range(1,n_hi)]
    xd=hi*2+(1-lo)
    grp=[(d,(s+j)%n_s) for j in range(1,n_s)]
    bar=pltpu.get_barrier_semaphore()
    peers=grp+[(z,s) for z in zs]+[(xd,s)]
    moved=jnp.logical_or(td!=d,ts!=s)
    for p in peers:
        pl.semaphore_signal(bar,inc=1,device_id=p,device_id_type=MESH)
    @pl.when(moved)
    def _():
        pl.semaphore_signal(bar,inc=1,device_id=(td,ts),device_id_type=MESH)
        pl.semaphore_signal(bar,inc=1,device_id=(fd,fs),device_id_type=MESH)
    @pl.when(moved)
    def _():
        pl.semaphore_wait(bar,len(peers)+2)
    @pl.when(jnp.logical_not(moved))
    def _():
        pl.semaphore_wait(bar,len(peers))
    sends=[]
    local=[]
    for k in range(nact):
        src=ins[np_+k]; dst=outs[np_+k]
        c=pltpu.make_async_copy(src,dst.at[s],lsem.at[np_+k]); c.start(); local.append(c)
        for j,p in enumerate(grp):
            c=remote(src,dst.at[s],sa.at[k,j],ra.at[k,j],p); c.start(); sends.append(c)
    col={}
    def phase0(k):
        if k<ncol:
            c=pltpu.make_async_copy(ins[k].at[s],outs[k].at[d,s],lsem.at[k]); c.start()
            col[k]=[c]
            for j,p in enumerate(grp):
                c=remote(ins[k].at[p[1]],outs[k].at[d,s],s0.at[k,j],r0.at[k,j],p); c.start(); col[k].append(c)
        else:
            @pl.when(moved)
            def _():
                remote(ins[k],outs[k].at[td],s0.at[k,0],r0.at[k,0],(td,ts)).start()
            @pl.when(jnp.logical_not(moved))
            def _():
                pltpu.make_async_copy(ins[k],outs[k].at[d],r0.at[k,0]).start()
    def ready(k):
        if k<ncol:
            for c in col[k]: c.wait()
        else:
            pltpu.make_async_copy(ins[k],outs[k].at[d],r0.at[k,0]).wait()
            @pl.when(moved)
            def _():
                remote(ins[k],outs[k].at[td],s0.at[k,0],r0.at[k,0],(td,ts)).wait_send()
    pieces=[]
    for k,_,_ in order:
        if k not in pieces: pieces.append(k)
    for k in pieces: phase0(k)
    def blk(i,src):
        k,a,m=order[i]
        return outs[k].at[src,a:a+m] if m else outs[k].at[src]
    def first(i):
        own=blk(i,d)
        for j,z in enumerate(zs):
            remote(own,own,s1.at[i,j],r1.at[i,j],(z,s)).start()
        remote(own,own,s1.at[i,n_hi-1],r1.at[i,n_hi-1],(xd,s)).start()
    def second(i):
        for j in range(1,n_hi):
            b=blk(i,((hi-j)%n_hi)*2+lo)
            remote(b,b,s1.at[i,j-1],r1.at[i,j-1],(xd,s)).wait()
            remote(b,b,s1.at[i,n_hi-1+j],r1.at[i,n_hi-1+j],(xd,s)).start()
    def third(i):
        for j in range(n_hi):
            b=blk(i,((hi-j)%n_hi)*2+(1-lo))
            remote(b,b,s1.at[i,n_hi-1+j],r1.at[i,n_hi-1+j],(xd,s)).wait()
    done=set()
    nch=len(order)
    for i in range(nch+W+1):
        if i<nch:
            k=order[i][0]
            if k not in done:
                ready(k); done.add(k)
            first(i)
        if 0<=i-W<nch: second(i-W)
        if 0<=i-W-1<nch: third(i-W-1)
    for k in range(nact): local[k].wait()
    for c in sends: c.wait()

def gather(cols,rows,acts,n_dp,n_s,cid,order,W=1):
    pieces=list(cols)+list(rows); np_=len(pieces); n_hi=n_dp//2
    shapes=[jax.ShapeDtypeStruct((n_dp,)+x.shape,x.dtype) for x in pieces]+[jax.ShapeDtypeStruct((n_s,)+x.shape,x.dtype) for x in acts]
    D=pltpu.SemaphoreType.DMA
    na=max(len(acts),1); nch=len(order)
    return pl.pallas_call(functools.partial(gather_kernel,n_dp,n_s,len(cols),len(rows),len(acts),order,W),
        out_shape=shapes,in_specs=[ANY]*(np_+len(acts)),out_specs=[ANY]*(np_+len(acts)),
        scratch_shapes=[D((np_,n_s)),D((np_,n_s)),D((nch,2*n_hi)),D((nch,2*n_hi)),D((na,n_s)),D((na,n_s)),D((np_+na,))],
        compiler_params=pltpu.CompilerParams(collective_id=cid,has_side_effects=True),name="gather_weights")(*pieces,*acts)

NORM_EPS=1e-6
D_=pltpu.SemaphoreType.DMA
def ring(n_s):
    d,s,_,_=place()
    return [(d,(s+j)%n_s) for j in range(1,n_s)]

def push_parts(n_s,part,land,ss,rs):
    cs=[]
    for j,p in enumerate(ring(n_s)):
        c=remote(part.at[p[1]],land.at[j],ss.at[j],rs.at[j],p); c.start(); cs.append(c)
    return cs

def push_all(n_s,out,ss,rs):
    _,s,_,_=place()
    cs=[]
    for j,p in enumerate(ring(n_s)):
        c=remote(out.at[s],out.at[s],ss.at[j],rs.at[j],p); c.start(); cs.append(c)
    return cs

def add_up(n_s,part,land):
    _,s,_,_=place()
    t=part[s].astype(f32)
    for j in range(n_s-1): t=t+land[j].astype(f32)
    return t

def norm_back(u,g,dn):
    w=u.shape[-1]
    r=lax.rsqrt(jnp.mean(u*u,axis=-1,keepdims=True)+NORM_EPS)
    gd=g*dn
    du=r*gd-u*(r*r*r*(jnp.sum(u*gd,axis=-1,keepdims=True)/w))
    return du,jnp.sum(u*r*dn,axis=0,keepdims=True)

def mid_kernel(n_s,part,x,gain,middle,gathered,land,s0,r0,s1,r1):
    _,s,_,_=place()
    greet(ring(n_s))
    a=push_parts(n_s,part,land,s0,r0)
    for c in a: c.wait()
    m=x[...].astype(f32)+add_up(n_s,part,land)
    middle[...]=m
    r=lax.rsqrt(jnp.mean(m*m,axis=-1,keepdims=True)+NORM_EPS)
    gathered[s]=(m*r*gain[0:1]).astype(bf16)
    for c in push_all(n_s,gathered,s1,r1): c.wait()

def mid(part,x,gain,n_s,cid):
    rows,w=x.shape
    return pl.pallas_call(functools.partial(mid_kernel,n_s),
        out_shape=[jax.ShapeDtypeStruct((rows,w),f32),jax.ShapeDtypeStruct((n_s,rows,w),bf16)],
        in_specs=[VM]*3,out_specs=[VM]*2,
        scratch_shapes=[pltpu.VMEM((n_s-1,rows,w),bf16)]+[D_((n_s,))]*4,
        compiler_params=pltpu.CompilerParams(collective_id=cid,has_side_effects=True,vmem_limit_bytes=40<<20),name="branch_sum")(part,x,gain)

def ffn_kernel(n_s,ypart,dpart,middle,dy,gain,out,dmid,gathered,dgain,yland,dland,s0,r0,s1,r1,s2,r2):
    _,s,_,_=place()
    greet(ring(n_s))
    b=push_parts(n_s,dpart,dland,s1,r1)
    for c in b: c.wait()
    a=push_parts(n_s,ypart,yland,s0,r0)
    m=middle[...]
    du,dg=norm_back(m,gain[0:1],add_up(n_s,dpart,dland))
    dm=dy[...].astype(f32)+du
    dmid[...]=dm
    dgain[...]=jnp.broadcast_to(dg,dgain.shape)
    gathered[s]=dm.astype(bf16)
    g=push_all(n_s,gathered,s2,r2)
    for c in a: c.wait()
    out[...]=(m+add_up(n_s,ypart,yland)).astype(bf16)
    for c in g: c.wait()

def ffn(ypart,dpart,middle,dy,gain,n_s,cid):
    rows,w=middle.shape
    return pl.pallas_call(functools.partial(ffn_kernel,n_s),
        out_shape=[jax.ShapeDtypeStruct((rows,w),bf16),jax.ShapeDtypeStruct((rows,w),f32),jax.ShapeDtypeStruct((n_s,rows,w),bf16),
                   jax.ShapeDtypeStruct((8,w),f32)],
        in_specs=[VM]*5,out_specs=[VM]*4,
        scratch_shapes=[pltpu.VMEM((n_s-1,rows,w),bf16)]*2+[D_((n_s,))]*6,
        compiler_params=pltpu.CompilerParams(collective_id=cid,has_side_effects=True,vmem_limit_bytes=40<<20),name="block_sum")(ypart,dpart,middle,dy,gain)

def end_kernel(n_s,part,x,dmid,gain,out,dgain,land,s0,r0):
    greet(ring(n_s))
    for c in push_parts(n_s,part,land,s0,r0): c.wait()
    du,dg=norm_back(x[...].astype(f32),gain[0:1],add_up(n_s,part,land))
    out[...]=(dmid[...]+du).astype(bf16)
    dgain[...]=jnp.broadcast_to(dg,dgain.shape)

def end(part,x,dmid,gain,n_s,cid):
    rows,w=x.shape
    return pl.pallas_call(functools.partial(end_kernel,n_s),
        out_shape=[jax.ShapeDtypeStruct((rows,w),bf16),jax.ShapeDtypeStruct((8,w),f32)],
        in_specs=[VM]*4,out_specs=[VM]*2,
        scratch_shapes=[pltpu.VMEM((n_s-1,rows,w),bf16)]+[D_((n_s,))]*2,
        compiler_params=pltpu.CompilerParams(collective_id=cid,has_side_effects=True,vmem_limit_bytes=40<<20),name="input_sum")(part,x,dmid,gain)

def scatter_kernel(n_dp,n_s,ncol,nrow,W,*refs):
    n=ncol+nrow
    g=refs[:n]; outs=refs[n:2*n]
    xl=refs[2*n:3*n]; zb=refs[3*n:4*n]; zl=refs[4*n:5*n]; fin=refs[5*n:6*n]
    sx,rx,sz,rz,sf,rf,lsem=refs[6*n:]
    d,s,hi,lo=place()
    n_hi=n_dp//2
    me=s*n_dp+d
    td=me//n_s; ts=me%n_s
    own=d*n_s+s
    fd=own%n_dp; fs=own//n_dp
    moved=jnp.logical_or(td!=d,ts!=s)
    zs=[((hi+j)%n_hi)*2+lo for j in range(1,n_hi)]
    xd=hi*2+(1-lo)
    grp=ring(n_s)
    bar=pltpu.get_barrier_semaphore()
    peers=grp+[(z,s) for z in zs]+[(xd,s)]
    for p in peers:
        pl.semaphore_signal(bar,inc=1,device_id=p,device_id_type=MESH)
    @pl.when(moved)
    def _():
        pl.semaphore_signal(bar,inc=1,device_id=(td,ts),device_id_type=MESH)
        pl.semaphore_signal(bar,inc=1,device_id=(fd,fs),device_id_type=MESH)
    @pl.when(moved)
    def _():
        pl.semaphore_wait(bar,len(peers)+2)
    @pl.when(jnp.logical_not(moved))
    def _():
        pl.semaphore_wait(bar,len(peers))
    order=[(k,j) for k in range(n) for j in list(range(1,n_hi))+[0]]
    def xc(i):
        k,j=order[i]; z=(hi+j)%n_hi
        return remote(g[k].at[z*2+1-lo],xl[k].at[z],sx.at[k,j],rx.at[k,j],(xd,s))
    def zc(k,j):
        return remote(zb[k].at[j-1],zl[k].at[j-1],sz.at[k,j],rz.at[k,j],(((hi+j)%n_hi)*2+lo,s))
    fc={}
    nch=len(order)
    for i in range(nch+W):
        if i<nch: xc(i).start()
        if i>=W:
            k,j=order[i-W]; z=(hi+j)%n_hi
            xc(i-W).wait()
            t=g[k][z*2+lo].astype(f32)+xl[k][z].astype(f32)
            if j:
                zb[k][j-1]=t.astype(bf16); zc(k,j).start()
            else:
                for jj in range(1,n_hi):
                    zc(k,jj).wait()
                    t=t+zl[k][jj-1].astype(f32)
                t=t.astype(bf16)
                if k<ncol:
                    rows=t.shape[0]//n_s
                    fin[k][...]=t.reshape(n_s,rows,t.shape[1])
                    c=pltpu.make_async_copy(fin[k].at[s],outs[k].at[s],lsem.at[k]); c.start()
                    fc[k]=[c]
                    for jj,p in enumerate(grp):
                        c=remote(fin[k].at[p[1]],outs[k].at[s],sf.at[k,jj],rf.at[k,jj],p); c.start(); fc[k].append(c)
                else:
                    fin[k][...]=t
                    @pl.when(moved)
                    def _():
                        remote(fin[k],outs[k],sf.at[k,0],rf.at[k,0],(td,ts)).start()
                    @pl.when(jnp.logical_not(moved))
                    def _():
                        pltpu.make_async_copy(fin[k],outs[k],rf.at[k,0]).start()
    for k in range(n):
        if k<ncol:
            for c in fc[k]: c.wait()
        else:
            pltpu.make_async_copy(fin[k],outs[k],rf.at[k,0]).wait()
            @pl.when(moved)
            def _():
                remote(fin[k],outs[k],sf.at[k,0],rf.at[k,0],(td,ts)).wait_send()

def scatter(cols,rows,n_dp,n_s,cid,W=2):
    ps=list(cols)+list(rows); n=len(ps); nc=len(cols); n_hi=n_dp//2
    oshape=lambda k,x:(n_s,x.shape[1]//n_s,x.shape[2]) if k<nc else x.shape[1:]
    outs=[jax.ShapeDtypeStruct(oshape(k,x),bf16) for k,x in enumerate(ps)]
    V=pltpu.VMEM
    sc=[V((n_hi,)+x.shape[1:],bf16) for x in ps]+[V((n_hi-1,)+x.shape[1:],bf16) for x in ps]*2+[V(oshape(k,x),bf16) for k,x in enumerate(ps)]
    return pl.pallas_call(functools.partial(scatter_kernel,n_dp,n_s,nc,len(rows),W),
        out_shape=outs,in_specs=[VM]*n,out_specs=[VM]*n,
        scratch_shapes=sc+[D_((n,n_hi))]*4+[D_((n,n_s))]*2+[D_((n,))],
        compiler_params=pltpu.CompilerParams(collective_id=cid,has_side_effects=True,vmem_limit_bytes=60<<20),name="scatter_gradients")(*ps)


f32=jnp.float32; bf16=jnp.bfloat16
CA,CB,CC=3.4445,-4.775,2.0315
def dg(a,b,ca,cb): return lax.dot_general(a,b,(((ca,),(cb,)),((),())),preferred_element_type=f32)
TB=256
def ns_wide(x,y,g,p,cols,iters=2,tm=256,tn=512):
    r=g.shape[0]
    cs=slice(0,cols)
    def sq(i,a):
        v=x[pl.ds(i*TB,TB),cs].astype(f32)
        return a+jnp.sum(v*v,axis=0,keepdims=True)
    t=lax.fori_loop(0,r//TB,sq,jnp.zeros((1,cols),f32))
    inv=1.0/(jnp.sqrt(jnp.sum(t,axis=1,keepdims=True))+1e-7)
    def sc(i,_):
        x[pl.ds(i*TB,TB),cs]=(x[pl.ds(i*TB,TB),cs].astype(f32)*inv).astype(bf16)
        return 0
    lax.fori_loop(0,r//TB,sc,0)
    a,b=x,y
    for _ in range(iters):
        def gram(i,_):
            ri=pl.ds(pl.multiple_of(i*tm,tm),tm)
            g[ri,:]=dg(a[ri,cs],a[:,cs],1,1).astype(bf16)
            return 0
        lax.fori_loop(0,r//tm,gram,0)
        def poly(i,_):
            ri=pl.ds(pl.multiple_of(i*tm,tm),tm)
            p[ri,:]=(CB*g[ri,:].astype(f32)+CC*dg(g[ri,:],g[...],1,0)).astype(bf16)
            return 0
        lax.fori_loop(0,r//tm,poly,0)
        def nxt(i,_):
            ri=pl.ds(pl.multiple_of(i*tm,tm),tm)
            b[ri,cs]=(CA*a[ri,cs].astype(f32)+dg(p[ri,:],a[:,cs],1,0)).astype(bf16)
            return 0
        lax.fori_loop(0,r//tm,nxt,0)
        a,b=b,a
def ns_tall(x,y,g,p,n=None,iters=2,tm=256):
    n=n or x.shape[0]; r=x.shape[1]
    def sq(i,a):
        v=x[pl.ds(i*TB,TB),:].astype(f32)
        return a+jnp.sum(v*v,axis=0,keepdims=True)
    t=lax.fori_loop(0,n//TB,sq,jnp.zeros((1,r),f32))
    inv=1.0/(jnp.sqrt(jnp.sum(t,axis=1,keepdims=True))+1e-7)
    def sc(i,_):
        x[pl.ds(i*TB,TB),:]=(x[pl.ds(i*TB,TB),:].astype(f32)*inv).astype(bf16)
        return 0
    lax.fori_loop(0,n//TB,sc,0)
    a,b=x,y
    for _ in range(iters):
        for j in range(r//tm):
            cj=slice(j*tm,(j+1)*tm)
            g[cj,:]=dg(a[0:n,cj],a[0:n,:],0,0).astype(bf16)
        def poly(i,_):
            ri=pl.ds(pl.multiple_of(i*tm,tm),tm)
            p[ri,:]=(CB*g[ri,:].astype(f32)+CC*dg(g[ri,:],g[...],1,0)).astype(bf16)
            return 0
        lax.fori_loop(0,r//tm,poly,0)
        def nxt(i,_):
            ri=pl.ds(pl.multiple_of(i*tm,tm),tm)
            b[ri,:]=(CA*a[ri,:].astype(f32)+dg(a[ri,:],p[...],1,0)).astype(bf16)
            return 0
        lax.fori_loop(0,n//tm,nxt,0)
        a,b=b,a


def muon_owner(i,n_dp):
    base=n_dp//2-2
    d,s=((2,0),(3,0),(1,2),(3,2),(2,2),(0,0),(1,0),(0,2))[i]
    return base+d,s

def muon_kernel(n_dp,n_s,kinds,*refs):
    n=len(kinds)
    ins=refs[:n]; outs=refs[n:2*n]
    wide,wide2,tall,tall2,g,p,rin,sin,rout,sout,lsem=refs[2*n:]
    d,s,_,_=place()
    nd=n_dp*n_s
    me=d*n_s+s
    own=[muon_owner(i,n_dp) for i in range(n)]
    base=n_dp//2-2
    is_owner=lambda dd,ss: jnp.logical_and(jnp.logical_and(dd>=base,dd<base+4),ss%2==0)
    mine=is_owner(d,s)
    bar=pltpu.get_barrier_semaphore()
    for o in own:
        @pl.when(jnp.logical_or(d!=o[0],s!=o[1]))
        def _():
            pl.semaphore_signal(bar,inc=1,device_id=o,device_id_type=MESH)
    @pl.when(mine)
    def _():
        def greet_one(q,_):
            dd=q//n_s; ss=q%n_s
            @pl.when(jnp.logical_not(is_owner(dd,ss)))
            def _():
                pl.semaphore_signal(bar,inc=1,device_id=(dd,ss),device_id_type=MESH)
            return 0
        lax.fori_loop(0,nd,greet_one,0)
        pl.semaphore_wait(bar,nd-1)
    @pl.when(jnp.logical_not(mine))
    def _():
        pl.semaphore_wait(bar,n)
    def slot(buf,i,q):
        t,rows,cols=kinds[i]
        ds=pl.ds(pl.multiple_of(q*rows,rows),rows)
        return buf.at[ds] if t else buf.at[ds,pl.ds(0,cols)]
    for i in range(n):
        t,rows,cols=kinds[i]
        dst=slot(tall if t else wide,i,me)
        there=jnp.logical_and(d==own[i][0],s==own[i][1])
        @pl.when(there)
        def _():
            pltpu.make_async_copy(ins[i],dst,rin.at[0]).start()
        @pl.when(jnp.logical_not(there))
        def _():
            remote(ins[i],dst,sin.at[i],rin.at[0],own[i]).start()
    for i in range(n):
        t,rows,cols=kinds[i]
        there=jnp.logical_and(d==own[i][0],s==own[i][1])
        @pl.when(there)
        def _():
            buf=tall if t else wide
            full=buf.at[pl.ds(0,rows*nd)] if t else buf.at[:,pl.ds(0,cols)]
            pltpu.make_async_copy(full,full,rin.at[0]).wait()
            if t: ns_tall(tall,tall2,g,p,n=rows*nd)
            else: ns_wide(wide,wide2,g,p,cols,tm=512 if cols>1024 else 256)
            def send(q,_):
                src=slot(buf,i,q)
                @pl.when(q==me)
                def _():
                    pltpu.make_async_copy(src,outs[i],rout.at[i]).start()
                @pl.when(q!=me)
                def _():
                    remote(src,outs[i],sout.at[0],rout.at[i],(q//n_s,q%n_s)).start()
                return 0
            lax.fori_loop(0,nd,send,0)
            part=buf.at[pl.ds(0,rows*(nd-1))] if t else buf.at[pl.ds(0,rows*(nd-1)),pl.ds(0,cols)]
            pltpu.make_async_copy(part,part,sout.at[0]).wait()
    for i in range(n):
        there=jnp.logical_and(d==own[i][0],s==own[i][1])
        @pl.when(jnp.logical_not(there))
        def _():
            pltpu.make_async_copy(ins[i],ins[i],sin.at[i]).wait()
        pltpu.make_async_copy(ins[i],outs[i],rout.at[i]).wait()

def muon(looks,n_dp,n_s,cid):
    nd=n_dp*n_s
    kinds=[]
    for x in looks:
        r,c=x.shape
        kinds.append((r*nd>c,r,c))
    r=min(min(k[1]*nd,k[2]) for k in kinds)
    wc=max(k[2] for k in kinds if not k[0]); tr=max(k[1]*nd for k in kinds if k[0])
    V=pltpu.VMEM
    return pl.pallas_call(functools.partial(muon_kernel,n_dp,n_s,tuple(kinds)),
        out_shape=[jax.ShapeDtypeStruct(x.shape,bf16) for x in looks],in_specs=[VM]*8,out_specs=[VM]*8,
        scratch_shapes=[V((r,wc),bf16)]*2+[V((tr,r),bf16)]*2+[V((r,r),bf16)]*2+[D_((1,)),D_((8,)),D_((8,)),D_((1,)),D_((1,))],
        compiler_params=pltpu.CompilerParams(collective_id=cid,has_side_effects=True,vmem_limit_bytes=60<<20),name="muon")(*looks)


D = 1024
H = 8
STEP_COUNT = 10
MOMENTUM = 0.95
MUON_RATE = 0.1
MUON_DECAY = 0.01
ADAM_RATE = 0.05
BETA_ONE = 0.9
BETA_TWO = 0.95
ADAM_EPS = 1e-08
PASSES = dict(kk=3, qk=3, inv=3, u=3, s=3, o=3, g=3)


def unpack(packed):
    layouts = [(D, H), (D, H), (KCONV, H * DK), (KCONV, H * DK), (KCONV, H * DV), (D,), (D,), (DV,), (H,), (H,)]
    pieces = []
    offset = 0
    for layout in layouts:
        amount = math.prod(layout)
        pieces.append(packed[offset : offset + amount].reshape(layout))
        offset = offset + amount
    return pieces


def mm(a, b, ca, cb, kind=f32):
    return lax.dot_general(
        a, b, (((ca,), (cb,)), ((), ())), preferred_element_type=f32
    ).astype(kind)


def row_facts(lengths, rows):
    count = lengths.shape[0]
    ends = jnp.sum(jnp.where(jnp.arange(count)[:, None] >= jnp.arange(count)[None, :], lengths[None, :], 0), axis=1)
    pos = jnp.arange(rows, dtype=jnp.int32)

    def number(p):
        seg = jnp.sum((p[:, None] >= ends[None, :]).astype(jnp.int32), axis=1)
        return jnp.where(p < 0, -1, seg).astype(f32)

    seg = number(pos)
    cols = [seg]
    for k in (1, 2, 3):
        cols.append((number(pos - k) == seg).astype(f32))
    for k in (1, 2, 3):
        cols.append((number(pos + k) == seg).astype(f32))
    info = jnp.pad(jnp.stack(cols, axis=1), ((0, 0), (0, 128 - len(cols))))
    return info, jnp.broadcast_to(seg[None, :], (8, rows))


def top(rows, array):
    return jnp.pad(array, ((0, rows - array.shape[0]), (0, 0)))


def by_member(parts, n_s):
    split = [p.reshape(p.shape[0], n_s, p.shape[1] // n_s) for p in parts]
    return jnp.swapaxes(jnp.concatenate(split, axis=2), 0, 1)


def whole_rows(piece, widths):
    out = []
    at = 0
    for w in widths:
        p = jnp.swapaxes(piece[:, :, at : at + w], 0, 1)
        out.append(p.reshape(p.shape[0], -1))
        at += w
    return out


def body(
    n_dp,
    n_s,
    tokens,
    cotangent,
    query_key,
    value_gate,
    output_weight,
    gate_up,
    down_weight,
    small_params,
    momentum_query_key,
    momentum_value_gate,
    momentum_output,
    momentum_gate_up,
    momentum_down,
    moment_one,
    moment_two,
    seq_lengths,
):
    member = lax.axis_index("shard")
    nh = H // n_s
    local = tokens.shape[0]
    rows = local * n_s
    ff = gate_up.shape[2] // n_s
    (w_decay, w_beta, conv_query, conv_keys, conv_value, gain_one, gain_two, gain_out, a_log, dt_bias) = unpack(
        small_params
    )

    def mine(array, axis, size):
        return lax.dynamic_slice_in_dim(array, member * size, size, axis)

    def put(array, axis, full):
        shape = list(array.shape)
        shape[axis] = full
        return lax.dynamic_update_slice_in_dim(
            jnp.zeros(shape, array.dtype), array, member * array.shape[axis], axis
        )

    info, segr = row_facts(seq_lengths[0], rows)
    w_small = jnp.concatenate([mine(w_decay, 1, nh), mine(w_beta, 1, nh)], axis=1)
    w_small = jnp.pad(w_small, ((0, 0), (0, 128 - 2 * nh))).astype(bf16)
    taps = jnp.concatenate(
        [mine(conv_query, 1, nh * DK), mine(conv_keys, 1, nh * DK), mine(conv_value, 1, nh * DV)], axis=1
    )
    taps = top(8, taps)
    vec = jnp.stack([jnp.exp(mine(a_log, 0, nh)), mine(dt_bias, 0, nh)])
    vec = top(8, jnp.pad(vec, ((0, 0), (0, 128 - nh))))
    gain_o = top(8, gain_out[None])
    gain_1 = top(8, gain_one[None])
    gain_2 = top(8, gain_two[None])

    x = tokens.astype(f32)
    normed_own = (x * lax.rsqrt(jnp.mean(x * x, axis=-1, keepdims=True) + NORM_EPS) * gain_one).astype(bf16)
    cast = [
        by_member([query_key[0].astype(bf16), query_key[1].astype(bf16), value_gate[0].astype(bf16), value_gate[1].astype(bf16)], n_s),
        by_member([gate_up[0].astype(bf16), gate_up[1].astype(bf16)], n_s),
        output_weight.astype(bf16),
        down_weight.astype(bf16),
    ]
    order = [(0, i, 1) for i in range(n_s)] + [(2, 0, 0)] + [(1, i, 1) for i in range(n_s)] + [(3, 0, 0)]
    w_in, w_gu, w_out, w_dn, normed, dy = gather(
        cast[:2], cast[2:], [normed_own, cotangent], n_dp, n_s, 0, tuple(order)
    )
    w_in = w_in.reshape(D, -1)
    w_gu = w_gu.reshape(D, -1)
    w_out = w_out.reshape(-1, D)
    w_dn = w_dn.reshape(-1, D)
    normed = normed.reshape(rows, D)
    dy = dy.reshape(rows, D)

    raw = mm(normed, w_in, 1, 0)
    raw_small = mm(normed, w_small, 1, 0)
    gated, mixed, updates, states, inverses = m1(raw, raw_small, taps, vec, gain_o, info, segr, PASSES)
    part = mm(gated, w_out, 1, 0, bf16).reshape(n_s, local, D)
    middle, normed_two = mid(part, tokens, gain_2, n_s, 1)
    normed_two = normed_two.reshape(rows, D)
    gu = mm(normed_two, w_gu, 1, 0)
    gate = gu[:, :ff]
    upper = gu[:, ff:]
    sig = jax.nn.sigmoid(gate)
    hidden = (gate * sig * upper).astype(bf16)
    y_part = mm(hidden, w_dn, 1, 0, bf16).reshape(n_s, local, D)
    d_hidden = mm(dy, w_dn, 1, 1)
    d_gate = (d_hidden * upper * sig * (1.0 + gate * (1.0 - sig))).astype(bf16)
    d_upper = (d_hidden * (gate * sig)).astype(bf16)
    d_gu = jnp.concatenate([d_gate, d_upper], axis=1)
    d_part = mm(d_gu, w_gu, 1, 1, bf16).reshape(n_s, local, D)
    block_out, d_middle, d_branch, d_gain_two = ffn(y_part, d_part, middle, cotangent, gain_2, n_s, 2)
    d_branch = d_branch.reshape(rows, D)
    part_dn = mm(hidden, dy, 0, 0, bf16)
    part_gu = mm(normed_two, d_gu, 0, 0, bf16)
    part_out = mm(gated, d_branch, 0, 0, bf16)
    d_gated = mm(d_branch, w_out, 1, 1)
    d_raw, d_small, g_taps, g_vec, g_gain = m2(
        raw, raw_small, taps, vec, gain_o, info, segr, d_gated, mixed, updates, states, inverses, PASSES
    )
    d_small = d_small.astype(bf16)
    part_in = mm(normed, d_raw, 0, 0, bf16)
    part_small = mm(normed, d_small, 0, 0)
    d_part_one = (mm(d_raw, w_in, 1, 1) + mm(d_small, w_small, 1, 1)).astype(bf16).reshape(n_s, local, D)
    input_grad, d_gain_one = end(d_part_one, tokens, d_middle, gain_1, n_s, 3)

    kq = nh * DK
    small_local = jnp.concatenate(
        [
            put(part_small[:, :nh], 1, H).reshape(-1),
            put(part_small[:, nh : 2 * nh], 1, H).reshape(-1),
            put(g_taps[:KCONV, :kq], 1, H * DK).reshape(-1),
            put(g_taps[:KCONV, kq : 2 * kq], 1, H * DK).reshape(-1),
            put(g_taps[:KCONV, 2 * kq :], 1, H * DV).reshape(-1),
            d_gain_one[0],
            d_gain_two[0],
            g_gain[0],
            put(g_vec[0, :nh], 0, H),
            put(g_vec[1, :nh], 0, H),
        ]
    )
    small_grad = lax.psum(small_local, ("dp", "shard"))

    g_in, g_gu, grad_out, grad_dn = scatter(
        [part_in.reshape(n_dp, -1, part_in.shape[1]), part_gu.reshape(n_dp, -1, part_gu.shape[1])],
        [part_out.reshape(n_dp, -1, D), part_dn.reshape(n_dp, -1, D)],
        n_dp,
        n_s,
        4,
    )
    grads = [p.astype(f32) for p in whole_rows(g_in, [kq, kq, nh * DV, nh * DV])]
    grads += [grad_out.astype(f32)]
    grads += [p.astype(f32) for p in whole_rows(g_gu, [ff, ff])]
    grads += [grad_dn.astype(f32)]
    masters = [query_key[0], query_key[1], value_gate[0], value_gate[1], output_weight, gate_up[0], gate_up[1], down_weight]
    momenta = [
        momentum_query_key[0],
        momentum_query_key[1],
        momentum_value_gate[0],
        momentum_value_gate[1],
        momentum_output,
        momentum_gate_up[0],
        momentum_gate_up[1],
        momentum_down,
    ]
    moms = [MOMENTUM * m + g for m, g in zip(momenta, grads)]
    looks = [(g + MOMENTUM * m).astype(bf16) for m, g in zip(moms, grads)]
    devices = n_dp * n_s
    pads = []
    for look in looks:
        r_count, c_count = look.shape
        tall = r_count * devices > c_count
        pads.append(top(-(-r_count // 16) * 16, look) if tall else look)
    orthos = muon(pads, n_dp, n_s, 5)
    steps = []
    for master, ortho in zip(masters, orthos):
        r_count, c_count = master.shape
        scale = 0.2 * math.sqrt(max(r_count * devices, c_count))
        steps.append(-MUON_RATE * (scale * ortho[:r_count].astype(f32) + MUON_DECAY * master))
    new_one = BETA_ONE * moment_one + (1.0 - BETA_ONE) * small_grad
    new_two = BETA_TWO * moment_two + (1.0 - BETA_TWO) * small_grad * small_grad
    small_step = (
        -ADAM_RATE
        * (new_one / (1.0 - BETA_ONE**STEP_COUNT))
        / (jnp.sqrt(new_two / (1.0 - BETA_TWO**STEP_COUNT)) + ADAM_EPS)
    )

    def bundle(a):
        return (jnp.stack(a[0:2]), jnp.stack(a[2:4]), a[4], jnp.stack(a[5:7]), a[7])

    return (
        (block_out, input_grad)
        + bundle(grads)
        + bundle(steps)
        + bundle(moms)
        + (small_grad, small_step, new_one, new_two)
    )


def solution(mesh):
    cols = P(None, ("dp", "shard"), None)
    rows = P(("dp", "shard"), None)
    weights = (cols, cols, rows, cols, rows)
    return jax.shard_map(
        functools.partial(body, mesh.shape["dp"], mesh.shape["shard"]),
        mesh=mesh,
        in_specs=(rows, rows) + weights + (P(),) + weights + (P(), P(), P("dp", None)),
        out_specs=(rows, rows) + weights * 3 + (P(),) * 4,
        check_vma=False,
    )
```

```python
import functools
import math

import jax
import jax.numpy as jnp
from jax import lax
from jax.experimental import pallas as pl
from jax.experimental.pallas import tpu as pltpu
from jax.sharding import PartitionSpec as P

DK=128; DV=256; KCONV=4; CH=128
f32=jnp.float32; bf16=jnp.bfloat16
HI=lax.Precision.HIGHEST
GATE_EPS=1e-5; UNIT_EPS=1e-6

def _split(a):
    h=a.astype(bf16)
    return h,(a-h.astype(f32)).astype(bf16)

def dot(a,b,ca,cb,passes=3):
    dn=(((ca,),(cb,)),((),()))
    if passes==6:
        return lax.dot_general(a,b,dn,precision=HI,preferred_element_type=f32)
    if passes==1:
        return lax.dot_general(a.astype(bf16),b.astype(bf16),dn,preferred_element_type=f32)
    ah,al=_split(a); bh,bl=_split(b)
    g=functools.partial(lax.dot_general,dimension_numbers=dn,preferred_element_type=f32)
    return g(ah,bh)+(g(ah,bl)+g(al,bh))

def softplus(x): return jnp.maximum(x,0.0)+jnp.log1p(jnp.exp(-jnp.abs(x)))
def sigmoid(x): return lax.logistic(x)

def iota2(n,ax): return lax.broadcasted_iota(jnp.int32,(n,n),ax)

def inverse(A,p):
    n=A[0].shape[0]
    ri=iota2(n,0); ci=iota2(n,1)
    eye=(ri==ci).astype(f32)
    same=lambda b:(ri//b)==(ci//b)
    pw=[jnp.where(same(16),a,0.0) for a in A]
    X=[eye-q for q in pw]
    for _ in range(3):
        pw=[dot(q,q,1,0,p) for q in pw]
        X=[x+dot(x,q,1,0,p) for x,q in zip(X,pw)]
    b=16
    while b<n:
        m=jnp.logical_and(same(2*b),jnp.logical_not(same(b)))
        off=[jnp.where(m,a,0.0) for a in A]
        t=[dot(o,x,1,0,p) for o,x in zip(off,X)]
        X=[x-dot(x,q,1,0,p) for x,q in zip(X,t)]
        b*=2
    return X

def conv_pre(u,taps,info):
    s=taps[3:4]*u
    for k in (1,2,3):
        s=s+taps[3-k:4-k]*(pltpu.roll(u,k,0)*info[:,k:k+1])
    return s

def l2(u):
    return lax.rsqrt(jnp.sum(u*u,axis=-1,keepdims=True)+UNIT_EPS)

def acts(raw,taps,info,nh):
    out=[]
    kq=nh*DK
    for h in range(nh):
        d={}
        for nm,off,w in (("q",h*DK,DK),("k",kq+h*DK,DK),("v",2*kq+h*DV,DV)):
            pre=conv_pre(raw[:,off:off+w],taps[:,off:off+w],info)
            act=pre*sigmoid(pre)
            d[nm+"pre"]=pre; d[nm]=act
        rq=l2(d["q"])*(DK**-0.5); rk=l2(d["k"])
        d["rq"]=rq; d["rk"]=rk
        d["qn"]=d["q"]*rq; d["kn"]=d["k"]*rk
        out.append(d)
    return out

def decays(small,vec,nh):
    z=small+vec[1:2]
    ld=-vec[0:1]*softplus(z)
    beta=sigmoid(small)
    return z,ld,beta

def chunk_terms(ld,segc,segr,R,nh):
    n=CH
    ri=iota2(n,0); ci=iota2(n,1)
    low=(ri>=ci)
    L=low.astype(f32)
    out=[]
    for c in range(R//n):
        sl=slice(c*n,(c+1)*n)
        ldc=ld[sl]
        cc=dot(L,ldc,1,0,6)
        cr=dot(ldc,L,0,1,6)
        sc=segc[sl]; sr=segr[:,sl]
        M=jnp.logical_and(low,sc==sr)
        prev=segc[c*n-1:c*n] if c else None
        last=segc[(c+1)*n-1:(c+1)*n]
        heads=[]
        for h in range(nh):
            col=cc[:,h:h+1]; row=cr[h:h+1,:]
            R_=jnp.where(M,jnp.exp(jnp.where(M,col-row,0.0)),0.0)
            end=cc[n-1:n,h:h+1]
            t=jnp.where(sc==last,jnp.exp(end-col),0.0)
            if c:
                e=jnp.where(sc==prev,jnp.exp(col),0.0)
                g=jnp.where(last==prev,jnp.exp(end),0.0)
            else:
                e=jnp.zeros_like(col); g=jnp.zeros_like(end)
            heads.append((R_,e,t,g))
        out.append(heads)
    return out

def mixer_fwd(raw,small,taps,vec,gain,info,segr,nh,P):
    R=raw.shape[0]; nc=R//CH; n=CH
    segc=info[:,0:1]
    a=acts(raw,taps,info,nh)
    z,ld,beta=decays(small,vec,nh)
    terms=chunk_terms(ld,segc,segr,R,nh)
    ri=iota2(n,0); ci=iota2(n,1)
    strict=ri>ci
    idx=[(h,c) for c in range(nc) for h in range(nh)]
    sl=lambda c:slice(c*n,(c+1)*n)
    A=[];Pm=[]
    for h,c in idx:
        K=a[h]["kn"][sl(c)]; Q=a[h]["qn"][sl(c)]
        R_=terms[c][h][0]
        b=beta[sl(c),nh+h:nh+h+1]
        A.append(jnp.where(strict,b*R_*dot(K,K,1,1,P["kk"]),0.0))
        Pm.append(dot(Q,K,1,1,P["qk"])*R_)
    X=inverse(A,P["inv"])
    U0=[];W=[]
    for i,(h,c) in enumerate(idx):
        b=beta[sl(c),nh+h:nh+h+1]; e=terms[c][h][1]
        U0.append(dot(X[i],b*a[h]["v"][sl(c)],1,0,P["u"]))
        W.append(dot(X[i],(b*e)*a[h]["kn"][sl(c)],1,0,P["u"]) if c else None)
    S=[None]*nh
    S0s={};Us={};O={}
    for i,(h,c) in enumerate(idx):
        R_,e,t,g=terms[c][h]
        K=a[h]["kn"][sl(c)]; Q=a[h]["qn"][sl(c)]
        S0=S[h]
        U=U0[i] if c==0 else U0[i]-dot(W[i],S0,1,0,P["s"])
        o=dot(Pm[i],U,1,0,P["o"])
        if c: o=o+dot(e*Q,S0,1,0,P["o"])
        up=dot(t*K,U,0,0,P["s"])
        S[h]=up if c==0 else g*S0+up
        S0s[h,c]=S0; Us[h,c]=U; O[h,c]=o
    off=2*nh*DK+nh*DV
    gated={}
    for h,c in idx:
        o=O[h,c]
        r=lax.rsqrt(jnp.mean(o*o,axis=-1,keepdims=True)+GATE_EPS)
        gt=raw[sl(c),off+h*DV:off+(h+1)*DV]
        gated[h,c]=o*r*gain*(gt*sigmoid(gt))
    return gated,O,Us,S0s,{(h,c):X[i] for i,(h,c) in enumerate(idx)}

def gate_back(raw_ref,gain,dgated_ref,o_ref,nh,emit):
    R=raw_ref.shape[0]; nc=R//CH; n=CH
    off=2*nh*DK+nh*DV
    dO={};ggain=None
    for c in range(nc):
        for h in range(nh):
            r_=slice(c*n,(c+1)*n); co=slice(h*DV,(h+1)*DV)
            o=o_ref[r_,co]
            r=lax.rsqrt(jnp.mean(o*o,axis=-1,keepdims=True)+GATE_EPS)
            gt=raw_ref[r_,off+h*DV:off+(h+1)*DV]
            s=sigmoid(gt); sg=gt*s
            dg=dgated_ref[r_,co]
            nrm=o*r
            emit(h,c,dg*nrm*gain*(s*(1.0+gt*(1.0-s))))
            dsn=dg*sg
            part=jnp.sum(dsn*nrm,axis=0,keepdims=True)
            ggain=part if ggain is None else ggain+part
            dn=dsn*gain
            dO[h,c]=r*dn-nrm*(r*jnp.mean(nrm*dn,axis=-1,keepdims=True))
    return dO,ggain

def mixer_bwd(raw_ref,small_ref,taps_ref,vec_ref,info_ref,segr_ref,dO,u_ref,s_ref,x_ref,nh,P,result):
    R=raw_ref.shape[0]; nc=R//CH; n=CH
    raw=raw_ref; taps=taps_ref[...]; vec=vec_ref[...]; info=info_ref[...]
    segc=info[:,0:1]
    a=acts(raw,taps,info,nh)
    z,ld,beta=decays(small_ref[...],vec,nh)
    yield
    terms=chunk_terms(ld,segc,segr_ref[0:1],R,nh)
    ri=iota2(n,0); ci=iota2(n,1)
    strict=ri>ci
    U_=(ri<=ci).astype(f32)
    idx=[(h,c) for c in reversed(range(nc)) for h in range(nh)]
    sl=lambda c:slice(c*n,(c+1)*n)
    yield
    dU0={};KK={};QK={}
    for h,c in idx:
        K=a[h]["kn"][sl(c)]; Q=a[h]["qn"][sl(c)]
        KK[h,c]=dot(K,K,1,1,P["kk"]); QK[h,c]=dot(Q,K,1,1,P["qk"])
        dU0[h,c]=dot(QK[h,c]*terms[c][h][0],dO[h,c],0,0,P["u"])
    yield
    dS=[None]*nh
    dS1s={};Ys={}
    for c in reversed(range(nc)):
        for h in range(nh):
            R_,e,t,g=terms[c][h]
            K=a[h]["kn"][sl(c)]; Q=a[h]["qn"][sl(c)]
            b=beta[sl(c),nh+h:nh+h+1]
            dS1=dS[h]
            dS1s[h,c]=dS1
            dU=dU0[h,c]
            if dS1 is not None: dU=dU+dot(t*K,dS1,1,0,P["s"])
            Y=dot(x_ref[c*nh+h],dU,0,0,P["s"])
            Ys[h,c]=Y
            if c:
                d0=dot(e*Q,dO[h,c],0,0,P["s"])-dot((b*e)*K,Y,0,0,P["s"])
                dS[h]=d0 if dS1 is None else g*dS1+d0
        yield
    dQ={};dK={};dV={};dbeta={};dld={}
    for h,c in idx:
        R_,e,t,g=terms[c][h]
        K=a[h]["kn"][sl(c)]; Q=a[h]["qn"][sl(c)]; V=a[h]["v"][sl(c)]
        b=beta[sl(c),nh+h:nh+h+1]
        Y=Ys[h,c]; U=u_ref[sl(c),h*DV:(h+1)*DV]; dS1=dS1s[h,c]
        dA=jnp.where(strict,-dot(Y,U,1,1,P["g"]),0.0)
        dP=dot(dO[h,c],U,1,1,P["g"])
        H=dP*R_
        Gr=dA*R_
        G=b*Gr
        dq=dot(H,K,1,0,P["g"])
        dk=dot(G,K,1,0,P["g"])+dot(G,K,0,0,P["g"])+dot(H,Q,0,0,P["g"])
        dV[h,c]=b*Y
        db=jnp.sum(Y*V,axis=-1,keepdims=True)+jnp.sum(Gr*KK[h,c],axis=-1,keepdims=True)
        Z=H*QK[h,c]+G*KK[h,c]
        dc=jnp.sum(Z,axis=-1,keepdims=True)-jnp.sum(Z.T,axis=-1,keepdims=True)
        last=(lax.broadcasted_iota(jnp.int32,(n,1),0)==n-1).astype(f32)
        if c:
            S0=s_ref[c*nh+h]
            YS=dot(Y,S0,1,1,P["g"]); OS=dot(dO[h,c],S0,1,1,P["g"])
            dq=dq+e*OS
            dk=dk-(b*e)*YS
            ks=jnp.sum(YS*K,axis=-1,keepdims=True)
            qs=jnp.sum(OS*Q,axis=-1,keepdims=True)
            db=db-e*ks
            dc=dc+e*(qs-b*ks)
        if dS1 is not None:
            US=dot(U,dS1,1,1,P["g"])
            dk=dk+t*US
            tt=t*jnp.sum(US*K,axis=-1,keepdims=True)
            dc=dc-tt
            tot=jnp.sum(tt,axis=0,keepdims=True)
            if c:
                tot=tot+g*jnp.sum(jnp.sum(dS1*S0,axis=-1,keepdims=True),axis=0,keepdims=True)
            dc=dc+last*tot
        dQ[h,c]=dq; dK[h,c]=dk; dbeta[h,c]=db
        dld[h,c]=dc
        if h==nh-1: yield
    lane=lax.broadcasted_iota(jnp.int32,(n,128),1)
    dsm=[]
    for c in range(nc):
        acc_d=jnp.zeros((n,128),f32); acc_b=jnp.zeros((n,128),f32)
        for h in range(nh):
            acc_d=acc_d+jnp.where(lane==h,dld[h,c],0.0)
            acc_b=acc_b+jnp.where(lane==nh+h,dbeta[h,c],0.0)
        acc_d=dot(U_,acc_d,1,0,6)
        dsm.append((acc_d,acc_b))
    dldf=jnp.concatenate([x[0] for x in dsm],axis=0)
    dbf=jnp.concatenate([x[1] for x in dsm],axis=0)
    dz=-dldf*vec[0:1]*sigmoid(z)
    dsmall=dz+dbf*beta*(1.0-beta)
    g_dt=jnp.sum(dz,axis=0,keepdims=True)
    g_al=jnp.sum(dldf*ld,axis=0,keepdims=True)
    result.append((dsmall,g_dt,g_al))
    for nm in ("q","k","v"):
        for h in range(nh):
            d=a[h]
            w=DV if nm=="v" else DK
            coff={"q":h*DK,"k":nh*DK+h*DK,"v":2*nh*DK+h*DV}[nm]
            dy=jnp.concatenate([{"q":dQ,"k":dK,"v":dV}[nm][h,c] for c in range(nc)],axis=0)
            if nm!="v":
                y=d[nm+"n"]
                if nm=="q": y=y*(DK**0.5)
                dy=d["r"+nm]*(dy-y*jnp.sum(y*dy,axis=-1,keepdims=True))
            pre=d[nm+"pre"]; s=sigmoid(pre)
            dp=dy*(s*(1.0+pre*(1.0-s)))
            u=raw[:,coff:coff+w]; tp=taps[:,coff:coff+w]
            du=tp[3:4]*dp
            tg=[None]*4
            tg[3]=jnp.sum(dp*u,axis=0,keepdims=True)
            for k in (1,2,3):
                su=pltpu.roll(dp,dp.shape[0]-k,0)*info[:,3+k:4+k]
                du=du+tp[3-k:4-k]*su
                tg[3-k]=jnp.sum(su*u,axis=0,keepdims=True)
            result.append((coff,w,du,tg))
        yield

def m1_kernel(nh,P,raw_ref,small_ref,taps_ref,vec_ref,gain_ref,info_ref,segr_ref,gated_ref,o_ref,u_ref,s_ref,x_ref):
    gated,O,U,S0,X=mixer_fwd(raw_ref[...],small_ref[...],taps_ref[...],vec_ref[...],gain_ref[0:1],info_ref[...],segr_ref[0:1],nh,P)
    n=CH
    for (h,c) in gated:
        r=slice(c*n,(c+1)*n); co=slice(h*DV,(h+1)*DV)
        gated_ref[r,co]=gated[h,c].astype(bf16)
        o_ref[r,co]=O[h,c]; u_ref[r,co]=U[h,c]
        x_ref[c*nh+h]=X[h,c]
        s_ref[c*nh+h]=S0[h,c] if c else jnp.zeros((DK,DV),f32)

def m1(raw,small,taps,vec,gain,info,segr,P):
    R=raw.shape[0]; nh=raw.shape[1]//(2*DK+2*DV); nb=nh*R//CH
    vm=pl.BlockSpec(memory_space=pltpu.VMEM)
    return pl.pallas_call(functools.partial(m1_kernel,nh,P),
      out_shape=[jax.ShapeDtypeStruct((R,nh*DV),bf16),jax.ShapeDtypeStruct((R,nh*DV),f32),jax.ShapeDtypeStruct((R,nh*DV),f32),
                 jax.ShapeDtypeStruct((nb,DK,DV),f32),jax.ShapeDtypeStruct((nb,CH,CH),f32)],
      in_specs=[vm]*7,out_specs=[vm]*5,
      compiler_params=pltpu.CompilerParams(vmem_limit_bytes=56<<20),name="mixer_forward")(raw,small,taps,vec,gain,info,segr)


f32=jnp.float32; bf16=jnp.bfloat16
MESH=pl.DeviceIdType.MESH
ANY=pl.BlockSpec(memory_space=pl.ANY)
VM=pl.BlockSpec(memory_space=pltpu.VMEM)

def place():
    d=lax.axis_index("dp"); s=lax.axis_index("shard")
    return d,s,d//2,d%2

def greet(peers):
    bar=pltpu.get_barrier_semaphore()
    for p in peers:
        pl.semaphore_signal(bar,inc=1,device_id=p,device_id_type=MESH)
    pl.semaphore_wait(bar,len(peers))

def remote(src,dst,ss,rs,dev):
    return pltpu.make_async_remote_copy(src_ref=src,dst_ref=dst,send_sem=ss,recv_sem=rs,device_id=dev,device_id_type=MESH)

def gather_kernel(n_dp,n_s,ncol,nrow,nact,order,W,*refs):
    n=ncol+nrow+nact
    ins=refs[:n]; outs=refs[n:2*n]
    s0,r0,s1,r1,sa,ra,lsem=refs[2*n:]
    d,s,hi,lo=place()
    n_hi=n_dp//2
    np_=ncol+nrow
    me=d*n_s+s
    td=me%n_dp; ts=me//n_dp
    fd=(s*n_dp+d)//n_s; fs=(s*n_dp+d)%n_s
    zs=[((hi+j)%n_hi)*2+lo for j in range(1,n_hi)]
    xd=hi*2+(1-lo)
    grp=[(d,(s+j)%n_s) for j in range(1,n_s)]
    bar=pltpu.get_barrier_semaphore()
    peers=grp+[(z,s) for z in zs]+[(xd,s)]
    moved=jnp.logical_or(td!=d,ts!=s)
    for p in peers:
        pl.semaphore_signal(bar,inc=1,device_id=p,device_id_type=MESH)
    @pl.when(moved)
    def _():
        pl.semaphore_signal(bar,inc=1,device_id=(td,ts),device_id_type=MESH)
        pl.semaphore_signal(bar,inc=1,device_id=(fd,fs),device_id_type=MESH)
    @pl.when(moved)
    def _():
        pl.semaphore_wait(bar,len(peers)+2)
    @pl.when(jnp.logical_not(moved))
    def _():
        pl.semaphore_wait(bar,len(peers))
    sends=[]
    local=[]
    for k in range(nact):
        src=ins[np_+k]; dst=outs[np_+k]
        c=pltpu.make_async_copy(src,dst.at[s],lsem.at[np_+k]); c.start(); local.append(c)
        for j,p in enumerate(grp):
            c=remote(src,dst.at[s],sa.at[k,j],ra.at[k,j],p); c.start(); sends.append(c)
    col={}
    def phase0(k):
        if k<ncol:
            c=pltpu.make_async_copy(ins[k].at[s],outs[k].at[d,s],lsem.at[k]); c.start()
            col[k]=[c]
            for j,p in enumerate(grp):
                c=remote(ins[k].at[p[1]],outs[k].at[d,s],s0.at[k,j],r0.at[k,j],p); c.start(); col[k].append(c)
        else:
            @pl.when(moved)
            def _():
                remote(ins[k],outs[k].at[td],s0.at[k,0],r0.at[k,0],(td,ts)).start()
            @pl.when(jnp.logical_not(moved))
            def _():
                pltpu.make_async_copy(ins[k],outs[k].at[d],r0.at[k,0]).start()
    def ready(k):
        if k<ncol:
            for c in col[k]: c.wait()
        else:
            pltpu.make_async_copy(ins[k],outs[k].at[d],r0.at[k,0]).wait()
            @pl.when(moved)
            def _():
                remote(ins[k],outs[k].at[td],s0.at[k,0],r0.at[k,0],(td,ts)).wait_send()
    pieces=[]
    for k,_,_ in order:
        if k not in pieces: pieces.append(k)
    for k in pieces: phase0(k)
    def blk(i,src):
        k,a,m=order[i]
        return outs[k].at[src,a:a+m] if m else outs[k].at[src]
    def first(i):
        own=blk(i,d)
        for j,z in enumerate(zs):
            remote(own,own,s1.at[i,j],r1.at[i,j],(z,s)).start()
        remote(own,own,s1.at[i,n_hi-1],r1.at[i,n_hi-1],(xd,s)).start()
    def second(i):
        for j in range(1,n_hi):
            b=blk(i,((hi-j)%n_hi)*2+lo)
            remote(b,b,s1.at[i,j-1],r1.at[i,j-1],(xd,s)).wait()
            remote(b,b,s1.at[i,n_hi-1+j],r1.at[i,n_hi-1+j],(xd,s)).start()
    def third(i):
        for j in range(n_hi):
            b=blk(i,((hi-j)%n_hi)*2+(1-lo))
            remote(b,b,s1.at[i,n_hi-1+j],r1.at[i,n_hi-1+j],(xd,s)).wait()
    done=set()
    nch=len(order)
    for i in range(nch+W+1):
        if i<nch:
            k=order[i][0]
            if k not in done:
                ready(k); done.add(k)
            first(i)
        if 0<=i-W<nch: second(i-W)
        if 0<=i-W-1<nch: third(i-W-1)
    for k in range(nact): local[k].wait()
    for c in sends: c.wait()

def gather(cols,rows,acts,n_dp,n_s,cid,order,W=1):
    pieces=list(cols)+list(rows); np_=len(pieces); n_hi=n_dp//2
    shapes=[jax.ShapeDtypeStruct((n_dp,)+x.shape,x.dtype) for x in pieces]+[jax.ShapeDtypeStruct((n_s,)+x.shape,x.dtype) for x in acts]
    D=pltpu.SemaphoreType.DMA
    na=max(len(acts),1); nch=len(order)
    return pl.pallas_call(functools.partial(gather_kernel,n_dp,n_s,len(cols),len(rows),len(acts),order,W),
        out_shape=shapes,in_specs=[ANY]*(np_+len(acts)),out_specs=[ANY]*(np_+len(acts)),
        scratch_shapes=[D((np_,n_s)),D((np_,n_s)),D((nch,2*n_hi)),D((nch,2*n_hi)),D((na,n_s)),D((na,n_s)),D((np_+na,))],
        compiler_params=pltpu.CompilerParams(collective_id=cid,has_side_effects=True),name="gather_weights")(*pieces,*acts)

NORM_EPS=1e-6
D_=pltpu.SemaphoreType.DMA
def ring(n_s):
    d,s,_,_=place()
    return [(d,(s+j)%n_s) for j in range(1,n_s)]

def push_parts(n_s,part,land,ss,rs):
    cs=[]
    for j,p in enumerate(ring(n_s)):
        c=remote(part.at[p[1]],land.at[j],ss.at[j],rs.at[j],p); c.start(); cs.append(c)
    return cs

def push_all(n_s,out,ss,rs):
    _,s,_,_=place()
    cs=[]
    for j,p in enumerate(ring(n_s)):
        c=remote(out.at[s],out.at[s],ss.at[j],rs.at[j],p); c.start(); cs.append(c)
    return cs

def add_up(n_s,part,land):
    _,s,_,_=place()
    t=part[s].astype(f32)
    for j in range(n_s-1): t=t+land[j].astype(f32)
    return t

def norm_back(u,g,dn):
    w=u.shape[-1]
    r=lax.rsqrt(jnp.mean(u*u,axis=-1,keepdims=True)+NORM_EPS)
    gd=g*dn
    du=r*gd-u*(r*r*r*(jnp.sum(u*gd,axis=-1,keepdims=True)/w))
    return du,jnp.sum(u*r*dn,axis=0,keepdims=True)

def mid_kernel(n_s,part,x,gain,middle,gathered,land,s0,r0,s1,r1):
    _,s,_,_=place()
    greet(ring(n_s))
    a=push_parts(n_s,part,land,s0,r0)
    for c in a: c.wait()
    m=x[...].astype(f32)+add_up(n_s,part,land)
    middle[...]=m
    r=lax.rsqrt(jnp.mean(m*m,axis=-1,keepdims=True)+NORM_EPS)
    gathered[s]=(m*r*gain[0:1]).astype(bf16)
    for c in push_all(n_s,gathered,s1,r1): c.wait()

def mid(part,x,gain,n_s,cid):
    rows,w=x.shape
    return pl.pallas_call(functools.partial(mid_kernel,n_s),
        out_shape=[jax.ShapeDtypeStruct((rows,w),f32),jax.ShapeDtypeStruct((n_s,rows,w),bf16)],
        in_specs=[VM]*3,out_specs=[VM]*2,
        scratch_shapes=[pltpu.VMEM((n_s-1,rows,w),bf16)]+[D_((n_s,))]*4,
        compiler_params=pltpu.CompilerParams(collective_id=cid,has_side_effects=True,vmem_limit_bytes=40<<20),name="branch_sum")(part,x,gain)


f32=jnp.float32; bf16=jnp.bfloat16
CA,CB,CC=3.4445,-4.775,2.0315
def dg(a,b,ca,cb): return lax.dot_general(a,b,(((ca,),(cb,)),((),())),preferred_element_type=f32)
TB=256
def ns_wide(x,y,g,p,cols,iters=2,tm=256,tn=512):
    r=g.shape[0]
    cs=slice(0,cols)
    def sq(i,a):
        v=x[pl.ds(i*TB,TB),cs].astype(f32)
        return a+jnp.sum(v*v,axis=0,keepdims=True)
    t=lax.fori_loop(0,r//TB,sq,jnp.zeros((1,cols),f32))
    inv=1.0/(jnp.sqrt(jnp.sum(t,axis=1,keepdims=True))+1e-7)
    def sc(i,_):
        x[pl.ds(i*TB,TB),cs]=(x[pl.ds(i*TB,TB),cs].astype(f32)*inv).astype(bf16)
        return 0
    lax.fori_loop(0,r//TB,sc,0)
    a,b=x,y
    for _ in range(iters):
        def gram(i,_):
            ri=pl.ds(pl.multiple_of(i*tm,tm),tm)
            g[ri,:]=dg(a[ri,cs],a[:,cs],1,1).astype(bf16)
            return 0
        lax.fori_loop(0,r//tm,gram,0)
        def poly(i,_):
            ri=pl.ds(pl.multiple_of(i*tm,tm),tm)
            p[ri,:]=(CB*g[ri,:].astype(f32)+CC*dg(g[ri,:],g[...],1,0)).astype(bf16)
            return 0
        lax.fori_loop(0,r//tm,poly,0)
        def nxt(i,_):
            ri=pl.ds(pl.multiple_of(i*tm,tm),tm)
            b[ri,cs]=(CA*a[ri,cs].astype(f32)+dg(p[ri,:],a[:,cs],1,0)).astype(bf16)
            return 0
        lax.fori_loop(0,r//tm,nxt,0)
        a,b=b,a
def ns_tall(x,y,g,p,n=None,iters=2,tm=256):
    n=n or x.shape[0]; r=x.shape[1]
    def sq(i,a):
        v=x[pl.ds(i*TB,TB),:].astype(f32)
        return a+jnp.sum(v*v,axis=0,keepdims=True)
    t=lax.fori_loop(0,n//TB,sq,jnp.zeros((1,r),f32))
    inv=1.0/(jnp.sqrt(jnp.sum(t,axis=1,keepdims=True))+1e-7)
    def sc(i,_):
        x[pl.ds(i*TB,TB),:]=(x[pl.ds(i*TB,TB),:].astype(f32)*inv).astype(bf16)
        return 0
    lax.fori_loop(0,n//TB,sc,0)
    a,b=x,y
    for _ in range(iters):
        for j in range(r//tm):
            cj=slice(j*tm,(j+1)*tm)
            g[cj,:]=dg(a[0:n,cj],a[0:n,:],0,0).astype(bf16)
        def poly(i,_):
            ri=pl.ds(pl.multiple_of(i*tm,tm),tm)
            p[ri,:]=(CB*g[ri,:].astype(f32)+CC*dg(g[ri,:],g[...],1,0)).astype(bf16)
            return 0
        lax.fori_loop(0,r//tm,poly,0)
        def nxt(i,_):
            ri=pl.ds(pl.multiple_of(i*tm,tm),tm)
            b[ri,:]=(CA*a[ri,:].astype(f32)+dg(a[ri,:],p[...],1,0)).astype(bf16)
            return 0
        lax.fori_loop(0,n//tm,nxt,0)
        a,b=b,a


def muon_owner(i,n_dp):
    base=n_dp//2-2
    d,s=((2,0),(3,0),(1,2),(3,2),(2,2),(0,0),(1,0),(0,2))[i]
    return base+d,s

def muon_kernel(n_dp,n_s,kinds,*refs):
    n=len(kinds)
    ins=refs[:n]; outs=refs[n:2*n]
    wide,wide2,tall,tall2,g,p,rin,sin,rout,sout,lsem=refs[2*n:]
    d,s,_,_=place()
    nd=n_dp*n_s
    me=d*n_s+s
    own=[muon_owner(i,n_dp) for i in range(n)]
    base=n_dp//2-2
    is_owner=lambda dd,ss: jnp.logical_and(jnp.logical_and(dd>=base,dd<base+4),ss%2==0)
    mine=is_owner(d,s)
    bar=pltpu.get_barrier_semaphore()
    for o in own:
        @pl.when(jnp.logical_or(d!=o[0],s!=o[1]))
        def _():
            pl.semaphore_signal(bar,inc=1,device_id=o,device_id_type=MESH)
    @pl.when(mine)
    def _():
        def greet_one(q,_):
            dd=q//n_s; ss=q%n_s
            @pl.when(jnp.logical_not(is_owner(dd,ss)))
            def _():
                pl.semaphore_signal(bar,inc=1,device_id=(dd,ss),device_id_type=MESH)
            return 0
        lax.fori_loop(0,nd,greet_one,0)
        pl.semaphore_wait(bar,nd-1)
    @pl.when(jnp.logical_not(mine))
    def _():
        pl.semaphore_wait(bar,n)
    def slot(buf,i,q):
        t,rows,cols=kinds[i]
        ds=pl.ds(pl.multiple_of(q*rows,rows),rows)
        return buf.at[ds] if t else buf.at[ds,pl.ds(0,cols)]
    for i in range(n):
        t,rows,cols=kinds[i]
        dst=slot(tall if t else wide,i,me)
        there=jnp.logical_and(d==own[i][0],s==own[i][1])
        @pl.when(there)
        def _():
            pltpu.make_async_copy(ins[i],dst,rin.at[0]).start()
        @pl.when(jnp.logical_not(there))
        def _():
            remote(ins[i],dst,sin.at[i],rin.at[0],own[i]).start()
    for i in range(n):
        t,rows,cols=kinds[i]
        there=jnp.logical_and(d==own[i][0],s==own[i][1])
        @pl.when(there)
        def _():
            buf=tall if t else wide
            full=buf.at[pl.ds(0,rows*nd)] if t else buf.at[:,pl.ds(0,cols)]
            pltpu.make_async_copy(full,full,rin.at[0]).wait()
            if t: ns_tall(tall,tall2,g,p,n=rows*nd)
            else: ns_wide(wide,wide2,g,p,cols,tm=512 if cols>1024 else 256)
            def send(q,_):
                src=slot(buf,i,q)
                @pl.when(q==me)
                def _():
                    pltpu.make_async_copy(src,outs[i],rout.at[i]).start()
                @pl.when(q!=me)
                def _():
                    remote(src,outs[i],sout.at[0],rout.at[i],(q//n_s,q%n_s)).start()
                return 0
            lax.fori_loop(0,nd,send,0)
            part=buf.at[pl.ds(0,rows*(nd-1))] if t else buf.at[pl.ds(0,rows*(nd-1)),pl.ds(0,cols)]
            pltpu.make_async_copy(part,part,sout.at[0]).wait()
    for i in range(n):
        there=jnp.logical_and(d==own[i][0],s==own[i][1])
        @pl.when(jnp.logical_not(there))
        def _():
            pltpu.make_async_copy(ins[i],ins[i],sin.at[i]).wait()
        pltpu.make_async_copy(ins[i],outs[i],rout.at[i]).wait()

def muon(looks,n_dp,n_s,cid):
    nd=n_dp*n_s
    kinds=[]
    for x in looks:
        r,c=x.shape
        kinds.append((r*nd>c,r,c))
    r=min(min(k[1]*nd,k[2]) for k in kinds)
    wc=max(k[2] for k in kinds if not k[0]); tr=max(k[1]*nd for k in kinds if k[0])
    V=pltpu.VMEM
    return pl.pallas_call(functools.partial(muon_kernel,n_dp,n_s,tuple(kinds)),
        out_shape=[jax.ShapeDtypeStruct(x.shape,bf16) for x in looks],in_specs=[VM]*8,out_specs=[VM]*8,
        scratch_shapes=[V((r,wc),bf16)]*2+[V((tr,r),bf16)]*2+[V((r,r),bf16)]*2+[D_((1,)),D_((8,)),D_((8,)),D_((1,)),D_((1,))],
        compiler_params=pltpu.CompilerParams(collective_id=cid,has_side_effects=True,vmem_limit_bytes=60<<20),name="muon")(*looks)


class Reducer:
    def __init__(self,n_dp,n_s,pieces,sems,W):
        self.n_s=n_s; self.n_hi=n_dp//2; self.p=pieces; self.W=W
        self.sx,self.rx,self.sz,self.rz,self.sf,self.rf,self.lsem=sems
        d,s,hi,lo=place()
        self.s=s; self.hi=hi; self.lo=lo
        me=s*n_dp+d
        self.td=me//n_s; self.ts=me%n_s
        own=d*n_s+s
        self.fd=own%n_dp; self.fs=own//n_dp
        self.moved=jnp.logical_or(self.td!=d,self.ts!=s)
        self.xd=(hi*2+(1-lo),s)
        self.zd=lambda j:(((hi+j)%self.n_hi)*2+lo,s)
        self.grp=ring(n_s)
        self.q=[]; self.ns=0; self.nh=0; self.late=[]; self.fc={}
    def greet(self):
        bar=pltpu.get_barrier_semaphore()
        peers=self.grp+[self.zd(j) for j in range(1,self.n_hi)]+[self.xd]
        for p in peers: pl.semaphore_signal(bar,inc=1,device_id=p,device_id_type=MESH)
        @pl.when(self.moved)
        def _():
            pl.semaphore_signal(bar,inc=1,device_id=(self.td,self.ts),device_id_type=MESH)
            pl.semaphore_signal(bar,inc=1,device_id=(self.fd,self.fs),device_id_type=MESH)
            pl.semaphore_wait(bar,len(peers)+2)
        @pl.when(jnp.logical_not(self.moved))
        def _():
            pl.semaphore_wait(bar,len(peers))
    def xc(self,k,j):
        z=(self.hi+j)%self.n_hi; p=self.p[k]
        return remote(p["g"].at[z*2+1-self.lo],p["xl"].at[j],self.sx.at[k,j],self.rx.at[k,j],self.xd)
    def xw(self,k,j):
        return self.xc(k,j)
    def zc(self,k,j):
        p=self.p[k]
        return remote(p["zb"].at[j-1],p["zl"].at[j-1],self.sz.at[k,j],self.rz.at[k,j],self.zd(j))
    def add(self,k):
        self.q+=[(k,j) for j in list(range(1,self.n_hi))+[0]]
    def handle(self,k,j):
        p=self.p[k]; z=(self.hi+j)%self.n_hi
        self.xw(k,j).wait()
        t=p["g"][z*2+self.lo].astype(f32)+p["xl"][j].astype(f32)
        if j:
            p["zb"][j-1]=t.astype(bf16); self.zc(k,j).start()
        else:
            p["own"][...]=t
            self.late.append([k,2])
    def finish(self,k):
        p=self.p[k]; t=p["own"][...]
        for j in range(1,self.n_hi):
            self.zc(k,j).wait()
            t=t+p["zl"][j-1].astype(f32)
        t=t.astype(bf16)
        fin,out=p["fin"],p["out"]
        if p["col"]:
            rows=t.shape[0]//self.n_s
            fin[...]=t.reshape(self.n_s,rows,t.shape[1])
            c=pltpu.make_async_copy(fin.at[self.s],out.at[self.s],self.lsem.at[k]); c.start()
            self.fc[k]=[c]
            for j,q in enumerate(self.grp):
                c=remote(fin.at[q[1]],out.at[self.s],self.sf.at[k,j],self.rf.at[k,j],q); c.start(); self.fc[k].append(c)
        else:
            fin[...]=t
            @pl.when(self.moved)
            def _():
                remote(fin,out,self.sf.at[k,0],self.rf.at[k,0],(self.td,self.ts)).start()
            @pl.when(jnp.logical_not(self.moved))
            def _():
                pltpu.make_async_copy(fin,out,self.rf.at[k,0]).start()
    def tick(self,times=1):
        for _ in range(times):
            if self.ns<len(self.q):
                self.xc(*self.q[self.ns]).start(); self.ns+=1
                if self.ns-self.nh>self.W:
                    self.handle(*self.q[self.nh]); self.nh+=1
            elif self.nh<self.ns:
                self.handle(*self.q[self.nh]); self.nh+=1
            for e in list(self.late):
                e[1]-=1
                if e[1]<0:
                    self.late.remove(e); self.finish(e[0])
    def drain(self):
        while self.nh<len(self.q) or self.late: self.tick()
        for k,p in enumerate(self.p):
            if p["col"]:
                for c in self.fc[k]: c.wait()
            else:
                pltpu.make_async_copy(p["fin"],p["out"],self.rf.at[k,0]).wait()
                @pl.when(self.moved)
                def _():
                    remote(p["fin"],p["out"],self.sf.at[k,0],self.rf.at[k,0],(self.td,self.ts)).wait_send()

def dotb(a,b,ca,cb): return lax.dot_general(a,b,(((ca,),(cb,)),((),())),preferred_element_type=f32)

def back_kernel(n_dp,n_s,nh,P,W,*refs):
    (gu_ref,dn_ref,ypart,dpart,middle,dy,x_ref,gain2,gain1,w_out,w_in,w_sm,raw,small,taps,vec,gain,info,segr,normed,gated,o_ref,u_ref,s_ref,xi_ref,
     out_gu,out_dn,out_out,out_g,out_q,bout,igrad,psm,gtaps,gvec,ggain,dg1,dg2,
     yland,dland,eland,gath,dgt,draw,dsb,epart,dmid,
     p_out,p_g,p_q)=refs[:50]
    rest=refs[50:]
    xl=rest[0:5]; zb=rest[5:10]; zl=rest[10:15]; own=rest[15:20]; fin=rest[20:25]
    sems=rest[25:32]; ss,rs=rest[32:34]
    gs=(gu_ref,dn_ref,p_out,p_g,p_q); outs=(out_gu,out_dn,out_out,out_g,out_q)
    pieces=[dict(g=gs[k],xl=xl[k],zb=zb[k],zl=zl[k],own=own[k],fin=fin[k],out=outs[k],col=k in (0,3,4)) for k in range(5)]
    E=Reducer(n_dp,n_s,pieces,sems,W)
    s=E.s
    E.greet()
    b=push_parts(n_s,dpart,dland,ss.at[0],rs.at[0])
    E.add(0); E.add(1)
    E.tick(2)
    for c in b: c.wait()
    m=middle[...]
    du,dg=norm_back(m,gain2[0:1],add_up(n_s,dpart,dland))
    dm=dy[...].astype(f32)+du
    dmid[...]=dm
    dg2[...]=jnp.broadcast_to(dg,dg2.shape)
    gath[s]=dm.astype(bf16)
    g=push_all(n_s,gath,ss.at[1],rs.at[1])
    E.tick(1)
    for c in g: c.wait()
    a=push_parts(n_s,ypart,yland,ss.at[2],rs.at[2])
    rows=raw.shape[0]; D=gath.shape[2]
    dbr=gath[...].reshape(rows,D)
    dgt[...]=dotb(dbr,w_out[...],1,1)
    E.tick(1)
    p_out[...]=dotb(gated[...],dbr,0,0).astype(bf16).reshape(p_out.shape)
    E.add(2)
    n=CH; off=2*nh*DK+nh*DV
    def emit(h,c,v): draw[c*n:(c+1)*n,off+h*DV:off+(h+1)*DV]=v.astype(bf16)
    dO,gg=gate_back(raw,gain[0:1],dgt,o_ref,nh,emit)
    ggain[...]=jnp.broadcast_to(gg,ggain.shape)
    E.tick(1)
    p_g[...]=dotb(normed[...],draw[:,off:],0,0).astype(bf16).reshape(p_g.shape)
    E.add(3)
    res=[]
    for _ in mixer_bwd(raw,small,taps,vec,info,segr,dO,u_ref,s_ref,xi_ref,nh,P,res):
        E.tick(1)
    dsmall,g_dt,g_al=res[0]
    gtaps[...]=jnp.zeros_like(gtaps); gvec[...]=jnp.zeros_like(gvec)
    for coff,w,dcol,tg in res[1:]:
        draw[:,coff:coff+w]=dcol.astype(bf16)
        for i in range(4): gtaps[i:i+1,coff:coff+w]=tg[i]
    gvec[0:1]=g_al; gvec[1:2]=g_dt
    dsb[...]=dsmall.astype(bf16)
    p_q[...]=dotb(normed[...],draw[:,:off],0,0).astype(bf16).reshape(p_q.shape)
    E.add(4)
    E.tick(2)
    epart[...]=(dotb(draw[...],w_in[...],1,1)+dotb(dsb[...],w_sm[...],1,1)).astype(bf16).reshape(epart.shape)
    e=push_parts(n_s,epart,eland,ss.at[3],rs.at[3])
    for c in a: c.wait()
    bout[...]=(middle[...]+add_up(n_s,ypart,yland)).astype(bf16)
    psm[...]=dotb(normed[...],dsb[...],0,0)
    E.tick(2)
    for c in e: c.wait()
    du,dg=norm_back(x_ref[...].astype(f32),gain1[0:1],add_up(n_s,epart,eland))
    igrad[...]=(dmid[...]+du).astype(bf16)
    dg1[...]=jnp.broadcast_to(dg,dg1.shape)
    E.drain()

def back(part_gu,part_dn,ypart,dpart,middle,dy,x,gain2,gain1,w_out,w_in,w_sm,raw,small,taps,vec,gain,info,segr,normed,gated,O,U,S,X,n_dp,n_s,P,cid,W=2):
    ins=[part_gu,part_dn,ypart,dpart,middle,dy,x,gain2,gain1,w_out,w_in,w_sm,raw,small,taps,vec,gain,info,segr,normed,gated,O,U,S,X]
    local,D=x.shape; rows=local*n_s; nh=raw.shape[1]//(2*DK+2*DV); n_hi=n_dp//2
    off=2*nh*DK+nh*DV
    shp=[part_gu.shape,part_dn.shape,(n_dp,w_out.shape[0]//n_dp,D),(n_dp,D//n_dp,nh*DV),(n_dp,D//n_dp,off)]
    col=(0,3,4)
    osh=[(n_s,q[1]//n_s,q[2]) if k in col else q[1:] for k,q in enumerate(shp)]
    S_=jax.ShapeDtypeStruct; V=pltpu.VMEM
    outs=[S_(q,bf16) for q in osh]+[S_((local,D),bf16),S_((local,D),bf16),S_((D,128),f32),S_((8,off),f32),S_((8,128),f32),S_((8,DV),f32),S_((8,D),f32),S_((8,D),f32)]
    sc=[V((n_s-1,local,D),bf16)]*3+[V((n_s,local,D),bf16),V((rows,nh*DV),f32),V((rows,raw.shape[1]),bf16),V((rows,128),bf16),V((n_s,local,D),bf16),V((local,D),f32)]
    sc+=[V(shp[k],bf16) for k in (2,3,4)]
    sc+=[V((n_hi,)+q[1:],bf16) for q in shp]+[V((n_hi-1,)+q[1:],bf16) for q in shp]*2+[V(q[1:],f32) for q in shp]+[V(q,bf16) for q in osh]
    sc+=[D_((5,n_hi))]*4+[D_((5,n_s))]*2+[D_((5,))]+[D_((4,n_s))]*2
    return pl.pallas_call(functools.partial(back_kernel,n_dp,n_s,nh,P,W),
        out_shape=outs,in_specs=[VM]*len(ins),out_specs=[VM]*len(outs),scratch_shapes=sc,
        compiler_params=pltpu.CompilerParams(collective_id=cid,has_side_effects=True,vmem_limit_bytes=63<<20),name="backward")(*ins)


D = 1024
H = 8
STEP_COUNT = 10
MOMENTUM = 0.95
MUON_RATE = 0.1
MUON_DECAY = 0.01
ADAM_RATE = 0.05
BETA_ONE = 0.9
BETA_TWO = 0.95
ADAM_EPS = 1e-08
PASSES = dict(kk=3, qk=3, inv=3, u=3, s=3, o=3, g=3)


def unpack(packed):
    layouts = [(D, H), (D, H), (KCONV, H * DK), (KCONV, H * DK), (KCONV, H * DV), (D,), (D,), (DV,), (H,), (H,)]
    pieces = []
    offset = 0
    for layout in layouts:
        amount = math.prod(layout)
        pieces.append(packed[offset : offset + amount].reshape(layout))
        offset = offset + amount
    return pieces


def mm(a, b, ca, cb, kind=f32):
    return lax.dot_general(
        a, b, (((ca,), (cb,)), ((), ())), preferred_element_type=f32
    ).astype(kind)


def row_facts(lengths, rows):
    count = lengths.shape[0]
    ends = jnp.sum(jnp.where(jnp.arange(count)[:, None] >= jnp.arange(count)[None, :], lengths[None, :], 0), axis=1)
    pos = jnp.arange(rows, dtype=jnp.int32)

    def number(p):
        seg = jnp.sum((p[:, None] >= ends[None, :]).astype(jnp.int32), axis=1)
        return jnp.where(p < 0, -1, seg).astype(f32)

    seg = number(pos)
    cols = [seg]
    for k in (1, 2, 3):
        cols.append((number(pos - k) == seg).astype(f32))
    for k in (1, 2, 3):
        cols.append((number(pos + k) == seg).astype(f32))
    info = jnp.pad(jnp.stack(cols, axis=1), ((0, 0), (0, 128 - len(cols))))
    return info, jnp.broadcast_to(seg[None, :], (8, rows))


def top(rows, array):
    return jnp.pad(array, ((0, rows - array.shape[0]), (0, 0)))


def by_member(parts, n_s):
    split = [p.reshape(p.shape[0], n_s, p.shape[1] // n_s) for p in parts]
    return jnp.swapaxes(jnp.concatenate(split, axis=2), 0, 1)


def whole_rows(piece, widths):
    out = []
    at = 0
    for w in widths:
        p = jnp.swapaxes(piece[:, :, at : at + w], 0, 1)
        out.append(p.reshape(p.shape[0], -1))
        at += w
    return out


def body(
    n_dp,
    n_s,
    tokens,
    cotangent,
    query_key,
    value_gate,
    output_weight,
    gate_up,
    down_weight,
    small_params,
    momentum_query_key,
    momentum_value_gate,
    momentum_output,
    momentum_gate_up,
    momentum_down,
    moment_one,
    moment_two,
    seq_lengths,
):
    member = lax.axis_index("shard")
    nh = H // n_s
    local = tokens.shape[0]
    rows = local * n_s
    ff = gate_up.shape[2] // n_s
    (w_decay, w_beta, conv_query, conv_keys, conv_value, gain_one, gain_two, gain_out, a_log, dt_bias) = unpack(
        small_params
    )

    def mine(array, axis, size):
        return lax.dynamic_slice_in_dim(array, member * size, size, axis)

    def put(array, axis, full):
        shape = list(array.shape)
        shape[axis] = full
        return lax.dynamic_update_slice_in_dim(
            jnp.zeros(shape, array.dtype), array, member * array.shape[axis], axis
        )

    info, segr = row_facts(seq_lengths[0], rows)
    w_small = jnp.concatenate([mine(w_decay, 1, nh), mine(w_beta, 1, nh)], axis=1)
    w_small = jnp.pad(w_small, ((0, 0), (0, 128 - 2 * nh))).astype(bf16)
    taps = jnp.concatenate(
        [mine(conv_query, 1, nh * DK), mine(conv_keys, 1, nh * DK), mine(conv_value, 1, nh * DV)], axis=1
    )
    taps = top(8, taps)
    vec = jnp.stack([jnp.exp(mine(a_log, 0, nh)), mine(dt_bias, 0, nh)])
    vec = top(8, jnp.pad(vec, ((0, 0), (0, 128 - nh))))
    gain_o = top(8, gain_out[None])
    gain_1 = top(8, gain_one[None])
    gain_2 = top(8, gain_two[None])

    x = tokens.astype(f32)
    normed_own = (x * lax.rsqrt(jnp.mean(x * x, axis=-1, keepdims=True) + NORM_EPS) * gain_one).astype(bf16)
    cast = [
        by_member([query_key[0].astype(bf16), query_key[1].astype(bf16), value_gate[0].astype(bf16), value_gate[1].astype(bf16)], n_s),
        by_member([gate_up[0].astype(bf16), gate_up[1].astype(bf16)], n_s),
        output_weight.astype(bf16),
        down_weight.astype(bf16),
    ]
    order = [(0, i, 1) for i in range(n_s)] + [(2, 0, 0)] + [(1, i, 1) for i in range(n_s)] + [(3, 0, 0)]
    w_in, w_gu, w_out, w_dn, normed, dy = gather(
        cast[:2], cast[2:], [normed_own, cotangent], n_dp, n_s, 0, tuple(order)
    )
    w_in = w_in.reshape(D, -1)
    w_gu = w_gu.reshape(D, -1)
    w_out = w_out.reshape(-1, D)
    w_dn = w_dn.reshape(-1, D)
    normed = normed.reshape(rows, D)
    dy = dy.reshape(rows, D)

    raw = mm(normed, w_in, 1, 0)
    raw_small = mm(normed, w_small, 1, 0)
    gated, mixed, updates, states, inverses = m1(raw, raw_small, taps, vec, gain_o, info, segr, PASSES)
    part = mm(gated, w_out, 1, 0, bf16).reshape(n_s, local, D)
    middle, normed_two = mid(part, tokens, gain_2, n_s, 1)
    normed_two = normed_two.reshape(rows, D)
    gu = mm(normed_two, w_gu, 1, 0)
    gate = gu[:, :ff]
    upper = gu[:, ff:]
    sig = jax.nn.sigmoid(gate)
    hidden = (gate * sig * upper).astype(bf16)
    y_part = mm(hidden, w_dn, 1, 0, bf16).reshape(n_s, local, D)
    d_hidden = mm(dy, w_dn, 1, 1)
    d_gate = (d_hidden * upper * sig * (1.0 + gate * (1.0 - sig))).astype(bf16)
    d_upper = (d_hidden * (gate * sig)).astype(bf16)
    d_gu = jnp.concatenate([d_gate, d_upper], axis=1)
    d_part = mm(d_gu, w_gu, 1, 1, bf16).reshape(n_s, local, D)
    part_dn = mm(hidden, dy, 0, 0, bf16)
    part_gu = mm(normed_two, d_gu, 0, 0, bf16)
    (g_gu, grad_dn, grad_out, g_gate, g_qkv, block_out, input_grad, part_small, g_taps, g_vec, g_gain, d_gain_one, d_gain_two) = back(
        part_gu.reshape(n_dp, -1, part_gu.shape[1]),
        part_dn.reshape(n_dp, -1, D),
        y_part,
        d_part,
        middle,
        cotangent,
        tokens,
        gain_2,
        gain_1,
        w_out,
        w_in,
        w_small,
        raw,
        raw_small,
        taps,
        vec,
        gain_o,
        info,
        segr,
        normed,
        gated,
        mixed,
        updates,
        states,
        inverses,
        n_dp,
        n_s,
        PASSES,
        2,
    )
    kq = nh * DK
    small_local = jnp.concatenate(
        [
            put(part_small[:, :nh], 1, H).reshape(-1),
            put(part_small[:, nh : 2 * nh], 1, H).reshape(-1),
            put(g_taps[:KCONV, :kq], 1, H * DK).reshape(-1),
            put(g_taps[:KCONV, kq : 2 * kq], 1, H * DK).reshape(-1),
            put(g_taps[:KCONV, 2 * kq :], 1, H * DV).reshape(-1),
            d_gain_one[0],
            d_gain_two[0],
            g_gain[0],
            put(g_vec[0, :nh], 0, H),
            put(g_vec[1, :nh], 0, H),
        ]
    )
    small_grad = lax.psum(small_local, ("dp", "shard"))

    grads = [p.astype(f32) for p in whole_rows(g_qkv, [kq, kq, nh * DV])]
    grads += [p.astype(f32) for p in whole_rows(g_gate, [nh * DV])]
    grads += [grad_out.astype(f32)]
    grads += [p.astype(f32) for p in whole_rows(g_gu, [ff, ff])]
    grads += [grad_dn.astype(f32)]
    masters = [query_key[0], query_key[1], value_gate[0], value_gate[1], output_weight, gate_up[0], gate_up[1], down_weight]
    momenta = [
        momentum_query_key[0],
        momentum_query_key[1],
        momentum_value_gate[0],
        momentum_value_gate[1],
        momentum_output,
        momentum_gate_up[0],
        momentum_gate_up[1],
        momentum_down,
    ]
    moms = [MOMENTUM * m + g for m, g in zip(momenta, grads)]
    looks = [(g + MOMENTUM * m).astype(bf16) for m, g in zip(moms, grads)]
    devices = n_dp * n_s
    pads = []
    for look in looks:
        r_count, c_count = look.shape
        tall = r_count * devices > c_count
        pads.append(top(-(-r_count // 16) * 16, look) if tall else look)
    orthos = muon(pads, n_dp, n_s, 5)
    steps = []
    for master, ortho in zip(masters, orthos):
        r_count, c_count = master.shape
        scale = 0.2 * math.sqrt(max(r_count * devices, c_count))
        steps.append(-MUON_RATE * (scale * ortho[:r_count].astype(f32) + MUON_DECAY * master))
    new_one = BETA_ONE * moment_one + (1.0 - BETA_ONE) * small_grad
    new_two = BETA_TWO * moment_two + (1.0 - BETA_TWO) * small_grad * small_grad
    small_step = (
        -ADAM_RATE
        * (new_one / (1.0 - BETA_ONE**STEP_COUNT))
        / (jnp.sqrt(new_two / (1.0 - BETA_TWO**STEP_COUNT)) + ADAM_EPS)
    )

    def bundle(a):
        return (jnp.stack(a[0:2]), jnp.stack(a[2:4]), a[4], jnp.stack(a[5:7]), a[7])

    return (
        (block_out, input_grad)
        + bundle(grads)
        + bundle(steps)
        + bundle(moms)
        + (small_grad, small_step, new_one, new_two)
    )


def solution(mesh):
    cols = P(None, ("dp", "shard"), None)
    rows = P(("dp", "shard"), None)
    weights = (cols, cols, rows, cols, rows)
    return jax.shard_map(
        functools.partial(body, mesh.shape["dp"], mesh.shape["shard"]),
        mesh=mesh,
        in_specs=(rows, rows) + weights + (P(),) + weights + (P(), P(), P("dp", None)),
        out_specs=(rows, rows) + weights * 3 + (P(),) * 4,
        check_vma=False,
    )
```

```python
import functools
import math

import jax
import jax.numpy as jnp
from jax import lax
from jax.experimental import pallas as pl
from jax.experimental.pallas import tpu as pltpu
from jax.sharding import PartitionSpec as P

DK=128; DV=256; KCONV=4; CH=128
f32=jnp.float32; bf16=jnp.bfloat16
HI=lax.Precision.HIGHEST
GATE_EPS=1e-5; UNIT_EPS=1e-6

def _split(a):
    h=a.astype(bf16)
    return h,(a-h.astype(f32)).astype(bf16)

def dot(a,b,ca,cb,passes=3):
    dn=(((ca,),(cb,)),((),()))
    if passes==6:
        return lax.dot_general(a,b,dn,precision=HI,preferred_element_type=f32)
    if passes==1:
        return lax.dot_general(a.astype(bf16),b.astype(bf16),dn,preferred_element_type=f32)
    ah,al=_split(a); bh,bl=_split(b)
    g=functools.partial(lax.dot_general,dimension_numbers=dn,preferred_element_type=f32)
    return g(ah,bh)+(g(ah,bl)+g(al,bh))

def softplus(x): return jnp.maximum(x,0.0)+jnp.log1p(jnp.exp(-jnp.abs(x)))
def sigmoid(x): return lax.logistic(x)

def iota2(n,ax): return lax.broadcasted_iota(jnp.int32,(n,n),ax)

def inverse(A,p):
    n=A[0].shape[0]
    ri=iota2(n,0); ci=iota2(n,1)
    eye=(ri==ci).astype(f32)
    same=lambda b:(ri//b)==(ci//b)
    pw=[jnp.where(same(16),a,0.0) for a in A]
    X=[eye-q for q in pw]
    for _ in range(3):
        pw=[dot(q,q,1,0,p) for q in pw]
        X=[x+dot(x,q,1,0,p) for x,q in zip(X,pw)]
    b=16
    while b<n:
        m=jnp.logical_and(same(2*b),jnp.logical_not(same(b)))
        off=[jnp.where(m,a,0.0) for a in A]
        t=[dot(o,x,1,0,p) for o,x in zip(off,X)]
        X=[x-dot(x,q,1,0,p) for x,q in zip(X,t)]
        b*=2
    return X

def conv_pre(u,taps,info):
    s=taps[3:4]*u
    for k in (1,2,3):
        s=s+taps[3-k:4-k]*(pltpu.roll(u,k,0)*info[:,k:k+1])
    return s

def l2(u):
    return lax.rsqrt(jnp.sum(u*u,axis=-1,keepdims=True)+UNIT_EPS)

def acts(raw,taps,info,nh):
    out=[]
    kq=nh*DK
    for h in range(nh):
        d={}
        for nm,off,w in (("q",h*DK,DK),("k",kq+h*DK,DK),("v",2*kq+h*DV,DV)):
            pre=conv_pre(raw[:,off:off+w],taps[:,off:off+w],info)
            act=pre*sigmoid(pre)
            d[nm+"pre"]=pre; d[nm]=act
        rq=l2(d["q"])*(DK**-0.5); rk=l2(d["k"])
        d["rq"]=rq; d["rk"]=rk
        d["qn"]=d["q"]*rq; d["kn"]=d["k"]*rk
        out.append(d)
    return out

def decays(small,vec,nh):
    z=small+vec[1:2]
    ld=-vec[0:1]*softplus(z)
    beta=sigmoid(small)
    return z,ld,beta

def chunk_terms(ld,segc,segr,R,nh):
    n=CH
    ri=iota2(n,0); ci=iota2(n,1)
    low=(ri>=ci)
    L=low.astype(f32)
    out=[]
    for c in range(R//n):
        sl=slice(c*n,(c+1)*n)
        ldc=ld[sl]
        cc=dot(L,ldc,1,0,6)
        cr=dot(ldc,L,0,1,6)
        sc=segc[sl]; sr=segr[:,sl]
        M=jnp.logical_and(low,sc==sr)
        prev=segc[c*n-1:c*n] if c else None
        last=segc[(c+1)*n-1:(c+1)*n]
        heads=[]
        for h in range(nh):
            col=cc[:,h:h+1]; row=cr[h:h+1,:]
            R_=jnp.where(M,jnp.exp(jnp.where(M,col-row,0.0)),0.0)
            end=cc[n-1:n,h:h+1]
            t=jnp.where(sc==last,jnp.exp(end-col),0.0)
            if c:
                e=jnp.where(sc==prev,jnp.exp(col),0.0)
                g=jnp.where(last==prev,jnp.exp(end),0.0)
            else:
                e=jnp.zeros_like(col); g=jnp.zeros_like(end)
            heads.append((R_,e,t,g))
        out.append(heads)
    return out

def mixer_fwd(raw_ref,small_ref,taps_ref,vec_ref,gain_ref,info_ref,segr_ref,gated_ref,o_ref,u_ref,s_ref,x_ref,nh,P):
    R=raw_ref.shape[0]; nc=R//CH; n=CH
    info=info_ref[...]; gain=gain_ref[0:1]
    segc=info[:,0:1]
    a=acts(raw_ref,taps_ref[...],info,nh)
    z,ld,beta=decays(small_ref[...],vec_ref[...],nh)
    yield
    terms=chunk_terms(ld,segc,segr_ref[0:1],R,nh)
    ri=iota2(n,0); ci=iota2(n,1)
    strict=ri>ci
    idx=[(h,c) for c in range(nc) for h in range(nh)]
    sl=lambda c:slice(c*n,(c+1)*n)
    A=[];Pm=[]
    for h,c in idx:
        K=a[h]["kn"][sl(c)]; Q=a[h]["qn"][sl(c)]
        R_=terms[c][h][0]
        b=beta[sl(c),nh+h:nh+h+1]
        A.append(jnp.where(strict,b*R_*dot(K,K,1,1,P["kk"]),0.0))
        Pm.append(dot(Q,K,1,1,P["qk"])*R_)
    yield
    X=inverse(A,P["inv"])
    for i in range(len(idx)): x_ref[i]=X[i]
    yield
    U0=[];W=[]
    for i,(h,c) in enumerate(idx):
        b=beta[sl(c),nh+h:nh+h+1]; e=terms[c][h][1]
        U0.append(dot(X[i],b*a[h]["v"][sl(c)],1,0,P["u"]))
        W.append(dot(X[i],(b*e)*a[h]["kn"][sl(c)],1,0,P["u"]) if c else None)
    yield
    S=[None]*nh
    off=2*nh*DK+nh*DV
    for i,(h,c) in enumerate(idx):
        R_,e,t,g=terms[c][h]
        K=a[h]["kn"][sl(c)]; Q=a[h]["qn"][sl(c)]
        S0=S[h]
        U=U0[i] if c==0 else U0[i]-dot(W[i],S0,1,0,P["s"])
        o=dot(Pm[i],U,1,0,P["o"])
        if c: o=o+dot(e*Q,S0,1,0,P["o"])
        up=dot(t*K,U,0,0,P["s"])
        S[h]=up if c==0 else g*S0+up
        co=slice(h*DV,(h+1)*DV)
        s_ref[i]=S0 if c else jnp.zeros((DK,DV),f32)
        u_ref[sl(c),co]=U; o_ref[sl(c),co]=o
        r=lax.rsqrt(jnp.mean(o*o,axis=-1,keepdims=True)+GATE_EPS)
        gt=raw_ref[sl(c),off+h*DV:off+(h+1)*DV]
        gated_ref[sl(c),co]=(o*r*gain*(gt*sigmoid(gt))).astype(bf16)
        if h==nh-1 and c==1: yield

def gate_back(raw_ref,gain,dgated_ref,o_ref,nh,emit):
    R=raw_ref.shape[0]; nc=R//CH; n=CH
    off=2*nh*DK+nh*DV
    dO={};ggain=None
    for c in range(nc):
        for h in range(nh):
            r_=slice(c*n,(c+1)*n); co=slice(h*DV,(h+1)*DV)
            o=o_ref[r_,co]
            r=lax.rsqrt(jnp.mean(o*o,axis=-1,keepdims=True)+GATE_EPS)
            gt=raw_ref[r_,off+h*DV:off+(h+1)*DV]
            s=sigmoid(gt); sg=gt*s
            dg=dgated_ref[r_,co]
            nrm=o*r
            emit(h,c,dg*nrm*gain*(s*(1.0+gt*(1.0-s))))
            dsn=dg*sg
            part=jnp.sum(dsn*nrm,axis=0,keepdims=True)
            ggain=part if ggain is None else ggain+part
            dn=dsn*gain
            dO[h,c]=r*dn-nrm*(r*jnp.mean(nrm*dn,axis=-1,keepdims=True))
    return dO,ggain

def mixer_bwd(raw_ref,small_ref,taps_ref,vec_ref,info_ref,segr_ref,dO,u_ref,s_ref,x_ref,nh,P,result):
    R=raw_ref.shape[0]; nc=R//CH; n=CH
    raw=raw_ref; taps=taps_ref[...]; vec=vec_ref[...]; info=info_ref[...]
    segc=info[:,0:1]
    a=acts(raw,taps,info,nh)
    z,ld,beta=decays(small_ref[...],vec,nh)
    yield
    terms=chunk_terms(ld,segc,segr_ref[0:1],R,nh)
    ri=iota2(n,0); ci=iota2(n,1)
    strict=ri>ci
    U_=(ri<=ci).astype(f32)
    idx=[(h,c) for c in reversed(range(nc)) for h in range(nh)]
    sl=lambda c:slice(c*n,(c+1)*n)
    yield
    dU0={};KK={};QK={}
    for h,c in idx:
        K=a[h]["kn"][sl(c)]; Q=a[h]["qn"][sl(c)]
        KK[h,c]=dot(K,K,1,1,P["kk"]); QK[h,c]=dot(Q,K,1,1,P["qk"])
        dU0[h,c]=dot(QK[h,c]*terms[c][h][0],dO[h,c],0,0,P["u"])
    yield
    dS=[None]*nh
    dS1s={};Ys={}
    for c in reversed(range(nc)):
        for h in range(nh):
            R_,e,t,g=terms[c][h]
            K=a[h]["kn"][sl(c)]; Q=a[h]["qn"][sl(c)]
            b=beta[sl(c),nh+h:nh+h+1]
            dS1=dS[h]
            dS1s[h,c]=dS1
            dU=dU0[h,c]
            if dS1 is not None: dU=dU+dot(t*K,dS1,1,0,P["s"])
            Y=dot(x_ref[c*nh+h],dU,0,0,P["s"])
            Ys[h,c]=Y
            if c:
                d0=dot(e*Q,dO[h,c],0,0,P["s"])-dot((b*e)*K,Y,0,0,P["s"])
                dS[h]=d0 if dS1 is None else g*dS1+d0
        yield
    dQ={};dK={};dV={};dbeta={};dld={}
    for h,c in idx:
        R_,e,t,g=terms[c][h]
        K=a[h]["kn"][sl(c)]; Q=a[h]["qn"][sl(c)]; V=a[h]["v"][sl(c)]
        b=beta[sl(c),nh+h:nh+h+1]
        Y=Ys[h,c]; U=u_ref[sl(c),h*DV:(h+1)*DV]; dS1=dS1s[h,c]
        dA=jnp.where(strict,-dot(Y,U,1,1,P["g"]),0.0)
        dP=dot(dO[h,c],U,1,1,P["g"])
        H=dP*R_
        Gr=dA*R_
        G=b*Gr
        dq=dot(H,K,1,0,P["g"])
        dk=dot(G,K,1,0,P["g"])+dot(G,K,0,0,P["g"])+dot(H,Q,0,0,P["g"])
        dV[h,c]=b*Y
        db=jnp.sum(Y*V,axis=-1,keepdims=True)+jnp.sum(Gr*KK[h,c],axis=-1,keepdims=True)
        Z=H*QK[h,c]+G*KK[h,c]
        dc=jnp.sum(Z,axis=-1,keepdims=True)-jnp.sum(Z.T,axis=-1,keepdims=True)
        last=(lax.broadcasted_iota(jnp.int32,(n,1),0)==n-1).astype(f32)
        if c:
            S0=s_ref[c*nh+h]
            YS=dot(Y,S0,1,1,P["g"]); OS=dot(dO[h,c],S0,1,1,P["g"])
            dq=dq+e*OS
            dk=dk-(b*e)*YS
            ks=jnp.sum(YS*K,axis=-1,keepdims=True)
            qs=jnp.sum(OS*Q,axis=-1,keepdims=True)
            db=db-e*ks
            dc=dc+e*(qs-b*ks)
        if dS1 is not None:
            US=dot(U,dS1,1,1,P["g"])
            dk=dk+t*US
            tt=t*jnp.sum(US*K,axis=-1,keepdims=True)
            dc=dc-tt
            tot=jnp.sum(tt,axis=0,keepdims=True)
            if c:
                tot=tot+g*jnp.sum(jnp.sum(dS1*S0,axis=-1,keepdims=True),axis=0,keepdims=True)
            dc=dc+last*tot
        dQ[h,c]=dq; dK[h,c]=dk; dbeta[h,c]=db
        dld[h,c]=dc
        if h==nh-1: yield
    lane=lax.broadcasted_iota(jnp.int32,(n,128),1)
    dsm=[]
    for c in range(nc):
        acc_d=jnp.zeros((n,128),f32); acc_b=jnp.zeros((n,128),f32)
        for h in range(nh):
            acc_d=acc_d+jnp.where(lane==h,dld[h,c],0.0)
            acc_b=acc_b+jnp.where(lane==nh+h,dbeta[h,c],0.0)
        acc_d=dot(U_,acc_d,1,0,6)
        dsm.append((acc_d,acc_b))
    dldf=jnp.concatenate([x[0] for x in dsm],axis=0)
    dbf=jnp.concatenate([x[1] for x in dsm],axis=0)
    dz=-dldf*vec[0:1]*sigmoid(z)
    dsmall=dz+dbf*beta*(1.0-beta)
    g_dt=jnp.sum(dz,axis=0,keepdims=True)
    g_al=jnp.sum(dldf*ld,axis=0,keepdims=True)
    result.append((dsmall,g_dt,g_al))
    for nm in ("q","k","v"):
        for h in range(nh):
            d=a[h]
            w=DV if nm=="v" else DK
            coff={"q":h*DK,"k":nh*DK+h*DK,"v":2*nh*DK+h*DV}[nm]
            dy=jnp.concatenate([{"q":dQ,"k":dK,"v":dV}[nm][h,c] for c in range(nc)],axis=0)
            if nm!="v":
                y=d[nm+"n"]
                if nm=="q": y=y*(DK**0.5)
                dy=d["r"+nm]*(dy-y*jnp.sum(y*dy,axis=-1,keepdims=True))
            pre=d[nm+"pre"]; s=sigmoid(pre)
            dp=dy*(s*(1.0+pre*(1.0-s)))
            u=raw[:,coff:coff+w]; tp=taps[:,coff:coff+w]
            du=tp[3:4]*dp
            tg=[None]*4
            tg[3]=jnp.sum(dp*u,axis=0,keepdims=True)
            for k in (1,2,3):
                su=pltpu.roll(dp,dp.shape[0]-k,0)*info[:,3+k:4+k]
                du=du+tp[3-k:4-k]*su
                tg[3-k]=jnp.sum(su*u,axis=0,keepdims=True)
            result.append((coff,w,du,tg))
        yield


f32=jnp.float32; bf16=jnp.bfloat16
MESH=pl.DeviceIdType.MESH
ANY=pl.BlockSpec(memory_space=pl.ANY)
VM=pl.BlockSpec(memory_space=pltpu.VMEM)

def place():
    d=lax.axis_index("dp"); s=lax.axis_index("shard")
    return d,s,d//2,d%2

def greet(peers):
    bar=pltpu.get_barrier_semaphore()
    for p in peers:
        pl.semaphore_signal(bar,inc=1,device_id=p,device_id_type=MESH)
    pl.semaphore_wait(bar,len(peers))

def remote(src,dst,ss,rs,dev):
    return pltpu.make_async_remote_copy(src_ref=src,dst_ref=dst,send_sem=ss,recv_sem=rs,device_id=dev,device_id_type=MESH)

NORM_EPS=1e-6
D_=pltpu.SemaphoreType.DMA
def ring(n_s):
    d,s,_,_=place()
    return [(d,(s+j)%n_s) for j in range(1,n_s)]

def push_parts(n_s,part,land,ss,rs):
    cs=[]
    for j,p in enumerate(ring(n_s)):
        c=remote(part.at[p[1]],land.at[j],ss.at[j],rs.at[j],p); c.start(); cs.append(c)
    return cs

def push_all(n_s,out,ss,rs):
    _,s,_,_=place()
    cs=[]
    for j,p in enumerate(ring(n_s)):
        c=remote(out.at[s],out.at[s],ss.at[j],rs.at[j],p); c.start(); cs.append(c)
    return cs

def add_up(n_s,part,land):
    _,s,_,_=place()
    t=part[s].astype(f32)
    for j in range(n_s-1): t=t+land[j].astype(f32)
    return t

def norm_back(u,g,dn):
    w=u.shape[-1]
    r=lax.rsqrt(jnp.mean(u*u,axis=-1,keepdims=True)+NORM_EPS)
    gd=g*dn
    du=r*gd-u*(r*r*r*(jnp.sum(u*gd,axis=-1,keepdims=True)/w))
    return du,jnp.sum(u*r*dn,axis=0,keepdims=True)


f32=jnp.float32; bf16=jnp.bfloat16
CA,CB,CC=3.4445,-4.775,2.0315
def dg(a,b,ca,cb): return lax.dot_general(a,b,(((ca,),(cb,)),((),())),preferred_element_type=f32)
TB=256
def ns_wide(x,y,g,p,cols,iters=2,tm=256,tn=512):
    r=g.shape[0]
    cs=slice(0,cols)
    def sq(i,a):
        v=x[pl.ds(i*TB,TB),cs].astype(f32)
        return a+jnp.sum(v*v,axis=0,keepdims=True)
    t=lax.fori_loop(0,r//TB,sq,jnp.zeros((1,cols),f32))
    inv=1.0/(jnp.sqrt(jnp.sum(t,axis=1,keepdims=True))+1e-7)
    def sc(i,_):
        x[pl.ds(i*TB,TB),cs]=(x[pl.ds(i*TB,TB),cs].astype(f32)*inv).astype(bf16)
        return 0
    lax.fori_loop(0,r//TB,sc,0)
    a,b=x,y
    for _ in range(iters):
        def gram(i,_):
            ri=pl.ds(pl.multiple_of(i*tm,tm),tm)
            g[ri,:]=dg(a[ri,cs],a[:,cs],1,1).astype(bf16)
            return 0
        lax.fori_loop(0,r//tm,gram,0)
        def poly(i,_):
            ri=pl.ds(pl.multiple_of(i*tm,tm),tm)
            p[ri,:]=(CB*g[ri,:].astype(f32)+CC*dg(g[ri,:],g[...],1,0)).astype(bf16)
            return 0
        lax.fori_loop(0,r//tm,poly,0)
        def nxt(i,_):
            ri=pl.ds(pl.multiple_of(i*tm,tm),tm)
            b[ri,cs]=(CA*a[ri,cs].astype(f32)+dg(p[ri,:],a[:,cs],1,0)).astype(bf16)
            return 0
        lax.fori_loop(0,r//tm,nxt,0)
        a,b=b,a
def ns_tall(x,y,g,p,n=None,iters=2,tm=256):
    n=n or x.shape[0]; r=x.shape[1]
    def sq(i,a):
        v=x[pl.ds(i*TB,TB),:].astype(f32)
        return a+jnp.sum(v*v,axis=0,keepdims=True)
    t=lax.fori_loop(0,n//TB,sq,jnp.zeros((1,r),f32))
    inv=1.0/(jnp.sqrt(jnp.sum(t,axis=1,keepdims=True))+1e-7)
    def sc(i,_):
        x[pl.ds(i*TB,TB),:]=(x[pl.ds(i*TB,TB),:].astype(f32)*inv).astype(bf16)
        return 0
    lax.fori_loop(0,n//TB,sc,0)
    a,b=x,y
    for _ in range(iters):
        for j in range(r//tm):
            cj=slice(j*tm,(j+1)*tm)
            g[cj,:]=dg(a[0:n,cj],a[0:n,:],0,0).astype(bf16)
        def poly(i,_):
            ri=pl.ds(pl.multiple_of(i*tm,tm),tm)
            p[ri,:]=(CB*g[ri,:].astype(f32)+CC*dg(g[ri,:],g[...],1,0)).astype(bf16)
            return 0
        lax.fori_loop(0,r//tm,poly,0)
        def nxt(i,_):
            ri=pl.ds(pl.multiple_of(i*tm,tm),tm)
            b[ri,:]=(CA*a[ri,:].astype(f32)+dg(a[ri,:],p[...],1,0)).astype(bf16)
            return 0
        lax.fori_loop(0,n//tm,nxt,0)
        a,b=b,a


def muon_owner(i,n_dp):
    base=n_dp//2-2
    d,s=((2,0),(3,0),(1,2),(3,2),(2,2),(0,0),(1,0),(0,2))[i]
    return base+d,s

def muon_kernel(n_dp,n_s,kinds,*refs):
    n=len(kinds)
    ins=refs[:n]; outs=refs[n:2*n]
    wide,wide2,tall,tall2,g,p,rin,sin,rout,sout,lsem=refs[2*n:]
    d,s,_,_=place()
    nd=n_dp*n_s
    me=d*n_s+s
    own=[muon_owner(i,n_dp) for i in range(n)]
    base=n_dp//2-2
    is_owner=lambda dd,ss: jnp.logical_and(jnp.logical_and(dd>=base,dd<base+4),ss%2==0)
    mine=is_owner(d,s)
    bar=pltpu.get_barrier_semaphore()
    for o in own:
        @pl.when(jnp.logical_or(d!=o[0],s!=o[1]))
        def _():
            pl.semaphore_signal(bar,inc=1,device_id=o,device_id_type=MESH)
    @pl.when(mine)
    def _():
        def greet_one(q,_):
            dd=q//n_s; ss=q%n_s
            @pl.when(jnp.logical_not(is_owner(dd,ss)))
            def _():
                pl.semaphore_signal(bar,inc=1,device_id=(dd,ss),device_id_type=MESH)
            return 0
        lax.fori_loop(0,nd,greet_one,0)
        pl.semaphore_wait(bar,nd-1)
    @pl.when(jnp.logical_not(mine))
    def _():
        pl.semaphore_wait(bar,n)
    def slot(buf,i,q):
        t,rows,cols=kinds[i]
        ds=pl.ds(pl.multiple_of(q*rows,rows),rows)
        return buf.at[ds] if t else buf.at[ds,pl.ds(0,cols)]
    for i in range(n):
        t,rows,cols=kinds[i]
        dst=slot(tall if t else wide,i,me)
        there=jnp.logical_and(d==own[i][0],s==own[i][1])
        @pl.when(there)
        def _():
            pltpu.make_async_copy(ins[i],dst,rin.at[0]).start()
        @pl.when(jnp.logical_not(there))
        def _():
            remote(ins[i],dst,sin.at[i],rin.at[0],own[i]).start()
    for i in range(n):
        t,rows,cols=kinds[i]
        there=jnp.logical_and(d==own[i][0],s==own[i][1])
        @pl.when(there)
        def _():
            buf=tall if t else wide
            full=buf.at[pl.ds(0,rows*nd)] if t else buf.at[:,pl.ds(0,cols)]
            pltpu.make_async_copy(full,full,rin.at[0]).wait()
            if t: ns_tall(tall,tall2,g,p,n=rows*nd)
            else: ns_wide(wide,wide2,g,p,cols,tm=512 if cols>1024 else 256)
            def send(q,_):
                src=slot(buf,i,q)
                @pl.when(q==me)
                def _():
                    pltpu.make_async_copy(src,outs[i],rout.at[i]).start()
                @pl.when(q!=me)
                def _():
                    remote(src,outs[i],sout.at[0],rout.at[i],(q//n_s,q%n_s)).start()
                return 0
            lax.fori_loop(0,nd,send,0)
            part=buf.at[pl.ds(0,rows*(nd-1))] if t else buf.at[pl.ds(0,rows*(nd-1)),pl.ds(0,cols)]
            pltpu.make_async_copy(part,part,sout.at[0]).wait()
    for i in range(n):
        there=jnp.logical_and(d==own[i][0],s==own[i][1])
        @pl.when(jnp.logical_not(there))
        def _():
            pltpu.make_async_copy(ins[i],ins[i],sin.at[i]).wait()
        pltpu.make_async_copy(ins[i],outs[i],rout.at[i]).wait()

def muon(looks,n_dp,n_s,cid):
    nd=n_dp*n_s
    kinds=[]
    for x in looks:
        r,c=x.shape
        kinds.append((r*nd>c,r,c))
    r=min(min(k[1]*nd,k[2]) for k in kinds)
    wc=max(k[2] for k in kinds if not k[0]); tr=max(k[1]*nd for k in kinds if k[0])
    V=pltpu.VMEM
    return pl.pallas_call(functools.partial(muon_kernel,n_dp,n_s,tuple(kinds)),
        out_shape=[jax.ShapeDtypeStruct(x.shape,bf16) for x in looks],in_specs=[VM]*8,out_specs=[VM]*8,
        scratch_shapes=[V((r,wc),bf16)]*2+[V((tr,r),bf16)]*2+[V((r,r),bf16)]*2+[D_((1,)),D_((8,)),D_((8,)),D_((1,)),D_((1,))],
        compiler_params=pltpu.CompilerParams(collective_id=cid,has_side_effects=True,vmem_limit_bytes=60<<20),name="muon")(*looks)


class Gatherer:
    def __init__(self,n_dp,n_s,ins,outs,ncol,sems,order):
        self.n_dp=n_dp; self.n_s=n_s; self.n_hi=n_dp//2; self.ins=ins; self.outs=outs; self.ncol=ncol; self.order=order
        self.s0,self.r0,self.s1,self.r1,self.lsem=sems
        d,s,hi,lo=place()
        self.d=d; self.s=s; self.hi=hi; self.lo=lo
        me=d*n_s+s
        self.td=me%n_dp; self.ts=me//n_dp
        self.fd=(s*n_dp+d)//n_s; self.fs=(s*n_dp+d)%n_s
        self.moved=jnp.logical_or(self.td!=d,self.ts!=s)
        self.zs=[((hi+j)%self.n_hi)*2+lo for j in range(1,self.n_hi)]
        self.xd=(hi*2+(1-lo),s)
        self.grp=ring(n_s)
        self.col={}; self.done=set(); self.i=0
    def greet(self):
        bar=pltpu.get_barrier_semaphore()
        peers=self.grp+[(z,self.s) for z in self.zs]+[self.xd]
        for p in peers: pl.semaphore_signal(bar,inc=1,device_id=p,device_id_type=MESH)
        @pl.when(self.moved)
        def _():
            pl.semaphore_signal(bar,inc=1,device_id=(self.td,self.ts),device_id_type=MESH)
            pl.semaphore_signal(bar,inc=1,device_id=(self.fd,self.fs),device_id_type=MESH)
            pl.semaphore_wait(bar,len(peers)+2)
        @pl.when(jnp.logical_not(self.moved))
        def _():
            pl.semaphore_wait(bar,len(peers))
    def phase0(self,k):
        src,dst=self.ins[k],self.outs[k]
        if k<self.ncol:
            c=pltpu.make_async_copy(src.at[self.s],dst.at[self.d,self.s],self.lsem.at[k]); c.start()
            self.col[k]=[c]
            for j,p in enumerate(self.grp):
                c=remote(src.at[p[1]],dst.at[self.d,self.s],self.s0.at[k,j],self.r0.at[k,j],p); c.start(); self.col[k].append(c)
        else:
            @pl.when(self.moved)
            def _():
                remote(src,dst.at[self.td],self.s0.at[k,0],self.r0.at[k,0],(self.td,self.ts)).start()
            @pl.when(jnp.logical_not(self.moved))
            def _():
                pltpu.make_async_copy(src,dst.at[self.d],self.r0.at[k,0]).start()
    def ready(self,k):
        if k in self.done: return
        self.done.add(k)
        if k<self.ncol:
            for c in self.col[k]: c.wait()
        else:
            src,dst=self.ins[k],self.outs[k]
            pltpu.make_async_copy(src,dst.at[self.d],self.r0.at[k,0]).wait()
            @pl.when(self.moved)
            def _():
                remote(src,dst.at[self.td],self.s0.at[k,0],self.r0.at[k,0],(self.td,self.ts)).wait_send()
    def blk(self,i,src):
        k,a,m=self.order[i]
        return self.outs[k].at[src,a:a+m] if m else self.outs[k].at[src]
    def go(self,i,j,b,dev):
        return remote(b,b,self.s1.at[i,j],self.r1.at[i,j],dev)
    def tick(self,times=1):
        n=len(self.order); nh=self.n_hi
        for _ in range(times):
            i=self.i; self.i+=1
            if i<n:
                self.ready(self.order[i][0])
                own=self.blk(i,self.d)
                for j,z in enumerate(self.zs): self.go(i,j,own,(z,self.s)).start()
                self.go(i,nh-1,own,self.xd).start()
            if 0<=i-1<n:
                for j in range(1,nh):
                    b=self.blk(i-1,((self.hi-j)%nh)*2+self.lo)
                    self.go(i-1,j-1,b,self.xd).wait()
                    self.go(i-1,nh-1+j,b,self.xd).start()
            if 0<=i-2<n:
                for j in range(nh):
                    self.go(i-2,nh-1+j,self.blk(i-2,((self.hi-j)%nh)*2+(1-self.lo)),self.xd).wait()
    def after(self,i):
        while self.i<i+3: self.tick()
    def drain(self):
        self.after(len(self.order)-1)

def dotb(a,b,ca,cb): return lax.dot_general(a,b,(((ca,),(cb,)),((),())),preferred_element_type=f32)

def fore_kernel(n_dp,n_s,nh,P,order,last_in,last_out,*refs):
    (c_in,c_gu,c_out,c_dn,nown,dyown,x_ref,gain2,w_sm,taps,vec,gain,info,segr,
     g_in,g_gu,g_out,g_dn,normed,dy,raw,small,gated,o_ref,u_ref,s_ref,xi_ref,middle,gath,
     part,land)=refs[:31]
    sems=refs[31:36]; ss,rs,ls=refs[36:39]
    E=Gatherer(n_dp,n_s,[c_in,c_gu,c_out,c_dn],[g_in,g_gu,g_out,g_dn],2,sems,order)
    s=E.s
    E.greet()
    normed[s]=nown[...]
    a=push_all(n_s,normed,ss.at[0],rs.at[0])
    for k in (0,2,1,3): E.phase0(k)
    E.tick(2)
    dy[s]=dyown[...]
    b=push_all(n_s,dy,ss.at[1],rs.at[1])
    for c in a: c.wait()
    local,D=x_ref.shape; rows=local*n_s
    nrm=normed[...].reshape(rows,D)
    small[...]=dotb(nrm,w_sm[...],1,0)
    E.after(last_in)
    raw[...]=dotb(nrm,g_in[...].reshape(D,raw.shape[1]),1,0)
    E.tick()
    for i,_ in enumerate(mixer_fwd(raw,small,taps,vec,gain,info,segr,gated,o_ref,u_ref,s_ref,xi_ref,nh,P)):
        if i%2==0: E.tick()
    E.after(last_out)
    part[...]=dotb(gated[...],g_out[...].reshape(nh*DV,D),1,0).astype(bf16).reshape(part.shape)
    c1=push_parts(n_s,part,land,ss.at[2],rs.at[2])
    E.tick()
    for c in c1: c.wait()
    m=x_ref[...].astype(f32)+add_up(n_s,part,land)
    middle[...]=m
    r=lax.rsqrt(jnp.mean(m*m,axis=-1,keepdims=True)+NORM_EPS)
    gath[s]=(m*r*gain2[0:1]).astype(bf16)
    c2=push_all(n_s,gath,ss.at[3],rs.at[3])
    E.drain()
    for c in c2: c.wait()
    for c in b: c.wait()

def fore(cols,rws,nown,dyown,x,gain2,w_sm,taps,vec,gain,info,segr,n_dp,n_s,P,cid):
    ins=list(cols)+list(rws)+[nown,dyown,x,gain2,w_sm,taps,vec,gain,info,segr]
    local,D=x.shape; rows=local*n_s; n_hi=n_dp//2
    nh=rws[0].shape[0]*n_dp//DV; wid=nh*(2*DK+2*DV); nb=nh*rows//CH
    order=tuple([(0,i,1) for i in range(n_s)]+[(2,0,0)]+[(1,i,1) for i in range(n_s)]+[(3,0,0)])
    S_=jax.ShapeDtypeStruct; V=pltpu.VMEM
    ps=list(cols)+list(rws)
    outs=[S_((n_dp,)+q.shape,bf16) for q in ps]+[S_((n_s,local,D),bf16)]*2+[S_((rows,wid),f32),S_((rows,128),f32),S_((rows,nh*DV),bf16),S_((rows,nh*DV),f32),S_((rows,nh*DV),f32),
          S_((nb,DK,DV),f32),S_((nb,CH,CH),f32),S_((local,D),f32),S_((n_s,local,D),bf16)]
    sc=[V((n_s,local,D),bf16),V((n_s-1,local,D),bf16)]
    sc+=[D_((4,n_s))]*2+[D_((len(order),2*n_hi))]*2+[D_((4,))]+[D_((4,n_s))]*2+[D_((2,))]
    return pl.pallas_call(functools.partial(fore_kernel,n_dp,n_s,nh,P,order,n_s-1,n_s),
        out_shape=outs,in_specs=[VM]*len(ins),out_specs=[VM]*len(outs),scratch_shapes=sc,
        compiler_params=pltpu.CompilerParams(collective_id=cid,has_side_effects=True,vmem_limit_bytes=63<<20),name="forward")(*ins)


class Reducer:
    def __init__(self,n_dp,n_s,pieces,sems,W):
        self.n_s=n_s; self.n_hi=n_dp//2; self.p=pieces; self.W=W
        self.sx,self.rx,self.sz,self.rz,self.sf,self.rf,self.lsem=sems
        d,s,hi,lo=place()
        self.s=s; self.hi=hi; self.lo=lo
        me=s*n_dp+d
        self.td=me//n_s; self.ts=me%n_s
        own=d*n_s+s
        self.fd=own%n_dp; self.fs=own//n_dp
        self.moved=jnp.logical_or(self.td!=d,self.ts!=s)
        self.xd=(hi*2+(1-lo),s)
        self.zd=lambda j:(((hi+j)%self.n_hi)*2+lo,s)
        self.grp=ring(n_s)
        self.q=[]; self.ns=0; self.nh=0; self.late=[]; self.fc={}
    def greet(self):
        bar=pltpu.get_barrier_semaphore()
        peers=self.grp+[self.zd(j) for j in range(1,self.n_hi)]+[self.xd]
        for p in peers: pl.semaphore_signal(bar,inc=1,device_id=p,device_id_type=MESH)
        @pl.when(self.moved)
        def _():
            pl.semaphore_signal(bar,inc=1,device_id=(self.td,self.ts),device_id_type=MESH)
            pl.semaphore_signal(bar,inc=1,device_id=(self.fd,self.fs),device_id_type=MESH)
            pl.semaphore_wait(bar,len(peers)+2)
        @pl.when(jnp.logical_not(self.moved))
        def _():
            pl.semaphore_wait(bar,len(peers))
    def xc(self,k,j):
        z=(self.hi+j)%self.n_hi; p=self.p[k]
        return remote(p["g"].at[z*2+1-self.lo],p["xl"].at[j],self.sx.at[k,j],self.rx.at[k,j],self.xd)
    def xw(self,k,j):
        return self.xc(k,j)
    def zc(self,k,j):
        p=self.p[k]
        return remote(p["zb"].at[j-1],p["zl"].at[j-1],self.sz.at[k,j],self.rz.at[k,j],self.zd(j))
    def add(self,k):
        self.q+=[(k,j) for j in list(range(1,self.n_hi))+[0]]
    def handle(self,k,j):
        p=self.p[k]; z=(self.hi+j)%self.n_hi
        self.xw(k,j).wait()
        t=p["g"][z*2+self.lo].astype(f32)+p["xl"][j].astype(f32)
        if j:
            p["zb"][j-1]=t.astype(bf16); self.zc(k,j).start()
        else:
            p["own"][...]=t
            self.late.append([k,2])
    def finish(self,k):
        p=self.p[k]; t=p["own"][...]
        for j in range(1,self.n_hi):
            self.zc(k,j).wait()
            t=t+p["zl"][j-1].astype(f32)
        t=t.astype(bf16)
        fin,out=p["fin"],p["out"]
        if p["col"]:
            rows=t.shape[0]//self.n_s
            fin[...]=t.reshape(self.n_s,rows,t.shape[1])
            c=pltpu.make_async_copy(fin.at[self.s],out.at[self.s],self.lsem.at[k]); c.start()
            self.fc[k]=[c]
            for j,q in enumerate(self.grp):
                c=remote(fin.at[q[1]],out.at[self.s],self.sf.at[k,j],self.rf.at[k,j],q); c.start(); self.fc[k].append(c)
        else:
            fin[...]=t
            @pl.when(self.moved)
            def _():
                remote(fin,out,self.sf.at[k,0],self.rf.at[k,0],(self.td,self.ts)).start()
            @pl.when(jnp.logical_not(self.moved))
            def _():
                pltpu.make_async_copy(fin,out,self.rf.at[k,0]).start()
    def tick(self,times=1):
        for _ in range(times):
            if self.ns<len(self.q):
                self.xc(*self.q[self.ns]).start(); self.ns+=1
                if self.ns-self.nh>self.W:
                    self.handle(*self.q[self.nh]); self.nh+=1
            elif self.nh<self.ns:
                self.handle(*self.q[self.nh]); self.nh+=1
            for e in list(self.late):
                e[1]-=1
                if e[1]<0:
                    self.late.remove(e); self.finish(e[0])
    def drain(self):
        while self.nh<len(self.q) or self.late: self.tick()
        for k,p in enumerate(self.p):
            if p["col"]:
                for c in self.fc[k]: c.wait()
            else:
                pltpu.make_async_copy(p["fin"],p["out"],self.rf.at[k,0]).wait()
                @pl.when(self.moved)
                def _():
                    remote(p["fin"],p["out"],self.sf.at[k,0],self.rf.at[k,0],(self.td,self.ts)).wait_send()

def dotb(a,b,ca,cb): return lax.dot_general(a,b,(((ca,),(cb,)),((),())),preferred_element_type=f32)

def back_kernel(n_dp,n_s,nh,P,W,*refs):
    (gu_ref,dn_ref,ypart,dpart,middle,dy,x_ref,gain2,gain1,w_out,w_in,w_sm,raw,small,taps,vec,gain,info,segr,normed,gated,o_ref,u_ref,s_ref,xi_ref,
     out_gu,out_dn,out_out,out_g,out_q,bout,igrad,psm,gtaps,gvec,ggain,dg1,dg2,
     yland,dland,eland,gath,dgt,draw,dsb,epart,dmid,
     p_out,p_g,p_q)=refs[:50]
    rest=refs[50:]
    xl=rest[0:5]; zb=rest[5:10]; zl=rest[10:15]; own=rest[15:20]; fin=rest[20:25]
    sems=rest[25:32]; ss,rs=rest[32:34]
    gs=(gu_ref,dn_ref,p_out,p_g,p_q); outs=(out_gu,out_dn,out_out,out_g,out_q)
    pieces=[dict(g=gs[k],xl=xl[k],zb=zb[k],zl=zl[k],own=own[k],fin=fin[k],out=outs[k],col=k in (0,3,4)) for k in range(5)]
    E=Reducer(n_dp,n_s,pieces,sems,W)
    s=E.s
    E.greet()
    b=push_parts(n_s,dpart,dland,ss.at[0],rs.at[0])
    E.add(0); E.add(1)
    E.tick(2)
    for c in b: c.wait()
    m=middle[...]
    du,dg=norm_back(m,gain2[0:1],add_up(n_s,dpart,dland))
    dm=dy[...].astype(f32)+du
    dmid[...]=dm
    dg2[...]=jnp.broadcast_to(dg,dg2.shape)
    gath[s]=dm.astype(bf16)
    g=push_all(n_s,gath,ss.at[1],rs.at[1])
    E.tick(1)
    for c in g: c.wait()
    a=push_parts(n_s,ypart,yland,ss.at[2],rs.at[2])
    rows=raw.shape[0]; D=gath.shape[2]
    dbr=gath[...].reshape(rows,D)
    dgt[...]=dotb(dbr,w_out[...],1,1)
    E.tick(1)
    p_out[...]=dotb(gated[...],dbr,0,0).astype(bf16).reshape(p_out.shape)
    E.add(2)
    n=CH; off=2*nh*DK+nh*DV
    def emit(h,c,v): draw[c*n:(c+1)*n,off+h*DV:off+(h+1)*DV]=v.astype(bf16)
    dO,gg=gate_back(raw,gain[0:1],dgt,o_ref,nh,emit)
    ggain[...]=jnp.broadcast_to(gg,ggain.shape)
    E.tick(1)
    p_g[...]=dotb(normed[...],draw[:,off:],0,0).astype(bf16).reshape(p_g.shape)
    E.add(3)
    res=[]
    for _ in mixer_bwd(raw,small,taps,vec,info,segr,dO,u_ref,s_ref,xi_ref,nh,P,res):
        E.tick(1)
    dsmall,g_dt,g_al=res[0]
    gtaps[...]=jnp.zeros_like(gtaps); gvec[...]=jnp.zeros_like(gvec)
    for coff,w,dcol,tg in res[1:]:
        draw[:,coff:coff+w]=dcol.astype(bf16)
        for i in range(4): gtaps[i:i+1,coff:coff+w]=tg[i]
    gvec[0:1]=g_al; gvec[1:2]=g_dt
    dsb[...]=dsmall.astype(bf16)
    p_q[...]=dotb(normed[...],draw[:,:off],0,0).astype(bf16).reshape(p_q.shape)
    E.add(4)
    E.tick(2)
    epart[...]=(dotb(draw[...],w_in[...],1,1)+dotb(dsb[...],w_sm[...],1,1)).astype(bf16).reshape(epart.shape)
    e=push_parts(n_s,epart,eland,ss.at[3],rs.at[3])
    for c in a: c.wait()
    bout[...]=(middle[...]+add_up(n_s,ypart,yland)).astype(bf16)
    psm[...]=dotb(normed[...],dsb[...],0,0)
    E.tick(2)
    for c in e: c.wait()
    du,dg=norm_back(x_ref[...].astype(f32),gain1[0:1],add_up(n_s,epart,eland))
    igrad[...]=(dmid[...]+du).astype(bf16)
    dg1[...]=jnp.broadcast_to(dg,dg1.shape)
    E.drain()

def back(part_gu,part_dn,ypart,dpart,middle,dy,x,gain2,gain1,w_out,w_in,w_sm,raw,small,taps,vec,gain,info,segr,normed,gated,O,U,S,X,n_dp,n_s,P,cid,W=2):
    ins=[part_gu,part_dn,ypart,dpart,middle,dy,x,gain2,gain1,w_out,w_in,w_sm,raw,small,taps,vec,gain,info,segr,normed,gated,O,U,S,X]
    local,D=x.shape; rows=local*n_s; nh=raw.shape[1]//(2*DK+2*DV); n_hi=n_dp//2
    off=2*nh*DK+nh*DV
    shp=[part_gu.shape,part_dn.shape,(n_dp,w_out.shape[0]//n_dp,D),(n_dp,D//n_dp,nh*DV),(n_dp,D//n_dp,off)]
    col=(0,3,4)
    osh=[(n_s,q[1]//n_s,q[2]) if k in col else q[1:] for k,q in enumerate(shp)]
    S_=jax.ShapeDtypeStruct; V=pltpu.VMEM
    outs=[S_(q,bf16) for q in osh]+[S_((local,D),bf16),S_((local,D),bf16),S_((D,128),f32),S_((8,off),f32),S_((8,128),f32),S_((8,DV),f32),S_((8,D),f32),S_((8,D),f32)]
    sc=[V((n_s-1,local,D),bf16)]*3+[V((n_s,local,D),bf16),V((rows,nh*DV),f32),V((rows,raw.shape[1]),bf16),V((rows,128),bf16),V((n_s,local,D),bf16),V((local,D),f32)]
    sc+=[V(shp[k],bf16) for k in (2,3,4)]
    sc+=[V((n_hi,)+q[1:],bf16) for q in shp]+[V((n_hi-1,)+q[1:],bf16) for q in shp]*2+[V(q[1:],f32) for q in shp]+[V(q,bf16) for q in osh]
    sc+=[D_((5,n_hi))]*4+[D_((5,n_s))]*2+[D_((5,))]+[D_((4,n_s))]*2
    return pl.pallas_call(functools.partial(back_kernel,n_dp,n_s,nh,P,W),
        out_shape=outs,in_specs=[VM]*len(ins),out_specs=[VM]*len(outs),scratch_shapes=sc,
        compiler_params=pltpu.CompilerParams(collective_id=cid,has_side_effects=True,vmem_limit_bytes=63<<20),name="backward")(*ins)


D = 1024
H = 8
STEP_COUNT = 10
MOMENTUM = 0.95
MUON_RATE = 0.1
MUON_DECAY = 0.01
ADAM_RATE = 0.05
BETA_ONE = 0.9
BETA_TWO = 0.95
ADAM_EPS = 1e-08
PASSES = dict(kk=3, qk=3, inv=3, u=3, s=3, o=3, g=3)


def unpack(packed):
    layouts = [(D, H), (D, H), (KCONV, H * DK), (KCONV, H * DK), (KCONV, H * DV), (D,), (D,), (DV,), (H,), (H,)]
    pieces = []
    offset = 0
    for layout in layouts:
        amount = math.prod(layout)
        pieces.append(packed[offset : offset + amount].reshape(layout))
        offset = offset + amount
    return pieces


def mm(a, b, ca, cb, kind=f32):
    return lax.dot_general(
        a, b, (((ca,), (cb,)), ((), ())), preferred_element_type=f32
    ).astype(kind)


def row_facts(lengths, rows):
    count = lengths.shape[0]
    ends = jnp.sum(jnp.where(jnp.arange(count)[:, None] >= jnp.arange(count)[None, :], lengths[None, :], 0), axis=1)
    pos = jnp.arange(rows, dtype=jnp.int32)

    def number(p):
        seg = jnp.sum((p[:, None] >= ends[None, :]).astype(jnp.int32), axis=1)
        return jnp.where(p < 0, -1, seg).astype(f32)

    seg = number(pos)
    cols = [seg]
    for k in (1, 2, 3):
        cols.append((number(pos - k) == seg).astype(f32))
    for k in (1, 2, 3):
        cols.append((number(pos + k) == seg).astype(f32))
    info = jnp.pad(jnp.stack(cols, axis=1), ((0, 0), (0, 128 - len(cols))))
    return info, jnp.broadcast_to(seg[None, :], (8, rows))


def top(rows, array):
    return jnp.pad(array, ((0, rows - array.shape[0]), (0, 0)))


def by_member(parts, n_s):
    split = [p.reshape(p.shape[0], n_s, p.shape[1] // n_s) for p in parts]
    return jnp.swapaxes(jnp.concatenate(split, axis=2), 0, 1)


def whole_rows(piece, widths):
    out = []
    at = 0
    for w in widths:
        p = jnp.swapaxes(piece[:, :, at : at + w], 0, 1)
        out.append(p.reshape(p.shape[0], -1))
        at += w
    return out


def body(
    n_dp,
    n_s,
    tokens,
    cotangent,
    query_key,
    value_gate,
    output_weight,
    gate_up,
    down_weight,
    small_params,
    momentum_query_key,
    momentum_value_gate,
    momentum_output,
    momentum_gate_up,
    momentum_down,
    moment_one,
    moment_two,
    seq_lengths,
):
    member = lax.axis_index("shard")
    nh = H // n_s
    local = tokens.shape[0]
    rows = local * n_s
    ff = gate_up.shape[2] // n_s
    (w_decay, w_beta, conv_query, conv_keys, conv_value, gain_one, gain_two, gain_out, a_log, dt_bias) = unpack(
        small_params
    )

    def mine(array, axis, size):
        return lax.dynamic_slice_in_dim(array, member * size, size, axis)

    def put(array, axis, full):
        shape = list(array.shape)
        shape[axis] = full
        return lax.dynamic_update_slice_in_dim(
            jnp.zeros(shape, array.dtype), array, member * array.shape[axis], axis
        )

    info, segr = row_facts(seq_lengths[0], rows)
    w_small = jnp.concatenate([mine(w_decay, 1, nh), mine(w_beta, 1, nh)], axis=1)
    w_small = jnp.pad(w_small, ((0, 0), (0, 128 - 2 * nh))).astype(bf16)
    taps = jnp.concatenate(
        [mine(conv_query, 1, nh * DK), mine(conv_keys, 1, nh * DK), mine(conv_value, 1, nh * DV)], axis=1
    )
    taps = top(8, taps)
    vec = jnp.stack([jnp.exp(mine(a_log, 0, nh)), mine(dt_bias, 0, nh)])
    vec = top(8, jnp.pad(vec, ((0, 0), (0, 128 - nh))))
    gain_o = top(8, gain_out[None])
    gain_1 = top(8, gain_one[None])
    gain_2 = top(8, gain_two[None])

    x = tokens.astype(f32)
    normed_own = (x * lax.rsqrt(jnp.mean(x * x, axis=-1, keepdims=True) + NORM_EPS) * gain_one).astype(bf16)
    cast = [
        by_member([query_key[0].astype(bf16), query_key[1].astype(bf16), value_gate[0].astype(bf16), value_gate[1].astype(bf16)], n_s),
        by_member([gate_up[0].astype(bf16), gate_up[1].astype(bf16)], n_s),
        output_weight.astype(bf16),
        down_weight.astype(bf16),
    ]
    (w_in, w_gu, w_out, w_dn, normed, dy, raw, raw_small, gated, mixed, updates, states, inverses, middle, normed_two) = fore(
        cast[:2], cast[2:], normed_own, cotangent, tokens, gain_2, w_small, taps, vec, gain_o, info, segr, n_dp, n_s, PASSES, 0
    )
    w_in = w_in.reshape(D, -1)
    w_gu = w_gu.reshape(D, -1)
    w_out = w_out.reshape(-1, D)
    w_dn = w_dn.reshape(-1, D)
    normed = normed.reshape(rows, D)
    dy = dy.reshape(rows, D)
    normed_two = normed_two.reshape(rows, D)
    gu = mm(normed_two, w_gu, 1, 0)
    gate = gu[:, :ff]
    upper = gu[:, ff:]
    sig = jax.nn.sigmoid(gate)
    hidden = (gate * sig * upper).astype(bf16)
    y_part = mm(hidden, w_dn, 1, 0, bf16).reshape(n_s, local, D)
    d_hidden = mm(dy, w_dn, 1, 1)
    d_gate = (d_hidden * upper * sig * (1.0 + gate * (1.0 - sig))).astype(bf16)
    d_upper = (d_hidden * (gate * sig)).astype(bf16)
    d_gu = jnp.concatenate([d_gate, d_upper], axis=1)
    d_part = mm(d_gu, w_gu, 1, 1, bf16).reshape(n_s, local, D)
    part_dn = mm(hidden, dy, 0, 0, bf16)
    part_gu = mm(normed_two, d_gu, 0, 0, bf16)
    (g_gu, grad_dn, grad_out, g_gate, g_qkv, block_out, input_grad, part_small, g_taps, g_vec, g_gain, d_gain_one, d_gain_two) = back(
        part_gu.reshape(n_dp, -1, part_gu.shape[1]),
        part_dn.reshape(n_dp, -1, D),
        y_part,
        d_part,
        middle,
        cotangent,
        tokens,
        gain_2,
        gain_1,
        w_out,
        w_in,
        w_small,
        raw,
        raw_small,
        taps,
        vec,
        gain_o,
        info,
        segr,
        normed,
        gated,
        mixed,
        updates,
        states,
        inverses,
        n_dp,
        n_s,
        PASSES,
        2,
    )
    kq = nh * DK
    small_local = jnp.concatenate(
        [
            put(part_small[:, :nh], 1, H).reshape(-1),
            put(part_small[:, nh : 2 * nh], 1, H).reshape(-1),
            put(g_taps[:KCONV, :kq], 1, H * DK).reshape(-1),
            put(g_taps[:KCONV, kq : 2 * kq], 1, H * DK).reshape(-1),
            put(g_taps[:KCONV, 2 * kq :], 1, H * DV).reshape(-1),
            d_gain_one[0],
            d_gain_two[0],
            g_gain[0],
            put(g_vec[0, :nh], 0, H),
            put(g_vec[1, :nh], 0, H),
        ]
    )
    small_grad = lax.psum(small_local, ("dp", "shard"))

    grads = [p.astype(f32) for p in whole_rows(g_qkv, [kq, kq, nh * DV])]
    grads += [p.astype(f32) for p in whole_rows(g_gate, [nh * DV])]
    grads += [grad_out.astype(f32)]
    grads += [p.astype(f32) for p in whole_rows(g_gu, [ff, ff])]
    grads += [grad_dn.astype(f32)]
    masters = [query_key[0], query_key[1], value_gate[0], value_gate[1], output_weight, gate_up[0], gate_up[1], down_weight]
    momenta = [
        momentum_query_key[0],
        momentum_query_key[1],
        momentum_value_gate[0],
        momentum_value_gate[1],
        momentum_output,
        momentum_gate_up[0],
        momentum_gate_up[1],
        momentum_down,
    ]
    moms = [MOMENTUM * m + g for m, g in zip(momenta, grads)]
    looks = [(g + MOMENTUM * m).astype(bf16) for m, g in zip(moms, grads)]
    devices = n_dp * n_s
    pads = []
    for look in looks:
        r_count, c_count = look.shape
        tall = r_count * devices > c_count
        pads.append(top(-(-r_count // 16) * 16, look) if tall else look)
    orthos = muon(pads, n_dp, n_s, 5)
    steps = []
    for master, ortho in zip(masters, orthos):
        r_count, c_count = master.shape
        scale = 0.2 * math.sqrt(max(r_count * devices, c_count))
        steps.append(-MUON_RATE * (scale * ortho[:r_count].astype(f32) + MUON_DECAY * master))
    new_one = BETA_ONE * moment_one + (1.0 - BETA_ONE) * small_grad
    new_two = BETA_TWO * moment_two + (1.0 - BETA_TWO) * small_grad * small_grad
    small_step = (
        -ADAM_RATE
        * (new_one / (1.0 - BETA_ONE**STEP_COUNT))
        / (jnp.sqrt(new_two / (1.0 - BETA_TWO**STEP_COUNT)) + ADAM_EPS)
    )

    def bundle(a):
        return (jnp.stack(a[0:2]), jnp.stack(a[2:4]), a[4], jnp.stack(a[5:7]), a[7])

    return (
        (block_out, input_grad)
        + bundle(grads)
        + bundle(steps)
        + bundle(moms)
        + (small_grad, small_step, new_one, new_two)
    )


def solution(mesh):
    cols = P(None, ("dp", "shard"), None)
    rows = P(("dp", "shard"), None)
    weights = (cols, cols, rows, cols, rows)
    return jax.shard_map(
        functools.partial(body, mesh.shape["dp"], mesh.shape["shard"]),
        mesh=mesh,
        in_specs=(rows, rows) + weights + (P(),) + weights + (P(), P(), P("dp", None)),
        out_specs=(rows, rows) + weights * 3 + (P(),) * 4,
        check_vma=False,
    )
```

```python
import functools
import math

import jax
import jax.numpy as jnp
from jax import lax
from jax.experimental import pallas as pl
from jax.experimental.pallas import tpu as pltpu
from jax.sharding import PartitionSpec as P

DK=128; DV=256; KCONV=4; CH=128
f32=jnp.float32; bf16=jnp.bfloat16
HI=lax.Precision.HIGHEST
GATE_EPS=1e-5; UNIT_EPS=1e-6

def _split(a):
    h=a.astype(bf16)
    return h,(a-h.astype(f32)).astype(bf16)

def dot(a,b,ca,cb,passes=3):
    dn=(((ca,),(cb,)),((),()))
    if passes==6:
        return lax.dot_general(a,b,dn,precision=HI,preferred_element_type=f32)
    if passes==1:
        return lax.dot_general(a.astype(bf16),b.astype(bf16),dn,preferred_element_type=f32)
    ah,al=_split(a); bh,bl=_split(b)
    g=functools.partial(lax.dot_general,dimension_numbers=dn,preferred_element_type=f32)
    return g(ah,bh)+(g(ah,bl)+g(al,bh))

def softplus(x): return jnp.maximum(x,0.0)+jnp.log1p(jnp.exp(-jnp.abs(x)))
def sigmoid(x): return lax.logistic(x)

def iota2(n,ax): return lax.broadcasted_iota(jnp.int32,(n,n),ax)

def inverse(A,p):
    n=A[0].shape[0]
    ri=iota2(n,0); ci=iota2(n,1)
    eye=(ri==ci).astype(f32)
    same=lambda b:(ri//b)==(ci//b)
    pw=[jnp.where(same(16),a,0.0) for a in A]
    X=[eye-q for q in pw]
    for _ in range(3):
        pw=[dot(q,q,1,0,p) for q in pw]
        X=[x+dot(x,q,1,0,p) for x,q in zip(X,pw)]
    b=16
    while b<n:
        m=jnp.logical_and(same(2*b),jnp.logical_not(same(b)))
        off=[jnp.where(m,a,0.0) for a in A]
        t=[dot(o,x,1,0,p) for o,x in zip(off,X)]
        X=[x-dot(x,q,1,0,p) for x,q in zip(X,t)]
        b*=2
    return X

def conv_pre(u,taps,info):
    s=taps[3:4]*u
    for k in (1,2,3):
        s=s+taps[3-k:4-k]*(pltpu.roll(u,k,0)*info[:,k:k+1])
    return s

def l2(u):
    return lax.rsqrt(jnp.sum(u*u,axis=-1,keepdims=True)+UNIT_EPS)

def acts(raw,taps,info,nh):
    out=[]
    kq=nh*DK
    for h in range(nh):
        d={}
        for nm,off,w in (("q",h*DK,DK),("k",kq+h*DK,DK),("v",2*kq+h*DV,DV)):
            pre=conv_pre(raw[:,off:off+w],taps[:,off:off+w],info)
            act=pre*sigmoid(pre)
            d[nm+"pre"]=pre; d[nm]=act
        rq=l2(d["q"])*(DK**-0.5); rk=l2(d["k"])
        d["rq"]=rq; d["rk"]=rk
        d["qn"]=d["q"]*rq; d["kn"]=d["k"]*rk
        out.append(d)
    return out

def decays(small,vec,nh):
    z=small+vec[1:2]
    ld=-vec[0:1]*softplus(z)
    beta=sigmoid(small)
    return z,ld,beta

def chunk_terms(ld,segc,segr,R,nh):
    n=CH
    ri=iota2(n,0); ci=iota2(n,1)
    low=(ri>=ci)
    L=low.astype(f32)
    out=[]
    for c in range(R//n):
        sl=slice(c*n,(c+1)*n)
        ldc=ld[sl]
        cc=dot(L,ldc,1,0,6)
        cr=dot(ldc,L,0,1,6)
        sc=segc[sl]; sr=segr[:,sl]
        M=jnp.logical_and(low,sc==sr)
        prev=segc[c*n-1:c*n] if c else None
        last=segc[(c+1)*n-1:(c+1)*n]
        heads=[]
        for h in range(nh):
            col=cc[:,h:h+1]; row=cr[h:h+1,:]
            R_=jnp.where(M,jnp.exp(jnp.where(M,col-row,0.0)),0.0)
            end=cc[n-1:n,h:h+1]
            t=jnp.where(sc==last,jnp.exp(end-col),0.0)
            if c:
                e=jnp.where(sc==prev,jnp.exp(col),0.0)
                g=jnp.where(last==prev,jnp.exp(end),0.0)
            else:
                e=jnp.zeros_like(col); g=jnp.zeros_like(end)
            heads.append((R_,e,t,g))
        out.append(heads)
    return out

def mixer_fwd(raw_ref,small_ref,taps_ref,vec_ref,gain_ref,info_ref,segr_ref,gated_ref,o_ref,u_ref,s_ref,x_ref,nh,P):
    R=raw_ref.shape[0]; nc=R//CH; n=CH
    info=info_ref[...]; gain=gain_ref[0:1]
    segc=info[:,0:1]
    a=acts(raw_ref,taps_ref[...],info,nh)
    z,ld,beta=decays(small_ref[...],vec_ref[...],nh)
    yield
    terms=chunk_terms(ld,segc,segr_ref[0:1],R,nh)
    ri=iota2(n,0); ci=iota2(n,1)
    strict=ri>ci
    idx=[(h,c) for c in range(nc) for h in range(nh)]
    sl=lambda c:slice(c*n,(c+1)*n)
    A=[];Pm=[]
    for h,c in idx:
        K=a[h]["kn"][sl(c)]; Q=a[h]["qn"][sl(c)]
        R_=terms[c][h][0]
        b=beta[sl(c),nh+h:nh+h+1]
        A.append(jnp.where(strict,b*R_*dot(K,K,1,1,P["kk"]),0.0))
        Pm.append(dot(Q,K,1,1,P["qk"])*R_)
    yield
    X=inverse(A,P["inv"])
    for i in range(len(idx)): x_ref[i]=X[i]
    yield
    U0=[];W=[]
    for i,(h,c) in enumerate(idx):
        b=beta[sl(c),nh+h:nh+h+1]; e=terms[c][h][1]
        U0.append(dot(X[i],b*a[h]["v"][sl(c)],1,0,P["u"]))
        W.append(dot(X[i],(b*e)*a[h]["kn"][sl(c)],1,0,P["u"]) if c else None)
    yield
    S=[None]*nh
    off=2*nh*DK+nh*DV
    for i,(h,c) in enumerate(idx):
        R_,e,t,g=terms[c][h]
        K=a[h]["kn"][sl(c)]; Q=a[h]["qn"][sl(c)]
        S0=S[h]
        U=U0[i] if c==0 else U0[i]-dot(W[i],S0,1,0,P["s"])
        o=dot(Pm[i],U,1,0,P["o"])
        if c: o=o+dot(e*Q,S0,1,0,P["o"])
        up=dot(t*K,U,0,0,P["s"])
        S[h]=up if c==0 else g*S0+up
        co=slice(h*DV,(h+1)*DV)
        s_ref[i]=S0 if c else jnp.zeros((DK,DV),f32)
        u_ref[sl(c),co]=U; o_ref[sl(c),co]=o
        r=lax.rsqrt(jnp.mean(o*o,axis=-1,keepdims=True)+GATE_EPS)
        gt=raw_ref[sl(c),off+h*DV:off+(h+1)*DV]
        gated_ref[sl(c),co]=(o*r*gain*(gt*sigmoid(gt))).astype(bf16)
        if h==nh-1 and c==1: yield

def gate_back(raw_ref,gain,dgated_ref,o_ref,nh,emit):
    R=raw_ref.shape[0]; nc=R//CH; n=CH
    off=2*nh*DK+nh*DV
    dO={};ggain=None
    for c in range(nc):
        for h in range(nh):
            r_=slice(c*n,(c+1)*n); co=slice(h*DV,(h+1)*DV)
            o=o_ref[r_,co]
            r=lax.rsqrt(jnp.mean(o*o,axis=-1,keepdims=True)+GATE_EPS)
            gt=raw_ref[r_,off+h*DV:off+(h+1)*DV]
            s=sigmoid(gt); sg=gt*s
            dg=dgated_ref[r_,co]
            nrm=o*r
            emit(h,c,dg*nrm*gain*(s*(1.0+gt*(1.0-s))))
            dsn=dg*sg
            part=jnp.sum(dsn*nrm,axis=0,keepdims=True)
            ggain=part if ggain is None else ggain+part
            dn=dsn*gain
            dO[h,c]=r*dn-nrm*(r*jnp.mean(nrm*dn,axis=-1,keepdims=True))
    return dO,ggain

def mixer_bwd(raw_ref,small_ref,taps_ref,vec_ref,info_ref,segr_ref,dO,u_ref,s_ref,x_ref,nh,P,result):
    R=raw_ref.shape[0]; nc=R//CH; n=CH
    raw=raw_ref; taps=taps_ref[...]; vec=vec_ref[...]; info=info_ref[...]
    segc=info[:,0:1]
    a=acts(raw,taps,info,nh)
    z,ld,beta=decays(small_ref[...],vec,nh)
    yield
    terms=chunk_terms(ld,segc,segr_ref[0:1],R,nh)
    ri=iota2(n,0); ci=iota2(n,1)
    strict=ri>ci
    U_=(ri<=ci).astype(f32)
    idx=[(h,c) for c in reversed(range(nc)) for h in range(nh)]
    sl=lambda c:slice(c*n,(c+1)*n)
    yield
    dU0={};KK={};QK={}
    for h,c in idx:
        K=a[h]["kn"][sl(c)]; Q=a[h]["qn"][sl(c)]
        KK[h,c]=dot(K,K,1,1,P["kk"]); QK[h,c]=dot(Q,K,1,1,P["qk"])
        dU0[h,c]=dot(QK[h,c]*terms[c][h][0],dO[h,c],0,0,P["u"])
    yield
    dS=[None]*nh
    dS1s={};Ys={}
    for c in reversed(range(nc)):
        for h in range(nh):
            R_,e,t,g=terms[c][h]
            K=a[h]["kn"][sl(c)]; Q=a[h]["qn"][sl(c)]
            b=beta[sl(c),nh+h:nh+h+1]
            dS1=dS[h]
            dS1s[h,c]=dS1
            dU=dU0[h,c]
            if dS1 is not None: dU=dU+dot(t*K,dS1,1,0,P["s"])
            Y=dot(x_ref[c*nh+h],dU,0,0,P["s"])
            Ys[h,c]=Y
            if c:
                d0=dot(e*Q,dO[h,c],0,0,P["s"])-dot((b*e)*K,Y,0,0,P["s"])
                dS[h]=d0 if dS1 is None else g*dS1+d0
        yield
    dQ={};dK={};dV={};dbeta={};dld={}
    for h,c in idx:
        R_,e,t,g=terms[c][h]
        K=a[h]["kn"][sl(c)]; Q=a[h]["qn"][sl(c)]; V=a[h]["v"][sl(c)]
        b=beta[sl(c),nh+h:nh+h+1]
        Y=Ys[h,c]; U=u_ref[sl(c),h*DV:(h+1)*DV]; dS1=dS1s[h,c]
        dA=jnp.where(strict,-dot(Y,U,1,1,P["g"]),0.0)
        dP=dot(dO[h,c],U,1,1,P["g"])
        H=dP*R_
        Gr=dA*R_
        G=b*Gr
        dq=dot(H,K,1,0,P["g"])
        dk=dot(G,K,1,0,P["g"])+dot(G,K,0,0,P["g"])+dot(H,Q,0,0,P["g"])
        dV[h,c]=b*Y
        db=jnp.sum(Y*V,axis=-1,keepdims=True)+jnp.sum(Gr*KK[h,c],axis=-1,keepdims=True)
        Z=H*QK[h,c]+G*KK[h,c]
        dc=jnp.sum(Z,axis=-1,keepdims=True)-jnp.sum(Z.T,axis=-1,keepdims=True)
        last=(lax.broadcasted_iota(jnp.int32,(n,1),0)==n-1).astype(f32)
        if c:
            S0=s_ref[c*nh+h]
            YS=dot(Y,S0,1,1,P["g"]); OS=dot(dO[h,c],S0,1,1,P["g"])
            dq=dq+e*OS
            dk=dk-(b*e)*YS
            ks=jnp.sum(YS*K,axis=-1,keepdims=True)
            qs=jnp.sum(OS*Q,axis=-1,keepdims=True)
            db=db-e*ks
            dc=dc+e*(qs-b*ks)
        if dS1 is not None:
            US=dot(U,dS1,1,1,P["g"])
            dk=dk+t*US
            tt=t*jnp.sum(US*K,axis=-1,keepdims=True)
            dc=dc-tt
            tot=jnp.sum(tt,axis=0,keepdims=True)
            if c:
                tot=tot+g*jnp.sum(jnp.sum(dS1*S0,axis=-1,keepdims=True),axis=0,keepdims=True)
            dc=dc+last*tot
        dQ[h,c]=dq; dK[h,c]=dk; dbeta[h,c]=db
        dld[h,c]=dc
        if h==nh-1: yield
    lane=lax.broadcasted_iota(jnp.int32,(n,128),1)
    dsm=[]
    for c in range(nc):
        acc_d=jnp.zeros((n,128),f32); acc_b=jnp.zeros((n,128),f32)
        for h in range(nh):
            acc_d=acc_d+jnp.where(lane==h,dld[h,c],0.0)
            acc_b=acc_b+jnp.where(lane==nh+h,dbeta[h,c],0.0)
        acc_d=dot(U_,acc_d,1,0,6)
        dsm.append((acc_d,acc_b))
    dldf=jnp.concatenate([x[0] for x in dsm],axis=0)
    dbf=jnp.concatenate([x[1] for x in dsm],axis=0)
    dz=-dldf*vec[0:1]*sigmoid(z)
    dsmall=dz+dbf*beta*(1.0-beta)
    g_dt=jnp.sum(dz,axis=0,keepdims=True)
    g_al=jnp.sum(dldf*ld,axis=0,keepdims=True)
    result.append((dsmall,g_dt,g_al))
    for nm in ("q","k","v"):
        for h in range(nh):
            d=a[h]
            w=DV if nm=="v" else DK
            coff={"q":h*DK,"k":nh*DK+h*DK,"v":2*nh*DK+h*DV}[nm]
            dy=jnp.concatenate([{"q":dQ,"k":dK,"v":dV}[nm][h,c] for c in range(nc)],axis=0)
            if nm!="v":
                y=d[nm+"n"]
                if nm=="q": y=y*(DK**0.5)
                dy=d["r"+nm]*(dy-y*jnp.sum(y*dy,axis=-1,keepdims=True))
            pre=d[nm+"pre"]; s=sigmoid(pre)
            dp=dy*(s*(1.0+pre*(1.0-s)))
            u=raw[:,coff:coff+w]; tp=taps[:,coff:coff+w]
            du=tp[3:4]*dp
            tg=[None]*4
            tg[3]=jnp.sum(dp*u,axis=0,keepdims=True)
            for k in (1,2,3):
                su=pltpu.roll(dp,dp.shape[0]-k,0)*info[:,3+k:4+k]
                du=du+tp[3-k:4-k]*su
                tg[3-k]=jnp.sum(su*u,axis=0,keepdims=True)
            result.append((coff,w,du,tg))
        yield


f32=jnp.float32; bf16=jnp.bfloat16
MESH=pl.DeviceIdType.MESH
ANY=pl.BlockSpec(memory_space=pl.ANY)
VM=pl.BlockSpec(memory_space=pltpu.VMEM)

def place():
    d=lax.axis_index("dp"); s=lax.axis_index("shard")
    return d,s,d//2,d%2

def greet(peers):
    bar=pltpu.get_barrier_semaphore()
    for p in peers:
        pl.semaphore_signal(bar,inc=1,device_id=p,device_id_type=MESH)
    pl.semaphore_wait(bar,len(peers))

def greet_all(n_dp,n_s):
    d,s,_,_=place()
    me=d*n_s+s
    bar=pltpu.get_barrier_semaphore()
    def one(q,_):
        @pl.when(q!=me)
        def _():
            pl.semaphore_signal(bar,inc=1,device_id=(q//n_s,q%n_s),device_id_type=MESH)
        return 0
    lax.fori_loop(0,n_dp*n_s,one,0)
    pl.semaphore_wait(bar,n_dp*n_s-1)

def remote(src,dst,ss,rs,dev):
    return pltpu.make_async_remote_copy(src_ref=src,dst_ref=dst,send_sem=ss,recv_sem=rs,device_id=dev,device_id_type=MESH)

NORM_EPS=1e-6
D_=pltpu.SemaphoreType.DMA
def ring(n_s):
    d,s,_,_=place()
    return [(d,(s+j)%n_s) for j in range(1,n_s)]

def push_parts(n_s,part,land,ss,rs):
    cs=[]
    for j,p in enumerate(ring(n_s)):
        c=remote(part.at[p[1]],land.at[j],ss.at[j],rs.at[j],p); c.start(); cs.append(c)
    return cs

def push_all(n_s,out,ss,rs):
    _,s,_,_=place()
    cs=[]
    for j,p in enumerate(ring(n_s)):
        c=remote(out.at[s],out.at[s],ss.at[j],rs.at[j],p); c.start(); cs.append(c)
    return cs

def add_up(n_s,part,land):
    _,s,_,_=place()
    t=part[s].astype(f32)
    for j in range(n_s-1): t=t+land[j].astype(f32)
    return t

def norm_back(u,g,dn):
    w=u.shape[-1]
    r=lax.rsqrt(jnp.mean(u*u,axis=-1,keepdims=True)+NORM_EPS)
    gd=g*dn
    du=r*gd-u*(r*r*r*(jnp.sum(u*gd,axis=-1,keepdims=True)/w))
    return du,jnp.sum(u*r*dn,axis=0,keepdims=True)


D = 1024
H = 8
ROW_CQ = 2 * D * H // 128
ROW_CK = ROW_CQ + KCONV * H * DK // 128
ROW_CV = ROW_CK + KCONV * H * DK // 128
ROW_G1 = ROW_CV + KCONV * H * DV // 128
ROW_G2 = ROW_G1 + D // 128
ROW_GO = ROW_G2 + D // 128
ROW_AL = ROW_GO + DV // 128
SMALL_ROWS = 288
SLICE = 16

def wide_row(ref,first,width):
    return jnp.concatenate([ref[first+i:first+i+1,:] for i in range(width//128)],axis=1)

def tap_rows(s,nh):
    out=[]
    for base,width,off in ((ROW_CQ,DK,0),(ROW_CK,DK,nh*DK),(ROW_CV,DV,2*nh*DK)):
        per=width//128
        for i in range(KCONV):
            for c in range(nh*per):
                out.append((base+i*H*per+s*nh*per+c,i,off+c*128))
    return out

def spread(n_d):
    per=128//H
    d=lax.broadcasted_iota(jnp.int32,(n_d,n_d//per),0); r=lax.broadcasted_iota(jnp.int32,(n_d,n_d//per),1)
    dd=lax.broadcasted_iota(jnp.int32,(n_d,128),0); l=lax.broadcasted_iota(jnp.int32,(n_d,128),1)
    return (d//per==r).astype(f32),(l//H==dd%per).astype(f32)

def pick(s,nh,first):
    l=lax.broadcasted_iota(jnp.int32,(128,128),0); j=lax.broadcasted_iota(jnp.int32,(128,128),1)-first
    return jnp.logical_and(jnp.logical_and(j>=0,j<nh),l%H==s*nh+j).astype(f32)

def unpack_small(packed,lens,s,nh,n_s,taps,vec,gain,gain1,gain2,w_sm,info,segr):
    taps[...]=jnp.zeros_like(taps)
    for row,i,off in tap_rows(s,nh): taps[i:i+1,off:off+128]=packed[pl.ds(row,1),:]
    lane=lax.broadcasted_iota(jnp.int32,(1,128),1)
    last=packed[ROW_AL:ROW_AL+1,:]
    vec[...]=jnp.zeros_like(vec)
    al=jnp.zeros((1,128),f32); dt=jnp.zeros((1,128),f32)
    for j in range(nh):
        al=al+jnp.where(lane==j,jnp.exp(jnp.sum(jnp.where(lane==s*nh+j,last,0.0),axis=1,keepdims=True)),0.0)
        dt=dt+jnp.where(lane==j,jnp.sum(jnp.where(lane==H+s*nh+j,last,0.0),axis=1,keepdims=True),0.0)
    vec[0:1]=al; vec[1:2]=dt
    gain[...]=jnp.broadcast_to(wide_row(packed,ROW_GO,gain.shape[1]),gain.shape)
    gain1[...]=jnp.broadcast_to(wide_row(packed,ROW_G1,gain1.shape[1]),gain1.shape)
    gain2[...]=jnp.broadcast_to(wide_row(packed,ROW_G2,gain2.shape[1]),gain2.shape)
    n_d=w_sm.shape[0]; per=n_d*H//128
    e1,mask=spread(n_d)
    t=jnp.zeros((n_d,128),f32)
    for k in range(2):
        a=dot(e1,packed[k*per:(k+1)*per,:],1,0,1)*mask
        t=t+dot(a,pick(s,nh,k*nh),1,0,1)
    w_sm[...]=t.astype(bf16)
    rows=info.shape[0]; count=lens.shape[1]
    lv=lens[...].astype(f32)
    ends=[];e=jnp.zeros((1,1),f32)
    for j in range(count):
        e=e+lv[:,j:j+1]; ends.append(e)
    def number(p):
        n=jnp.zeros_like(p)
        for e in ends: n=n+(p>=e).astype(f32)
        return jnp.where(p<0.0,-1.0,n)
    lanes=lax.broadcasted_iota(jnp.int32,(rows,128),1)
    pos=lax.broadcasted_iota(jnp.int32,(rows,128),0).astype(f32)
    shift=jnp.where(lanes<=3,-lanes,lanes-3).astype(f32)
    seg=number(pos)
    info[...]=jnp.where(lanes==0,seg,(number(pos+shift)==seg).astype(f32))
    segr[...]=number(lax.broadcasted_iota(jnp.int32,segr.shape,1).astype(f32))

def pack_small(sg,psm,taps,g_al,g_dt,gg,dg1,dg2,s,nh,n_s):
    sg[...]=jnp.zeros_like(sg)
    n_d=psm.shape[0]; per=n_d*H//128
    e1,mask=spread(n_d)
    for k in range(2):
        a=dot(psm,pick(s,nh,k*nh),1,1,6)*mask
        sg[k*per:(k+1)*per,:]=dot(e1,a,0,0,6)
    where={}
    for row,i,off in tap_rows(s,nh): where[i,off]=row
    for coff,w,_,tg in taps:
        for i in range(KCONV):
            for c in range(w//128):
                sg[pl.ds(where[i,coff+c*128],1),:]=tg[i][:,c*128:(c+1)*128]
    for first,v in ((ROW_G1,dg1),(ROW_G2,dg2),(ROW_GO,gg)):
        for i in range(v.shape[1]//128): sg[first+i:first+i+1,:]=v[:,i*128:(i+1)*128]
    lane=lax.broadcasted_iota(jnp.int32,(1,128),1)
    t=jnp.zeros((1,128),f32)
    for j in range(nh):
        t=t+jnp.where(lane==s*nh+j,g_al[:,j:j+1],0.0)+jnp.where(lane==H+s*nh+j,g_dt[:,j:j+1],0.0)
    sg[ROW_AL:ROW_AL+1,:]=t

def share_small(n_dp,n_s,sg,land,ss,rs):
    d,s,_,_=place()
    me=d*n_s+s
    def one(q,_):
        src=sg.at[pl.ds(pl.multiple_of(q*SLICE,SLICE),SLICE)]
        @pl.when(q==me)
        def _():
            pltpu.make_async_copy(src,land.at[me],rs.at[0]).start()
        @pl.when(q!=me)
        def _():
            remote(src,land.at[me],ss.at[0],rs.at[0],(q//n_s,q%n_s)).start()
        return 0
    lax.fori_loop(0,SMALL_ROWS//SLICE,one,0)

def shared_small(n_dp,n_s,sg,land,ss,rs):
    d,s,_,_=place()
    me=d*n_s+s
    n=SMALL_ROWS//SLICE
    @pl.when(me<n)
    def _():
        pltpu.make_async_copy(land,land,rs.at[0]).wait()
        part=sg.at[pl.ds(0,SLICE*(n-1))]
        pltpu.make_async_copy(part,part,ss.at[0]).wait()
    @pl.when(me>=n)
    def _():
        pltpu.make_async_copy(sg,sg,ss.at[0]).wait()

def spread_small(n_dp,n_s,land,total,part,ss,rs):
    d,s,_,_=place()
    me=d*n_s+s; nd=n_dp*n_s
    @pl.when(me<SMALL_ROWS//SLICE)
    def _():
        t=land[0]
        for q in range(1,nd): t=t+land[q]
        part[...]=t
        dst=total.at[pl.ds(pl.multiple_of(me*SLICE,SLICE),SLICE)]
        def one(q,_):
            @pl.when(q==me)
            def _():
                pltpu.make_async_copy(part,dst,rs.at[0]).start()
            @pl.when(q!=me)
            def _():
                remote(part,dst,ss.at[0],rs.at[0],(q//n_s,q%n_s)).start()
            return 0
        lax.fori_loop(0,nd,one,0)

def spread_done(n_dp,n_s,land,total,ss,rs):
    d,s,_,_=place()
    me=d*n_s+s; nd=n_dp*n_s
    @pl.when(me<SMALL_ROWS//SLICE)
    def _():
        sent=land.at[pl.ds(0,nd-1)]
        pltpu.make_async_copy(sent,sent,ss.at[0]).wait()
    pltpu.make_async_copy(total,total,rs.at[0]).wait()


f32=jnp.float32; bf16=jnp.bfloat16
CA,CB,CC=3.4445,-4.775,2.0315
NS_STEPS=2
PANEL=512
def dg(a,b,ca,cb): return lax.dot_general(a,b,(((ca,),(cb,)),((),())),preferred_element_type=f32)

def mirror(m,i,r,tm):
    for j in range(i+1,r//tm):
        m[j*tm:(j+1)*tm,i*tm:(i+1)*tm]=m[i*tm:(i+1)*tm,j*tm:(j+1)*tm].T

def newton_schulz(wide,tall,tmp,acc,g,p,is_tall,count,tm=256):
    r=g.shape[0]
    at=lambda c: pl.ds(pl.multiple_of(c*PANEL,PANEL),PANEL)
    def both(fw,ft):
        @pl.when(jnp.logical_not(is_tall))
        def _(): lax.fori_loop(0,count,fw,0)
        @pl.when(is_tall)
        def _(): lax.fori_loop(0,count,ft,0)
    tmp[...]=jnp.zeros_like(tmp)
    def sqw(c,_):
        def one(k,_):
            v=wide[pl.ds(pl.multiple_of(k*128,128),128),at(c)].astype(f32)
            tmp[0:1,0:PANEL]=tmp[0:1,0:PANEL]+jnp.sum(v*v,axis=0,keepdims=True)
            return 0
        return lax.fori_loop(0,r//128,one,0)
    def sqt(c,_):
        def one(k,_):
            v=tall[pl.ds(pl.multiple_of(c*PANEL+k*128,128),128),:].astype(f32)
            tmp[0:1,:]=tmp[0:1,:]+jnp.sum(v*v,axis=0,keepdims=True)
            return 0
        return lax.fori_loop(0,PANEL//128,one,0)
    both(sqw,sqt)
    inv=1.0/(jnp.sqrt(jnp.sum(tmp[0:1,:],axis=1,keepdims=True))+1e-7)
    def scw(c,_):
        def one(k,_):
            q=pl.ds(pl.multiple_of(k*128,128),128)
            wide[q,at(c)]=(wide[q,at(c)].astype(f32)*inv).astype(bf16)
            return 0
        return lax.fori_loop(0,r//128,one,0)
    def sct(c,_):
        def one(k,_):
            q=pl.ds(pl.multiple_of(c*PANEL+k*128,128),128)
            tall[q,:]=(tall[q,:].astype(f32)*inv).astype(bf16)
            return 0
        return lax.fori_loop(0,PANEL//128,one,0)
    both(scw,sct)
    def step(_,__):
        acc[...]=jnp.zeros_like(acc)
        def gw(c,_):
            for i in range(r//tm):
                ri=slice(i*tm,(i+1)*tm)
                acc[ri,i*tm:r]+=dg(wide[ri,at(c)],wide[i*tm:r,at(c)],1,1)
            return 0
        def gt(c,_):
            for i in range(r//tm):
                ri=slice(i*tm,(i+1)*tm)
                acc[ri,i*tm:r]+=dg(tall[at(c),ri],tall[at(c),i*tm:r],0,0)
            return 0
        both(gw,gt)
        for i in range(r//tm):
            ri=slice(i*tm,(i+1)*tm)
            g[ri,i*tm:r]=acc[ri,i*tm:r].astype(bf16)
            mirror(g,i,r,tm)
        for i in range(r//tm):
            ri=slice(i*tm,(i+1)*tm)
            p[ri,i*tm:r]=(CB*g[ri,i*tm:r].astype(f32)+CC*dg(g[ri,:],g[:,i*tm:r],1,0)).astype(bf16)
            mirror(p,i,r,tm)
        def nw(c,_):
            g[:,0:PANEL]=wide[:,at(c)]
            for i in range(r//PANEL):
                ri=slice(i*PANEL,(i+1)*PANEL)
                wide[ri,at(c)]=(CA*g[ri,0:PANEL].astype(f32)+dg(p[ri,:],g[:,0:PANEL],1,0)).astype(bf16)
            return 0
        def nt(c,_):
            v=tall[at(c),:]
            tall[at(c),:]=(CA*v.astype(f32)+dg(v,p[...],1,0)).astype(bf16)
            return 0
        both(nw,nt)
        return 0
    lax.fori_loop(0,NS_STEPS,step,0)


MOMENTUM = 0.95
MUON_RATE = 0.1
MUON_DECAY = 0.01

def muon_owner(i,n_dp):
    base=n_dp//2-2
    d,s=((2,0),(3,0),(1,2),(3,2),(2,2),(0,0),(1,0),(0,2))[i]
    return base+d,s

def grad_blocks(i,landed):
    gu,dn,out,gate,qkv=landed
    if i==4: return [(0,out[...].astype(f32))]
    if i==7: return [(0,dn[...].astype(f32))]
    n_s=gu.shape[0]
    if i in (5,6):
        ref,w=gu,gu.shape[2]//2; at=(i-5)*w
    elif i==3:
        ref,w,at=gate,gate.shape[2],0
    else:
        q=qkv.shape[2]//4
        ref,w,at=qkv,(q,q,2*q)[i],(0,q,2*q)[i]
    return [(t*w,ref[t,:,at:at+w].astype(f32)) for t in range(n_s)]

def member(i,refs):
    a,k=((0,0),(0,1),(1,0),(1,1),(2,None),(3,0),(3,1),(4,None))[i]
    return refs[a],k

def part_of(ref,k,col,w):
    return ref[:,col:col+w] if k is None else ref[k,:,col:col+w]

def store_part(ref,k,col,v):
    if k is None: ref[:,col:col+v.shape[1]]=v
    else: ref[k,:,col:col+v.shape[1]]=v

EARLY=(7,5,6,4,3)

def kinds_of(momenta,nd):
    kinds=[]
    for i in range(8):
        r,c=member(i,momenta)[0].shape[-2:]
        tall=r*nd>c
        kinds.append((tall,-(-r//16)*16 if tall else r,c))
    return tuple(kinds)

def land_shapes(kinds,nd):
    r=min(min(k[1]*nd,k[2]) for k in kinds)
    up=lambda x: -(-x//PANEL)*PANEL
    return (r,up(max(k[2] for k in kinds if not k[0]))),(up(max(k[1]*nd for k in kinds if k[0])),r)

def make_look(i,look,landed,momenta):
    ref,k=member(i,momenta)
    rows=ref.shape[-2]
    if look.shape[0]>rows: look[rows:,:]=jnp.zeros((look.shape[0]-rows,look.shape[1]),bf16)
    for col,v in grad_blocks(i,landed):
        m=MOMENTUM*part_of(ref,k,col,v.shape[1])+v
        look[0:rows,col:col+v.shape[1]]=(v+MOMENTUM*m).astype(bf16)

def slot(kind,buf,q):
    t,rows,cols=kind
    ds=pl.ds(pl.multiple_of(q*rows,rows),rows)
    return buf.at[ds] if t else buf.at[ds,pl.ds(0,cols)]

def whole(kind,buf,nd):
    t,rows,cols=kind
    return buf.at[pl.ds(0,rows*nd)] if t else buf.at[:,pl.ds(0,cols)]

class Early:
    def __init__(self,n_dp,n_s,kinds,look,landed,momenta,wide,tall,rin,sin):
        self.d,self.s,_,_=place()
        self.n_dp=n_dp; self.nd=n_dp*n_s; self.me=self.d*n_s+self.s
        self.kinds=kinds; self.look=look; self.landed=landed; self.momenta=momenta
        self.wide=wide; self.tall=tall; self.rin=rin; self.sin=sin; self.sent=[]
    def at(self,i):
        o=muon_owner(i,self.n_dp)
        return o,jnp.logical_and(self.d==o[0],self.s==o[1])
    def buf(self,i): return self.tall if self.kinds[i][0] else self.wide
    def push(self,i):
        self.sent.append(i)
        make_look(i,self.look[i],self.landed,self.momenta)
        o,there=self.at(i)
        dst=slot(self.kinds[i],self.buf(i),self.me)
        @pl.when(there)
        def _():
            pltpu.make_async_copy(self.look[i],dst,self.rin.at[0]).start()
        @pl.when(jnp.logical_not(there))
        def _():
            remote(self.look[i],dst,self.sin.at[i],self.rin.at[0],o).start()
    def arrived(self,i):
        full=whole(self.kinds[i],self.buf(i),self.nd)
        pltpu.make_async_copy(full,full,self.rin.at[0]).wait()
    def left(self,i):
        _,there=self.at(i)
        @pl.when(jnp.logical_not(there))
        def _():
            pltpu.make_async_copy(self.look[i],self.look[i],self.sin.at[i]).wait()
    def wait(self):
        for i in self.sent:
            _,there=self.at(i)
            @pl.when(there)
            def _():
                self.arrived(i)
            self.left(i)

def muon_kernel(n_dp,n_s,kinds,*refs):
    n=len(kinds)
    landed=refs[:5]; momenta=refs[5:10]; xwide,xtall,sland=refs[10:13]; outs=refs[13:13+n]; stot=refs[13+n]
    late=[i for i in (2,0,1)]
    look=dict(zip(late,refs[14+n:17+n]))
    wide,tall,tmp,acc,g,p,spart,rin,sin,rout,sout,lsem,st,rt=refs[17+n:]
    nd=n_dp*n_s
    E=Early(n_dp,n_s,kinds,look,landed,momenta,wide,tall,rin,sin)
    for i in EARLY:
        _,there=E.at(i)
        @pl.when(there)
        def _():
            pltpu.make_async_copy(whole(kinds[i],xtall if kinds[i][0] else xwide,nd),whole(kinds[i],E.buf(i),nd),lsem.at[0]).start()
    greet_all(n_dp,n_s)
    spread_small(n_dp,n_s,sland,stot,spart,st,rt)
    for i in late: E.push(i)
    count=jnp.int32(0); tall_here=jnp.int32(0); here=jnp.int32(0)
    for i in range(n):
        t,rows,cols=kinds[i]
        _,there=E.at(i)
        one=there.astype(jnp.int32)
        size=rows*nd if t else cols
        count=count+one*(-(-size//PANEL)); here=here+one
        if t: tall_here=tall_here+one
        pad=-size%PANEL
        @pl.when(there)
        def _():
            if pad:
                if t: tall[size:size+pad,:]=jnp.zeros((pad,tall.shape[1]),bf16)
                else: wide[:,size:size+pad]=jnp.zeros((wide.shape[0],pad),bf16)
            if i in late: E.arrived(i)
            else:
                full=whole(kinds[i],E.buf(i),nd)
                pltpu.make_async_copy(full,full,lsem.at[0]).wait()
    @pl.when(here>0)
    def _():
        newton_schulz(wide,tall,tmp,acc,g,p,tall_here>0,count)
    for i in range(n):
        t,rows,cols=kinds[i]
        _,there=E.at(i)
        @pl.when(there)
        def _():
            buf=E.buf(i)
            def send(k,_):
                q=((k+E.d)%n_dp)*n_s+(E.s+k//n_dp)%n_s
                src=slot(kinds[i],buf,q)
                @pl.when(q==E.me)
                def _():
                    pltpu.make_async_copy(src,outs[i],rout.at[i]).start()
                @pl.when(q!=E.me)
                def _():
                    remote(src,outs[i],sout.at[0],rout.at[i],(q//n_s,q%n_s)).start()
                return 0
            lax.fori_loop(0,nd,send,0)
            part=buf.at[pl.ds(0,rows*(nd-1))] if t else buf.at[pl.ds(0,rows*(nd-1)),pl.ds(0,cols)]
            pltpu.make_async_copy(part,part,sout.at[0]).wait()
    for i in late: E.left(i)
    spread_done(n_dp,n_s,sland,stot,st,rt)
    for i in range(n):
        pltpu.make_async_copy(outs[i],outs[i],rout.at[i]).wait()

def muon(landed,momenta,xwide,xtall,sland,n_dp,n_s,cid):
    nd=n_dp*n_s
    kinds=kinds_of(momenta,nd)
    xw,xt=land_shapes(kinds,nd); r=xw[0]
    V=pltpu.VMEM
    return pl.pallas_call(functools.partial(muon_kernel,n_dp,n_s,kinds),
        out_shape=[jax.ShapeDtypeStruct(k[1:],bf16) for k in kinds]+[jax.ShapeDtypeStruct((SMALL_ROWS,128),f32)],in_specs=[VM]*10+[ANY]*2+[VM],out_specs=[VM]*9,
        scratch_shapes=[V(kinds[i][1:],bf16) for i in (2,0,1)]+[V(xw,bf16),V(xt,bf16),V((8,r),f32),V((r,r),f32)]+[V((r,r),bf16)]*2+[V((SLICE,128),f32)]+[D_((1,)),D_((8,)),D_((8,)),D_((1,)),D_((1,)),D_((1,)),D_((1,))],
        compiler_params=pltpu.CompilerParams(collective_id=cid,has_side_effects=True,vmem_limit_bytes=62<<20),name="muon")(*landed,*momenta,xwide,xtall,sland)

def finish_kernel(nd,*refs):
    landed=refs[:5]; momenta=refs[5:10]; masters=refs[10:15]; orthos=refs[15:23]
    grads=refs[23:28]; steps=refs[28:33]; moms=refs[33:38]
    for i in range(8):
        ms,k=member(i,masters)
        rows,cols=ms.shape[-2:]
        scale=0.2*math.sqrt(max(rows*nd,cols))
        for col,v in grad_blocks(i,landed):
            w=v.shape[1]
            store_part(member(i,grads)[0],k,col,v)
            store_part(member(i,moms)[0],k,col,MOMENTUM*part_of(member(i,momenta)[0],k,col,w)+v)
        o=orthos[i][0:rows,:].astype(f32)
        store_part(member(i,steps)[0],k,0,-MUON_RATE*(scale*o+MUON_DECAY*part_of(ms,k,0,cols)))

def finish(landed,momenta,masters,orthos,nd):
    out=[jax.ShapeDtypeStruct(m.shape,f32) for m in masters]
    return pl.pallas_call(functools.partial(finish_kernel,nd),out_shape=out*3,in_specs=[VM]*23,out_specs=[VM]*15,
        compiler_params=pltpu.CompilerParams(vmem_limit_bytes=60<<20),name="updates")(*landed,*momenta,*masters,*orthos)


class Gatherer:
    def __init__(self,n_dp,n_s,ins,outs,ncol,sems,order):
        self.n_dp=n_dp; self.n_s=n_s; self.n_hi=n_dp//2; self.ins=ins; self.outs=outs; self.ncol=ncol; self.order=order
        self.s0,self.r0,self.s1,self.r1,self.lsem=sems
        d,s,hi,lo=place()
        self.d=d; self.s=s; self.hi=hi; self.lo=lo
        me=d*n_s+s
        self.td=me%n_dp; self.ts=me//n_dp
        self.fd=(s*n_dp+d)//n_s; self.fs=(s*n_dp+d)%n_s
        self.moved=jnp.logical_or(self.td!=d,self.ts!=s)
        self.zs=[((hi+j)%self.n_hi)*2+lo for j in range(1,self.n_hi)]
        self.xd=(hi*2+(1-lo),s)
        self.grp=ring(n_s)
        self.col={}; self.done=set(); self.i=0
    def greet(self):
        bar=pltpu.get_barrier_semaphore()
        peers=self.grp+[(z,self.s) for z in self.zs]+[self.xd]
        for p in peers: pl.semaphore_signal(bar,inc=1,device_id=p,device_id_type=MESH)
        @pl.when(self.moved)
        def _():
            pl.semaphore_signal(bar,inc=1,device_id=(self.td,self.ts),device_id_type=MESH)
            pl.semaphore_signal(bar,inc=1,device_id=(self.fd,self.fs),device_id_type=MESH)
            pl.semaphore_wait(bar,len(peers)+2)
        @pl.when(jnp.logical_not(self.moved))
        def _():
            pl.semaphore_wait(bar,len(peers))
    def phase0(self,k):
        src,dst=self.ins[k],self.outs[k]
        if k<self.ncol:
            c=pltpu.make_async_copy(src.at[self.s],dst.at[self.d,self.s],self.lsem.at[k]); c.start()
            self.col[k]=[c]
            for j,p in enumerate(self.grp):
                c=remote(src.at[p[1]],dst.at[self.d,self.s],self.s0.at[k,j],self.r0.at[k,j],p); c.start(); self.col[k].append(c)
        else:
            @pl.when(self.moved)
            def _():
                remote(src,dst.at[self.td],self.s0.at[k,0],self.r0.at[k,0],(self.td,self.ts)).start()
            @pl.when(jnp.logical_not(self.moved))
            def _():
                pltpu.make_async_copy(src,dst.at[self.d],self.r0.at[k,0]).start()
    def ready(self,k):
        if k in self.done: return
        self.done.add(k)
        if k<self.ncol:
            for c in self.col[k]: c.wait()
        else:
            src,dst=self.ins[k],self.outs[k]
            pltpu.make_async_copy(src,dst.at[self.d],self.r0.at[k,0]).wait()
            @pl.when(self.moved)
            def _():
                remote(src,dst.at[self.td],self.s0.at[k,0],self.r0.at[k,0],(self.td,self.ts)).wait_send()
    def blk(self,i,src):
        k,a,m=self.order[i]
        return self.outs[k].at[src,a:a+m] if m else self.outs[k].at[src]
    def go(self,i,j,b,dev):
        return remote(b,b,self.s1.at[i,j],self.r1.at[i,j],dev)
    def tick(self,times=1):
        n=len(self.order); nh=self.n_hi
        for _ in range(times):
            i=self.i; self.i+=1
            if i<n:
                self.ready(self.order[i][0])
                own=self.blk(i,self.d)
                for j,z in enumerate(self.zs): self.go(i,j,own,(z,self.s)).start()
                self.go(i,nh-1,own,self.xd).start()
            if 0<=i-1<n:
                for j in range(1,nh):
                    b=self.blk(i-1,((self.hi-j)%nh)*2+self.lo)
                    self.go(i-1,j-1,b,self.xd).wait()
                    self.go(i-1,nh-1+j,b,self.xd).start()
            if 0<=i-2<n:
                for j in range(nh):
                    self.go(i-2,nh-1+j,self.blk(i-2,((self.hi-j)%nh)*2+(1-self.lo)),self.xd).wait()
    def after(self,i):
        while self.i<i+3: self.tick()
    def drain(self):
        self.after(len(self.order)-1)

def dotb(a,b,ca,cb): return lax.dot_general(a,b,(((ca,),(cb,)),((),())),preferred_element_type=f32)

def fore_kernel(n_dp,n_s,nh,P,order,last_in,last_out,*refs):
    (qk,vg,gu,ow,dw,x_ref,dyown,packed,lens,
     g_in,g_gu,g_out,g_dn,normed,dy,raw,small,gated,o_ref,u_ref,s_ref,xi_ref,middle,gath,w_sm,taps,vec,gain,gain1,gain2,info,segr,
     c_in,c_gu,c_out,c_dn,part,land)=refs[:38]
    sems=refs[38:43]; ss,rs=refs[43:45]
    E=Gatherer(n_dp,n_s,[c_in,c_gu,c_out,c_dn],[g_in,g_gu,g_out,g_dn],2,sems,order)
    s=E.s
    kq=nh*DK; kv=nh*DV; ff=c_gu.shape[2]//2
    for t in range(n_s):
        c_in[t,:,0:kq]=qk[0,:,t*kq:(t+1)*kq].astype(bf16)
        c_in[t,:,kq:2*kq]=qk[1,:,t*kq:(t+1)*kq].astype(bf16)
        c_in[t,:,2*kq:2*kq+kv]=vg[0,:,t*kv:(t+1)*kv].astype(bf16)
        c_in[t,:,2*kq+kv:]=vg[1,:,t*kv:(t+1)*kv].astype(bf16)
    E.greet()
    E.phase0(0)
    g1=wide_row(packed,ROW_G1,gain1.shape[1])
    xv=x_ref[...].astype(f32)
    normed[s]=(xv*lax.rsqrt(jnp.mean(xv*xv,axis=-1,keepdims=True)+NORM_EPS)*g1).astype(bf16)
    c_out[...]=ow[...].astype(bf16)
    E.phase0(2)
    a=push_all(n_s,normed,ss.at[0],rs.at[0])
    E.tick(1)
    for t in range(n_s):
        c_gu[t,:,0:ff]=gu[0,:,t*ff:(t+1)*ff].astype(bf16)
        c_gu[t,:,ff:]=gu[1,:,t*ff:(t+1)*ff].astype(bf16)
    c_dn[...]=dw[...].astype(bf16)
    E.phase0(1); E.phase0(3)
    unpack_small(packed,lens,s,nh,n_s,taps,vec,gain,gain1,gain2,w_sm,info,segr)
    E.tick(1)
    dy[s]=dyown[...]
    b=push_all(n_s,dy,ss.at[1],rs.at[1])
    for c in a: c.wait()
    local,D=x_ref.shape; rows=local*n_s
    nrm=normed[...].reshape(rows,D)
    small[...]=dotb(nrm,w_sm[...],1,0)
    E.after(last_in)
    raw[...]=dotb(nrm,g_in[...].reshape(D,raw.shape[1]),1,0)
    E.tick()
    for i,_ in enumerate(mixer_fwd(raw,small,taps,vec,gain,info,segr,gated,o_ref,u_ref,s_ref,xi_ref,nh,P)):
        if i%2==0: E.tick()
    E.after(last_out)
    part[...]=dotb(gated[...],g_out[...].reshape(nh*DV,D),1,0).astype(bf16).reshape(part.shape)
    c1=push_parts(n_s,part,land,ss.at[2],rs.at[2])
    E.tick()
    for c in c1: c.wait()
    m=x_ref[...].astype(f32)+add_up(n_s,part,land)
    middle[...]=m
    r=lax.rsqrt(jnp.mean(m*m,axis=-1,keepdims=True)+NORM_EPS)
    gath[s]=(m*r*gain2[0:1]).astype(bf16)
    c2=push_all(n_s,gath,ss.at[3],rs.at[3])
    E.drain()
    for c in c2: c.wait()
    for c in b: c.wait()

def fore(qk,vg,gu,ow,dw,x,dyown,packed,lens,n_dp,n_s,P,cid):
    ins=[qk,vg,gu,ow,dw,x,dyown,packed,lens]
    local,D=x.shape; rows=local*n_s; n_hi=n_dp//2
    nh=H//n_s; wid=nh*(2*DK+2*DV); nb=nh*rows//CH
    order=tuple([(0,i,1) for i in range(n_s)]+[(2,0,0)]+[(1,i,1) for i in range(n_s)]+[(3,0,0)])
    S_=jax.ShapeDtypeStruct; V=pltpu.VMEM
    ps=[(n_s,qk.shape[1],wid),(n_s,gu.shape[1],2*gu.shape[2]//n_s),ow.shape,dw.shape]
    outs=[S_((n_dp,)+q,bf16) for q in ps]+[S_((n_s,local,D),bf16)]*2+[S_((rows,wid),f32),S_((rows,128),f32),S_((rows,nh*DV),bf16),S_((rows,nh*DV),f32),S_((rows,nh*DV),f32),
          S_((nb,DK,DV),f32),S_((nb,CH,CH),f32),S_((local,D),f32),S_((n_s,local,D),bf16)]
    outs+=[S_((D,128),bf16),S_((8,nh*(2*DK+DV)),f32),S_((8,128),f32),S_((8,DV),f32),S_((8,D),f32),S_((8,D),f32),S_((rows,128),f32),S_((8,rows),f32)]
    sc=[V(q,bf16) for q in ps]+[V((n_s,local,D),bf16),V((n_s-1,local,D),bf16)]
    sc+=[D_((4,n_s))]*2+[D_((len(order),2*n_hi))]*2+[D_((4,))]+[D_((4,n_s))]*2
    return pl.pallas_call(functools.partial(fore_kernel,n_dp,n_s,nh,P,order,n_s-1,n_s),
        out_shape=outs,in_specs=[VM]*len(ins),out_specs=[VM]*len(outs),scratch_shapes=sc,
        compiler_params=pltpu.CompilerParams(collective_id=cid,has_side_effects=True,vmem_limit_bytes=63<<20),name="forward")(*ins)


class Reducer:
    def __init__(self,n_dp,n_s,pieces,sems,W):
        self.n_s=n_s; self.n_hi=n_dp//2; self.p=pieces; self.W=W
        self.sx,self.rx,self.sz,self.rz,self.sf,self.rf,self.lsem=sems
        d,s,hi,lo=place()
        self.s=s; self.hi=hi; self.lo=lo
        me=s*n_dp+d
        self.td=me//n_s; self.ts=me%n_s
        own=d*n_s+s
        self.fd=own%n_dp; self.fs=own//n_dp
        self.moved=jnp.logical_or(self.td!=d,self.ts!=s)
        self.xd=(hi*2+(1-lo),s)
        self.zd=lambda j:(((hi+j)%self.n_hi)*2+lo,s)
        self.grp=ring(n_s)
        self.q=[]; self.ns=0; self.nh=0; self.late=[]; self.fc={}; self.hook=None
    def xc(self,k,j):
        z=(self.hi+j)%self.n_hi; p=self.p[k]
        return remote(p["g"].at[z*2+1-self.lo],p["xl"].at[j],self.sx.at[k,j],self.rx.at[k,j],self.xd)
    def xw(self,k,j):
        return self.xc(k,j)
    def zc(self,k,j):
        p=self.p[k]
        return remote(p["xl"].at[j],p["zl"].at[j-1],self.sz.at[k,j],self.rz.at[k,j],self.zd(j))
    def add(self,k):
        self.q+=[(k,j) for j in list(range(1,self.n_hi))+[0]]
    def handle(self,k,j):
        p=self.p[k]; z=(self.hi+j)%self.n_hi
        self.xw(k,j).wait()
        if j:
            p["xl"][j]=(p["g"][z*2+self.lo].astype(f32)+p["xl"][j].astype(f32)).astype(bf16); self.zc(k,j).start()
        else:
            self.late.append([k,2,self.finish])
    def finish(self,k):
        p=self.p[k]; t=p["g"][self.hi*2+self.lo].astype(f32)+p["xl"][0].astype(f32)
        for j in range(1,self.n_hi):
            self.zc(k,j).wait()
            t=t+p["zl"][j-1].astype(f32)
        t=t.astype(bf16)
        fin,out=p["fin"],p["out"]
        if p["col"]:
            rows=t.shape[0]//self.n_s
            fin[...]=t.reshape(self.n_s,rows,t.shape[1])
            c=pltpu.make_async_copy(fin.at[self.s],out.at[self.s],self.lsem.at[k]); c.start()
            self.fc[k]=[c]
            for j,q in enumerate(self.grp):
                c=remote(fin.at[q[1]],out.at[self.s],self.sf.at[k,j],self.rf.at[k,j],q); c.start(); self.fc[k].append(c)
        else:
            fin[...]=t
            @pl.when(self.moved)
            def _():
                remote(fin,out,self.sf.at[k,0],self.rf.at[k,0],(self.td,self.ts)).start()
            @pl.when(jnp.logical_not(self.moved))
            def _():
                pltpu.make_async_copy(fin,out,self.rf.at[k,0]).start()
        self.late.append([k,2,self.landed])
    def tick(self,times=1):
        for _ in range(times):
            if self.ns<len(self.q):
                self.xc(*self.q[self.ns]).start(); self.ns+=1
                if self.ns-self.nh>self.W:
                    self.handle(*self.q[self.nh]); self.nh+=1
            elif self.nh<self.ns:
                self.handle(*self.q[self.nh]); self.nh+=1
            for e in list(self.late):
                e[1]-=1
                if e[1]<0:
                    self.late.remove(e); e[2](e[0])
    def landed(self,k):
        p=self.p[k]
        if p["col"]:
            for c in self.fc[k]: c.wait()
        else:
            fin,out=p["fin"],p["out"]
            pltpu.make_async_copy(fin,out,self.rf.at[k,0]).wait()
            @pl.when(self.moved)
            def _():
                remote(fin,out,self.sf.at[k,0],self.rf.at[k,0],(self.td,self.ts)).wait_send()
        if self.hook: self.hook(k)
    def drain(self):
        while self.nh<len(self.q) or self.late: self.tick()

def dotb(a,b,ca,cb): return lax.dot_general(a,b,(((ca,),(cb,)),((),())),preferred_element_type=f32)

def back_kernel(n_dp,n_s,nh,P,W,kinds,*refs):
    (gu_ref,dn_ref,ypart,dpart,middle,dy,x_ref,gain2,gain1,w_out,w_in,w_sm,raw,small,taps,vec,gain,info,segr,normed,gated,o_ref,u_ref,s_ref,xi_ref,m_vg,m_out,m_gu,m_dn,
     out_gu,out_dn,out_out,out_g,out_q,bout,igrad,stot,xwide,xtall,
     yland,dland,gath,dgt,draw,dsb,epart,dmid,
     p_out,p_g,p_q,sg)=refs[:51]
    rest=refs[51:]
    xl=rest[0:5]; zl=rest[5:10]; fin=rest[10:15]; look=dict(zip(EARLY,rest[15:20]))
    sems=rest[20:27]; ss,rs,st,rt,lin,lout=rest[27:33]
    gs=(gu_ref,dn_ref,p_out,p_g,p_q); outs=(out_gu,out_dn,out_out,out_g,out_q)
    pieces=[dict(g=gs[k],xl=xl[k],zl=zl[k],fin=fin[k],out=outs[k],col=k in (0,3,4)) for k in range(5)]
    E=Reducer(n_dp,n_s,pieces,sems,W)
    s=E.s
    greet_all(n_dp,n_s)
    early=Early(n_dp,n_s,kinds,look,(out_gu,out_dn,out_out,out_g,None),(None,m_vg,m_out,m_gu,m_dn),xwide,xtall,lin,lout)
    E.hook=lambda k: [early.push(i) for i in {0:(5,6),1:(7,),2:(4,),3:(3,),4:()}[k]]
    b=push_parts(n_s,dpart,dland,ss.at[0],rs.at[0])
    E.add(1); E.add(0)
    E.tick(W)
    for c in b: c.wait()
    m=middle[...]
    du,dg=norm_back(m,gain2[0:1],add_up(n_s,dpart,dland))
    dm=dy[...].astype(f32)+du
    dmid[...]=dm
    dg2=dg
    gath[s]=dm.astype(bf16)
    g=push_all(n_s,gath,ss.at[1],rs.at[1])
    E.tick(3)
    for c in g: c.wait()
    a=push_parts(n_s,ypart,yland,ss.at[2],rs.at[2])
    rows=raw.shape[0]; D=gath.shape[2]
    dbr=gath[...].reshape(rows,D)
    dgt[...]=dotb(dbr,w_out[...],1,1)
    E.tick(1)
    p_out[...]=dotb(gated[...],dbr,0,0).astype(bf16).reshape(p_out.shape)
    E.add(2)
    n=CH; off=2*nh*DK+nh*DV
    def emit(h,c,v): draw[c*n:(c+1)*n,off+h*DV:off+(h+1)*DV]=v.astype(bf16)
    dO,gg=gate_back(raw,gain[0:1],dgt,o_ref,nh,emit)
    E.tick(1)
    p_g[...]=dotb(normed[...],draw[:,off:],0,0).astype(bf16).reshape(p_g.shape)
    E.add(3)
    res=[]
    for _ in mixer_bwd(raw,small,taps,vec,info,segr,dO,u_ref,s_ref,xi_ref,nh,P,res):
        E.tick(1)
    dsmall,g_dt,g_al=res[0]
    for coff,w,dcol,tg in res[1:]:
        draw[:,coff:coff+w]=dcol.astype(bf16)
    dsb[...]=dsmall.astype(bf16)
    p_q[...]=dotb(normed[...],draw[:,:off],0,0).astype(bf16).reshape(p_q.shape)
    E.add(4)
    E.tick(2)
    epart[...]=(dotb(draw[...],w_in[...],1,1)+dotb(dsb[...],w_sm[...],1,1)).astype(bf16).reshape(epart.shape)
    e=push_parts(n_s,epart,dland,ss.at[3],rs.at[3])
    for c in a: c.wait()
    bout[...]=(middle[...]+add_up(n_s,ypart,yland)).astype(bf16)
    psm=dotb(normed[...],dsb[...],0,0)
    E.tick(2)
    for c in e: c.wait()
    du,dg=norm_back(x_ref[...].astype(f32),gain1[0:1],add_up(n_s,epart,dland))
    igrad[...]=(dmid[...]+du).astype(bf16)
    pack_small(sg,psm,res[1:],g_al,g_dt,gg,dg,dg2,s,nh,n_s)
    share_small(n_dp,n_s,sg,stot,st,rt)
    E.drain()
    shared_small(n_dp,n_s,sg,stot,st,rt)
    early.wait()

def back(part_gu,part_dn,ypart,dpart,middle,dy,x,gain2,gain1,w_out,w_in,w_sm,raw,small,taps,vec,gain,info,segr,normed,gated,O,U,S,X,momenta,n_dp,n_s,P,cid,W=4):
    ins=[part_gu,part_dn,ypart,dpart,middle,dy,x,gain2,gain1,w_out,w_in,w_sm,raw,small,taps,vec,gain,info,segr,normed,gated,O,U,S,X]+list(momenta[1:])
    local,D=x.shape; rows=local*n_s; nh=raw.shape[1]//(2*DK+2*DV); n_hi=n_dp//2
    off=2*nh*DK+nh*DV
    shp=[part_gu.shape,part_dn.shape,(n_dp,w_out.shape[0]//n_dp,D),(n_dp,D//n_dp,nh*DV),(n_dp,D//n_dp,off)]
    col=(0,3,4)
    osh=[(n_s,q[1]//n_s,q[2]) if k in col else q[1:] for k,q in enumerate(shp)]
    S_=jax.ShapeDtypeStruct; V=pltpu.VMEM
    outs=[S_(q,bf16) for q in osh]+[S_((local,D),bf16),S_((local,D),bf16),S_((n_dp*n_s,SLICE,128),f32)]
    kinds=kinds_of(momenta,n_dp*n_s); xw,xt=land_shapes(kinds,n_dp*n_s)
    outs+=[S_(xw,bf16),S_(xt,bf16)]
    sc=[V((n_s-1,local,D),bf16)]*2+[V((n_s,local,D),bf16),V((rows,nh*DV),f32),V((rows,raw.shape[1]),bf16),V((rows,128),bf16),V((n_s,local,D),bf16),V((local,D),f32)]
    sc+=[V(shp[k],bf16) for k in (2,3,4)]+[V((SMALL_ROWS,128),f32)]
    sc+=[V((n_hi,)+q[1:],bf16) for q in shp]+[V((n_hi-1,)+q[1:],bf16) for q in shp]+[V(q,bf16) for q in osh]+[V(kinds[i][1:],bf16) for i in EARLY]
    sc+=[D_((5,n_hi))]*4+[D_((5,n_s))]*2+[D_((5,))]+[D_((4,n_s))]*2+[D_((1,))]*2+[D_((1,)),D_((8,))]
    return pl.pallas_call(functools.partial(back_kernel,n_dp,n_s,nh,P,W,kinds),
        out_shape=outs,in_specs=[VM]*len(ins),out_specs=[VM]*(len(outs)-2)+[ANY]*2,scratch_shapes=sc,
        compiler_params=pltpu.CompilerParams(collective_id=cid,has_side_effects=True,vmem_limit_bytes=63<<20),name="backward")(*ins)


STEP_COUNT = 10
ADAM_RATE = 0.05
BETA_ONE = 0.9
BETA_TWO = 0.95
ADAM_EPS = 1e-08
PASSES = dict(kk=3, qk=3, inv=3, u=3, s=3, o=3, g=3)


def mm(a, b, ca, cb, kind=f32):
    return lax.dot_general(
        a, b, (((ca,), (cb,)), ((), ())), preferred_element_type=f32
    ).astype(kind)


def body(
    n_dp,
    n_s,
    tokens,
    cotangent,
    query_key,
    value_gate,
    output_weight,
    gate_up,
    down_weight,
    small_params,
    momentum_query_key,
    momentum_value_gate,
    momentum_output,
    momentum_gate_up,
    momentum_down,
    moment_one,
    moment_two,
    seq_lengths,
):
    local = tokens.shape[0]
    rows = local * n_s
    ff = gate_up.shape[2] // n_s
    packed = jnp.pad(small_params, (0, SMALL_ROWS * 128 - small_params.shape[0])).reshape(SMALL_ROWS, 128)
    (w_in, w_gu, w_out, w_dn, normed, dy, raw, raw_small, gated, mixed, updates, states, inverses, middle, normed_two,
     w_small, taps, vec, gain_o, gain_1, gain_2, info, segr) = fore(
        query_key, value_gate, gate_up, output_weight, down_weight, tokens, cotangent, packed, seq_lengths, n_dp, n_s, PASSES, 0
    )
    w_in = w_in.reshape(D, -1)
    w_gu = w_gu.reshape(D, -1)
    w_out = w_out.reshape(-1, D)
    w_dn = w_dn.reshape(-1, D)
    normed = normed.reshape(rows, D)
    dy = dy.reshape(rows, D)
    normed_two = normed_two.reshape(rows, D)
    gu = mm(normed_two, w_gu, 1, 0)
    gate = gu[:, :ff]
    upper = gu[:, ff:]
    sig = jax.nn.sigmoid(gate)
    hidden = (gate * sig * upper).astype(bf16)
    y_part = mm(hidden, w_dn, 1, 0, bf16).reshape(n_s, local, D)
    d_hidden = mm(dy, w_dn, 1, 1)
    d_gate = (d_hidden * upper * sig * (1.0 + gate * (1.0 - sig))).astype(bf16)
    d_upper = (d_hidden * (gate * sig)).astype(bf16)
    d_gu = jnp.concatenate([d_gate, d_upper], axis=1)
    d_part = mm(d_gu, w_gu, 1, 1, bf16).reshape(n_s, local, D)
    part_dn = mm(hidden, dy, 0, 0, bf16)
    momenta = [momentum_query_key, momentum_value_gate, momentum_output, momentum_gate_up, momentum_down]
    part_gu = mm(normed_two, d_gu, 0, 0, bf16)
    (g_gu, grad_dn, grad_out, g_gate, g_qkv, block_out, input_grad, small_sum, xwide, xtall) = back(
        part_gu.reshape(n_dp, -1, part_gu.shape[1]),
        part_dn.reshape(n_dp, -1, D),
        y_part,
        d_part,
        middle,
        cotangent,
        tokens,
        gain_2,
        gain_1,
        w_out,
        w_in,
        w_small,
        raw,
        raw_small,
        taps,
        vec,
        gain_o,
        info,
        segr,
        normed,
        gated,
        mixed,
        updates,
        states,
        inverses,
        momenta,
        n_dp,
        n_s,
        PASSES,
        2,
    )
    landed = [g_gu, grad_dn, grad_out, g_gate, g_qkv]
    masters = [query_key, value_gate, output_weight, gate_up, down_weight]
    *orthos, small_total = muon(landed, momenta, xwide, xtall, small_sum, n_dp, n_s, 5)
    big = finish(landed, momenta, masters, orthos, n_dp * n_s)
    small_grad = small_total.reshape(-1)[: small_params.shape[0]]
    new_one = BETA_ONE * moment_one + (1.0 - BETA_ONE) * small_grad
    new_two = BETA_TWO * moment_two + (1.0 - BETA_TWO) * small_grad * small_grad
    small_step = (
        -ADAM_RATE
        * (new_one / (1.0 - BETA_ONE**STEP_COUNT))
        / (jnp.sqrt(new_two / (1.0 - BETA_TWO**STEP_COUNT)) + ADAM_EPS)
    )

    return (block_out, input_grad) + tuple(big) + (small_grad, small_step, new_one, new_two)


def solution(mesh):
    cols = P(None, ("dp", "shard"), None)
    rows = P(("dp", "shard"), None)
    weights = (cols, cols, rows, cols, rows)
    return jax.shard_map(
        functools.partial(body, mesh.shape["dp"], mesh.shape["shard"]),
        mesh=mesh,
        in_specs=(rows, rows) + weights + (P(),) + weights + (P(), P(), P("dp", None)),
        out_specs=(rows, rows) + weights * 3 + (P(),) * 4,
        check_vma=False,
    )
```

```python
import functools
import math

import jax
import jax.numpy as jnp
from jax import lax
from jax.experimental import pallas as pl
from jax.experimental.pallas import tpu as pltpu
from jax.sharding import PartitionSpec as P

DK=128; DV=256; KCONV=4; CH=128
f32=jnp.float32; bf16=jnp.bfloat16
HI=lax.Precision.HIGHEST
GATE_EPS=1e-5; UNIT_EPS=1e-6

def _split(a):
    h=a.astype(bf16)
    return h,(a-h.astype(f32)).astype(bf16)

def dot(a,b,ca,cb,passes=3):
    dn=(((ca,),(cb,)),((),()))
    if passes==6:
        return lax.dot_general(a,b,dn,precision=HI,preferred_element_type=f32)
    if passes==1:
        return lax.dot_general(a.astype(bf16),b.astype(bf16),dn,preferred_element_type=f32)
    ah,al=_split(a); bh,bl=_split(b)
    g=functools.partial(lax.dot_general,dimension_numbers=dn,preferred_element_type=f32)
    return g(ah,bh)+(g(ah,bl)+g(al,bh))

def softplus(x): return jnp.maximum(x,0.0)+jnp.log1p(jnp.exp(-jnp.abs(x)))
def sigmoid(x): return lax.logistic(x)

def iota2(n,ax): return lax.broadcasted_iota(jnp.int32,(n,n),ax)

def inverse(A,p):
    n=A[0].shape[0]
    ri=iota2(n,0); ci=iota2(n,1)
    eye=(ri==ci).astype(f32)
    same=lambda b:(ri//b)==(ci//b)
    pw=[jnp.where(same(16),a,0.0) for a in A]
    X=[eye-q for q in pw]
    for _ in range(3):
        pw=[dot(q,q,1,0,p) for q in pw]
        X=[x+dot(x,q,1,0,p) for x,q in zip(X,pw)]
    b=16
    while b<n:
        m=jnp.logical_and(same(2*b),jnp.logical_not(same(b)))
        off=[jnp.where(m,a,0.0) for a in A]
        t=[dot(o,x,1,0,p) for o,x in zip(off,X)]
        X=[x-dot(x,q,1,0,p) for x,q in zip(X,t)]
        b*=2
    return X

def conv_pre(u,taps,info):
    s=taps[3:4]*u
    for k in (1,2,3):
        s=s+taps[3-k:4-k]*(pltpu.roll(u,k,0)*info[:,k:k+1])
    return s

def l2(u):
    return lax.rsqrt(jnp.sum(u*u,axis=-1,keepdims=True)+UNIT_EPS)

def acts(raw,taps,info,nh):
    out=[]
    kq=nh*DK
    for h in range(nh):
        d={}
        for nm,off,w in (("q",h*DK,DK),("k",kq+h*DK,DK),("v",2*kq+h*DV,DV)):
            pre=conv_pre(raw[:,off:off+w],taps[:,off:off+w],info)
            act=pre*sigmoid(pre)
            d[nm+"pre"]=pre; d[nm]=act
        rq=l2(d["q"])*(DK**-0.5); rk=l2(d["k"])
        d["rq"]=rq; d["rk"]=rk
        d["qn"]=d["q"]*rq; d["kn"]=d["k"]*rk
        out.append(d)
    return out

def decays(small,vec,nh):
    z=small+vec[1:2]
    ld=-vec[0:1]*softplus(z)
    beta=sigmoid(small)
    return z,ld,beta

def chunk_terms(ld,segc,segr,R,nh):
    n=CH
    ri=iota2(n,0); ci=iota2(n,1)
    low=(ri>=ci)
    L=low.astype(f32)
    out=[]
    for c in range(R//n):
        sl=slice(c*n,(c+1)*n)
        ldc=ld[sl]
        cc=dot(L,ldc,1,0,6)
        cr=dot(ldc,L,0,1,6)
        sc=segc[sl]; sr=segr[:,sl]
        M=jnp.logical_and(low,sc==sr)
        prev=segc[c*n-1:c*n] if c else None
        last=segc[(c+1)*n-1:(c+1)*n]
        heads=[]
        for h in range(nh):
            col=cc[:,h:h+1]; row=cr[h:h+1,:]
            R_=jnp.where(M,jnp.exp(jnp.where(M,col-row,0.0)),0.0)
            end=cc[n-1:n,h:h+1]
            t=jnp.where(sc==last,jnp.exp(end-col),0.0)
            if c:
                e=jnp.where(sc==prev,jnp.exp(col),0.0)
                g=jnp.where(last==prev,jnp.exp(end),0.0)
            else:
                e=jnp.zeros_like(col); g=jnp.zeros_like(end)
            heads.append((R_,e,t,g))
        out.append(heads)
    return out

def mixer_fwd(raw_ref,small_ref,taps_ref,vec_ref,gain_ref,info_ref,segr_ref,gated_ref,o_ref,u_ref,s_ref,x_ref,nh,P):
    R=raw_ref.shape[0]; nc=R//CH; n=CH
    info=info_ref[...]; gain=gain_ref[0:1]
    segc=info[:,0:1]
    a=acts(raw_ref,taps_ref[...],info,nh)
    z,ld,beta=decays(small_ref[...],vec_ref[...],nh)
    yield
    terms=chunk_terms(ld,segc,segr_ref[0:1],R,nh)
    ri=iota2(n,0); ci=iota2(n,1)
    strict=ri>ci
    idx=[(h,c) for c in range(nc) for h in range(nh)]
    sl=lambda c:slice(c*n,(c+1)*n)
    A=[];Pm=[]
    for h,c in idx:
        K=a[h]["kn"][sl(c)]; Q=a[h]["qn"][sl(c)]
        R_=terms[c][h][0]
        b=beta[sl(c),nh+h:nh+h+1]
        A.append(jnp.where(strict,b*R_*dot(K,K,1,1,P["kk"]),0.0))
        Pm.append(dot(Q,K,1,1,P["qk"])*R_)
    yield
    X=inverse(A,P["inv"])
    for i in range(len(idx)): x_ref[i]=X[i]
    yield
    U0=[];W=[]
    for i,(h,c) in enumerate(idx):
        b=beta[sl(c),nh+h:nh+h+1]; e=terms[c][h][1]
        U0.append(dot(X[i],b*a[h]["v"][sl(c)],1,0,P["u"]))
        W.append(dot(X[i],(b*e)*a[h]["kn"][sl(c)],1,0,P["u"]) if c else None)
    yield
    S=[None]*nh
    off=2*nh*DK+nh*DV
    for i,(h,c) in enumerate(idx):
        R_,e,t,g=terms[c][h]
        K=a[h]["kn"][sl(c)]; Q=a[h]["qn"][sl(c)]
        S0=S[h]
        U=U0[i] if c==0 else U0[i]-dot(W[i],S0,1,0,P["s"])
        o=dot(Pm[i],U,1,0,P["o"])
        if c: o=o+dot(e*Q,S0,1,0,P["o"])
        up=dot(t*K,U,0,0,P["s"])
        S[h]=up if c==0 else g*S0+up
        co=slice(h*DV,(h+1)*DV)
        s_ref[i]=S0 if c else jnp.zeros((DK,DV),f32)
        u_ref[sl(c),co]=U; o_ref[sl(c),co]=o
        r=lax.rsqrt(jnp.mean(o*o,axis=-1,keepdims=True)+GATE_EPS)
        gt=raw_ref[sl(c),off+h*DV:off+(h+1)*DV]
        gated_ref[sl(c),co]=(o*r*gain*(gt*sigmoid(gt))).astype(bf16)
        if h==nh-1 and c==1: yield

def gate_back(raw_ref,gain,dgated_ref,o_ref,nh,emit):
    R=raw_ref.shape[0]; nc=R//CH; n=CH
    off=2*nh*DK+nh*DV
    dO={};ggain=None
    for c in range(nc):
        for h in range(nh):
            r_=slice(c*n,(c+1)*n); co=slice(h*DV,(h+1)*DV)
            o=o_ref[r_,co]
            r=lax.rsqrt(jnp.mean(o*o,axis=-1,keepdims=True)+GATE_EPS)
            gt=raw_ref[r_,off+h*DV:off+(h+1)*DV]
            s=sigmoid(gt); sg=gt*s
            dg=dgated_ref[r_,co]
            nrm=o*r
            emit(h,c,dg*nrm*gain*(s*(1.0+gt*(1.0-s))))
            dsn=dg*sg
            part=jnp.sum(dsn*nrm,axis=0,keepdims=True)
            ggain=part if ggain is None else ggain+part
            dn=dsn*gain
            dO[h,c]=r*dn-nrm*(r*jnp.mean(nrm*dn,axis=-1,keepdims=True))
    return dO,ggain

def mixer_bwd(raw_ref,small_ref,taps_ref,vec_ref,info_ref,segr_ref,dO,u_ref,s_ref,x_ref,nh,P,result):
    R=raw_ref.shape[0]; nc=R//CH; n=CH
    raw=raw_ref; taps=taps_ref[...]; vec=vec_ref[...]; info=info_ref[...]
    segc=info[:,0:1]
    a=acts(raw,taps,info,nh)
    z,ld,beta=decays(small_ref[...],vec,nh)
    yield
    terms=chunk_terms(ld,segc,segr_ref[0:1],R,nh)
    ri=iota2(n,0); ci=iota2(n,1)
    strict=ri>ci
    U_=(ri<=ci).astype(f32)
    idx=[(h,c) for c in reversed(range(nc)) for h in range(nh)]
    sl=lambda c:slice(c*n,(c+1)*n)
    yield
    dU0={};KK={};QK={}
    for h,c in idx:
        K=a[h]["kn"][sl(c)]; Q=a[h]["qn"][sl(c)]
        KK[h,c]=dot(K,K,1,1,P["kk"]); QK[h,c]=dot(Q,K,1,1,P["qk"])
        dU0[h,c]=dot(QK[h,c]*terms[c][h][0],dO[h,c],0,0,P["u"])
    yield
    dS=[None]*nh
    dS1s={};Ys={}
    for c in reversed(range(nc)):
        for h in range(nh):
            R_,e,t,g=terms[c][h]
            K=a[h]["kn"][sl(c)]; Q=a[h]["qn"][sl(c)]
            b=beta[sl(c),nh+h:nh+h+1]
            dS1=dS[h]
            dS1s[h,c]=dS1
            dU=dU0[h,c]
            if dS1 is not None: dU=dU+dot(t*K,dS1,1,0,P["s"])
            Y=dot(x_ref[c*nh+h],dU,0,0,P["s"])
            Ys[h,c]=Y
            if c:
                d0=dot(e*Q,dO[h,c],0,0,P["s"])-dot((b*e)*K,Y,0,0,P["s"])
                dS[h]=d0 if dS1 is None else g*dS1+d0
        yield
    dQ={};dK={};dV={};dbeta={};dld={}
    for h,c in idx:
        R_,e,t,g=terms[c][h]
        K=a[h]["kn"][sl(c)]; Q=a[h]["qn"][sl(c)]; V=a[h]["v"][sl(c)]
        b=beta[sl(c),nh+h:nh+h+1]
        Y=Ys[h,c]; U=u_ref[sl(c),h*DV:(h+1)*DV]; dS1=dS1s[h,c]
        dA=jnp.where(strict,-dot(Y,U,1,1,P["g"]),0.0)
        dP=dot(dO[h,c],U,1,1,P["g"])
        H=dP*R_
        Gr=dA*R_
        G=b*Gr
        dq=dot(H,K,1,0,P["g"])
        dk=dot(G,K,1,0,P["g"])+dot(G,K,0,0,P["g"])+dot(H,Q,0,0,P["g"])
        dV[h,c]=b*Y
        db=jnp.sum(Y*V,axis=-1,keepdims=True)+jnp.sum(Gr*KK[h,c],axis=-1,keepdims=True)
        Z=H*QK[h,c]+G*KK[h,c]
        dc=jnp.sum(Z,axis=-1,keepdims=True)-jnp.sum(Z.T,axis=-1,keepdims=True)
        last=(lax.broadcasted_iota(jnp.int32,(n,1),0)==n-1).astype(f32)
        if c:
            S0=s_ref[c*nh+h]
            YS=dot(Y,S0,1,1,P["g"]); OS=dot(dO[h,c],S0,1,1,P["g"])
            dq=dq+e*OS
            dk=dk-(b*e)*YS
            ks=jnp.sum(YS*K,axis=-1,keepdims=True)
            qs=jnp.sum(OS*Q,axis=-1,keepdims=True)
            db=db-e*ks
            dc=dc+e*(qs-b*ks)
        if dS1 is not None:
            US=dot(U,dS1,1,1,P["g"])
            dk=dk+t*US
            tt=t*jnp.sum(US*K,axis=-1,keepdims=True)
            dc=dc-tt
            tot=jnp.sum(tt,axis=0,keepdims=True)
            if c:
                tot=tot+g*jnp.sum(jnp.sum(dS1*S0,axis=-1,keepdims=True),axis=0,keepdims=True)
            dc=dc+last*tot
        dQ[h,c]=dq; dK[h,c]=dk; dbeta[h,c]=db
        dld[h,c]=dc
        if h==nh-1: yield
    lane=lax.broadcasted_iota(jnp.int32,(n,128),1)
    dsm=[]
    for c in range(nc):
        acc_d=jnp.zeros((n,128),f32); acc_b=jnp.zeros((n,128),f32)
        for h in range(nh):
            acc_d=acc_d+jnp.where(lane==h,dld[h,c],0.0)
            acc_b=acc_b+jnp.where(lane==nh+h,dbeta[h,c],0.0)
        acc_d=dot(U_,acc_d,1,0,6)
        dsm.append((acc_d,acc_b))
    dldf=jnp.concatenate([x[0] for x in dsm],axis=0)
    dbf=jnp.concatenate([x[1] for x in dsm],axis=0)
    dz=-dldf*vec[0:1]*sigmoid(z)
    dsmall=dz+dbf*beta*(1.0-beta)
    g_dt=jnp.sum(dz,axis=0,keepdims=True)
    g_al=jnp.sum(dldf*ld,axis=0,keepdims=True)
    result.append((dsmall,g_dt,g_al))
    for nm in ("q","k","v"):
        for h in range(nh):
            d=a[h]
            w=DV if nm=="v" else DK
            coff={"q":h*DK,"k":nh*DK+h*DK,"v":2*nh*DK+h*DV}[nm]
            dy=jnp.concatenate([{"q":dQ,"k":dK,"v":dV}[nm][h,c] for c in range(nc)],axis=0)
            if nm!="v":
                y=d[nm+"n"]
                if nm=="q": y=y*(DK**0.5)
                dy=d["r"+nm]*(dy-y*jnp.sum(y*dy,axis=-1,keepdims=True))
            pre=d[nm+"pre"]; s=sigmoid(pre)
            dp=dy*(s*(1.0+pre*(1.0-s)))
            u=raw[:,coff:coff+w]; tp=taps[:,coff:coff+w]
            du=tp[3:4]*dp
            tg=[None]*4
            tg[3]=jnp.sum(dp*u,axis=0,keepdims=True)
            for k in (1,2,3):
                su=pltpu.roll(dp,dp.shape[0]-k,0)*info[:,3+k:4+k]
                du=du+tp[3-k:4-k]*su
                tg[3-k]=jnp.sum(su*u,axis=0,keepdims=True)
            result.append((coff,w,du,tg))
        yield


f32=jnp.float32; bf16=jnp.bfloat16
MESH=pl.DeviceIdType.MESH
ANY=pl.BlockSpec(memory_space=pl.ANY)
VM=pl.BlockSpec(memory_space=pltpu.VMEM)

def place():
    d=lax.axis_index("dp"); s=lax.axis_index("shard")
    return d,s,d//2,d%2

def greet(peers):
    bar=pltpu.get_barrier_semaphore()
    for p in peers:
        pl.semaphore_signal(bar,inc=1,device_id=p,device_id_type=MESH)
    pl.semaphore_wait(bar,len(peers))

def greet_all(n_dp,n_s):
    d,s,_,_=place()
    me=d*n_s+s
    bar=pltpu.get_barrier_semaphore()
    def one(q,_):
        @pl.when(q!=me)
        def _():
            pl.semaphore_signal(bar,inc=1,device_id=(q//n_s,q%n_s),device_id_type=MESH)
        return 0
    lax.fori_loop(0,n_dp*n_s,one,0)
    pl.semaphore_wait(bar,n_dp*n_s-1)

def remote(src,dst,ss,rs,dev):
    return pltpu.make_async_remote_copy(src_ref=src,dst_ref=dst,send_sem=ss,recv_sem=rs,device_id=dev,device_id_type=MESH)

NORM_EPS=1e-6
D_=pltpu.SemaphoreType.DMA
def ring(n_s):
    d,s,_,_=place()
    return [(d,(s+j)%n_s) for j in range(1,n_s)]

def push_parts(n_s,part,land,ss,rs):
    cs=[]
    for j,p in enumerate(ring(n_s)):
        c=remote(part.at[p[1]],land.at[j],ss.at[j],rs.at[j],p); c.start(); cs.append(c)
    return cs

def push_all(n_s,out,ss,rs):
    _,s,_,_=place()
    cs=[]
    for j,p in enumerate(ring(n_s)):
        c=remote(out.at[s],out.at[s],ss.at[j],rs.at[j],p); c.start(); cs.append(c)
    return cs

def add_up(n_s,part,land):
    _,s,_,_=place()
    t=part[s].astype(f32)
    for j in range(n_s-1): t=t+land[j].astype(f32)
    return t

def norm_back(u,g,dn):
    w=u.shape[-1]
    r=lax.rsqrt(jnp.mean(u*u,axis=-1,keepdims=True)+NORM_EPS)
    gd=g*dn
    du=r*gd-u*(r*r*r*(jnp.sum(u*gd,axis=-1,keepdims=True)/w))
    return du,jnp.sum(u*r*dn,axis=0,keepdims=True)


D = 1024
H = 8
ROW_CQ = 2 * D * H // 128
ROW_CK = ROW_CQ + KCONV * H * DK // 128
ROW_CV = ROW_CK + KCONV * H * DK // 128
ROW_G1 = ROW_CV + KCONV * H * DV // 128
ROW_G2 = ROW_G1 + D // 128
ROW_GO = ROW_G2 + D // 128
ROW_AL = ROW_GO + DV // 128
SMALL_ROWS = 288
SLICE = 16

def wide_row(ref,first,width):
    return jnp.concatenate([ref[first+i:first+i+1,:] for i in range(width//128)],axis=1)

def tap_rows(s,nh):
    out=[]
    for base,width,off in ((ROW_CQ,DK,0),(ROW_CK,DK,nh*DK),(ROW_CV,DV,2*nh*DK)):
        per=width//128
        for i in range(KCONV):
            for c in range(nh*per):
                out.append((base+i*H*per+s*nh*per+c,i,off+c*128))
    return out

def spread(n_d):
    per=128//H
    d=lax.broadcasted_iota(jnp.int32,(n_d,n_d//per),0); r=lax.broadcasted_iota(jnp.int32,(n_d,n_d//per),1)
    dd=lax.broadcasted_iota(jnp.int32,(n_d,128),0); l=lax.broadcasted_iota(jnp.int32,(n_d,128),1)
    return (d//per==r).astype(f32),(l//H==dd%per).astype(f32)

def pick(s,nh,first):
    l=lax.broadcasted_iota(jnp.int32,(128,128),0); j=lax.broadcasted_iota(jnp.int32,(128,128),1)-first
    return jnp.logical_and(jnp.logical_and(j>=0,j<nh),l%H==s*nh+j).astype(f32)

def unpack_small(packed,lens,s,nh,n_s,taps,vec,gain,gain1,gain2,w_sm,info,segr):
    taps[...]=jnp.zeros_like(taps)
    for row,i,off in tap_rows(s,nh): taps[i:i+1,off:off+128]=packed[pl.ds(row,1),:]
    lane=lax.broadcasted_iota(jnp.int32,(1,128),1)
    last=packed[ROW_AL:ROW_AL+1,:]
    vec[...]=jnp.zeros_like(vec)
    al=jnp.zeros((1,128),f32); dt=jnp.zeros((1,128),f32)
    for j in range(nh):
        al=al+jnp.where(lane==j,jnp.exp(jnp.sum(jnp.where(lane==s*nh+j,last,0.0),axis=1,keepdims=True)),0.0)
        dt=dt+jnp.where(lane==j,jnp.sum(jnp.where(lane==H+s*nh+j,last,0.0),axis=1,keepdims=True),0.0)
    vec[0:1]=al; vec[1:2]=dt
    gain[...]=jnp.broadcast_to(wide_row(packed,ROW_GO,gain.shape[1]),gain.shape)
    gain1[...]=jnp.broadcast_to(wide_row(packed,ROW_G1,gain1.shape[1]),gain1.shape)
    gain2[...]=jnp.broadcast_to(wide_row(packed,ROW_G2,gain2.shape[1]),gain2.shape)
    n_d=w_sm.shape[0]; per=n_d*H//128
    e1,mask=spread(n_d)
    t=jnp.zeros((n_d,128),f32)
    for k in range(2):
        a=dot(e1,packed[k*per:(k+1)*per,:],1,0,1)*mask
        t=t+dot(a,pick(s,nh,k*nh),1,0,1)
    w_sm[...]=t.astype(bf16)
    rows=info.shape[0]; count=lens.shape[1]
    lv=lens[...].astype(f32)
    ends=[];e=jnp.zeros((1,1),f32)
    for j in range(count):
        e=e+lv[:,j:j+1]; ends.append(e)
    def number(p):
        n=jnp.zeros_like(p)
        for e in ends: n=n+(p>=e).astype(f32)
        return jnp.where(p<0.0,-1.0,n)
    lanes=lax.broadcasted_iota(jnp.int32,(rows,128),1)
    pos=lax.broadcasted_iota(jnp.int32,(rows,128),0).astype(f32)
    shift=jnp.where(lanes<=3,-lanes,lanes-3).astype(f32)
    seg=number(pos)
    info[...]=jnp.where(lanes==0,seg,(number(pos+shift)==seg).astype(f32))
    segr[...]=number(lax.broadcasted_iota(jnp.int32,segr.shape,1).astype(f32))

def pack_small(sg,psm,taps,g_al,g_dt,gg,dg1,dg2,s,nh,n_s):
    sg[...]=jnp.zeros_like(sg)
    n_d=psm.shape[0]; per=n_d*H//128
    e1,mask=spread(n_d)
    for k in range(2):
        a=dot(psm,pick(s,nh,k*nh),1,1,6)*mask
        sg[k*per:(k+1)*per,:]=dot(e1,a,0,0,6)
    where={}
    for row,i,off in tap_rows(s,nh): where[i,off]=row
    for coff,w,_,tg in taps:
        for i in range(KCONV):
            for c in range(w//128):
                sg[pl.ds(where[i,coff+c*128],1),:]=tg[i][:,c*128:(c+1)*128]
    for first,v in ((ROW_G1,dg1),(ROW_G2,dg2),(ROW_GO,gg)):
        for i in range(v.shape[1]//128): sg[first+i:first+i+1,:]=v[:,i*128:(i+1)*128]
    lane=lax.broadcasted_iota(jnp.int32,(1,128),1)
    t=jnp.zeros((1,128),f32)
    for j in range(nh):
        t=t+jnp.where(lane==s*nh+j,g_al[:,j:j+1],0.0)+jnp.where(lane==H+s*nh+j,g_dt[:,j:j+1],0.0)
    sg[ROW_AL:ROW_AL+1,:]=t

def share_small(n_dp,n_s,sg,land,ss,rs):
    d,s,_,_=place()
    me=d*n_s+s
    def one(q,_):
        src=sg.at[pl.ds(pl.multiple_of(q*SLICE,SLICE),SLICE)]
        @pl.when(q==me)
        def _():
            pltpu.make_async_copy(src,land.at[me],rs.at[0]).start()
        @pl.when(q!=me)
        def _():
            remote(src,land.at[me],ss.at[0],rs.at[0],(q//n_s,q%n_s)).start()
        return 0
    lax.fori_loop(0,SMALL_ROWS//SLICE,one,0)

def shared_small(n_dp,n_s,sg,land,ss,rs):
    d,s,_,_=place()
    me=d*n_s+s
    n=SMALL_ROWS//SLICE
    @pl.when(me<n)
    def _():
        pltpu.make_async_copy(land,land,rs.at[0]).wait()
        part=sg.at[pl.ds(0,SLICE*(n-1))]
        pltpu.make_async_copy(part,part,ss.at[0]).wait()
    @pl.when(me>=n)
    def _():
        pltpu.make_async_copy(sg,sg,ss.at[0]).wait()

def spread_small(n_dp,n_s,land,total,part,ss,rs):
    d,s,_,_=place()
    me=d*n_s+s; nd=n_dp*n_s
    @pl.when(me<SMALL_ROWS//SLICE)
    def _():
        t=land[0]
        for q in range(1,nd): t=t+land[q]
        part[...]=t
        dst=total.at[pl.ds(pl.multiple_of(me*SLICE,SLICE),SLICE)]
        def one(q,_):
            @pl.when(q==me)
            def _():
                pltpu.make_async_copy(part,dst,rs.at[0]).start()
            @pl.when(q!=me)
            def _():
                remote(part,dst,ss.at[0],rs.at[0],(q//n_s,q%n_s)).start()
            return 0
        lax.fori_loop(0,nd,one,0)

def spread_done(n_dp,n_s,land,total,ss,rs):
    d,s,_,_=place()
    me=d*n_s+s; nd=n_dp*n_s
    @pl.when(me<SMALL_ROWS//SLICE)
    def _():
        sent=land.at[pl.ds(0,nd-1)]
        pltpu.make_async_copy(sent,sent,ss.at[0]).wait()
    pltpu.make_async_copy(total,total,rs.at[0]).wait()


f32=jnp.float32; bf16=jnp.bfloat16
CA,CB,CC=3.4445,-4.775,2.0315
NS_STEPS=2
PANEL=512
def dg(a,b,ca,cb): return lax.dot_general(a,b,(((ca,),(cb,)),((),())),preferred_element_type=f32)

def mirror(m,i,r,tm):
    for j in range(i+1,r//tm):
        m[j*tm:(j+1)*tm,i*tm:(i+1)*tm]=m[i*tm:(i+1)*tm,j*tm:(j+1)*tm].T

def newton_schulz(wide,tall,tmp,acc,g,p,is_tall,count,tm=256):
    r=g.shape[0]
    at=lambda c: pl.ds(pl.multiple_of(c*PANEL,PANEL),PANEL)
    def both(fw,ft):
        @pl.when(jnp.logical_not(is_tall))
        def _(): lax.fori_loop(0,count,fw,0)
        @pl.when(is_tall)
        def _(): lax.fori_loop(0,count,ft,0)
    tmp[...]=jnp.zeros_like(tmp)
    def sqw(c,_):
        def one(k,_):
            v=wide[pl.ds(pl.multiple_of(k*128,128),128),at(c)].astype(f32)
            tmp[0:1,0:PANEL]=tmp[0:1,0:PANEL]+jnp.sum(v*v,axis=0,keepdims=True)
            return 0
        return lax.fori_loop(0,r//128,one,0)
    def sqt(c,_):
        def one(k,_):
            v=tall[pl.ds(pl.multiple_of(c*PANEL+k*128,128),128),:].astype(f32)
            tmp[0:1,:]=tmp[0:1,:]+jnp.sum(v*v,axis=0,keepdims=True)
            return 0
        return lax.fori_loop(0,PANEL//128,one,0)
    both(sqw,sqt)
    inv=1.0/(jnp.sqrt(jnp.sum(tmp[0:1,:],axis=1,keepdims=True))+1e-7)
    def scw(c,_):
        def one(k,_):
            q=pl.ds(pl.multiple_of(k*128,128),128)
            wide[q,at(c)]=(wide[q,at(c)].astype(f32)*inv).astype(bf16)
            return 0
        return lax.fori_loop(0,r//128,one,0)
    def sct(c,_):
        def one(k,_):
            q=pl.ds(pl.multiple_of(c*PANEL+k*128,128),128)
            tall[q,:]=(tall[q,:].astype(f32)*inv).astype(bf16)
            return 0
        return lax.fori_loop(0,PANEL//128,one,0)
    both(scw,sct)
    def step(_,__):
        acc[...]=jnp.zeros_like(acc)
        def gw(c,_):
            for i in range(r//tm):
                ri=slice(i*tm,(i+1)*tm)
                acc[ri,i*tm:r]+=dg(wide[ri,at(c)],wide[i*tm:r,at(c)],1,1)
            return 0
        def gt(c,_):
            for i in range(r//tm):
                ri=slice(i*tm,(i+1)*tm)
                acc[ri,i*tm:r]+=dg(tall[at(c),ri],tall[at(c),i*tm:r],0,0)
            return 0
        both(gw,gt)
        for i in range(r//tm):
            ri=slice(i*tm,(i+1)*tm)
            g[ri,i*tm:r]=acc[ri,i*tm:r].astype(bf16)
            mirror(g,i,r,tm)
        for i in range(r//tm):
            ri=slice(i*tm,(i+1)*tm)
            p[ri,i*tm:r]=(CB*g[ri,i*tm:r].astype(f32)+CC*dg(g[ri,:],g[:,i*tm:r],1,0)).astype(bf16)
            mirror(p,i,r,tm)
        def nw(c,_):
            g[:,0:PANEL]=wide[:,at(c)]
            for i in range(r//PANEL):
                ri=slice(i*PANEL,(i+1)*PANEL)
                wide[ri,at(c)]=(CA*g[ri,0:PANEL].astype(f32)+dg(p[ri,:],g[:,0:PANEL],1,0)).astype(bf16)
            return 0
        def nt(c,_):
            v=tall[at(c),:]
            tall[at(c),:]=(CA*v.astype(f32)+dg(v,p[...],1,0)).astype(bf16)
            return 0
        both(nw,nt)
        return 0
    lax.fori_loop(0,NS_STEPS,step,0)


MOMENTUM = 0.95
MUON_RATE = 0.1
MUON_DECAY = 0.01

def muon_owner(i,n_dp):
    base=n_dp//2-2
    d,s=((2,0),(3,0),(1,2),(3,2),(2,2),(0,0),(1,0),(0,2))[i]
    return base+d,s

def grad_blocks(i,landed):
    gu,dn,out,gate,qkv=landed
    if i==4: return [(0,out[...].astype(f32))]
    if i==7: return [(0,dn[...].astype(f32))]
    n_s=gu.shape[0]
    if i in (5,6):
        ref,w=gu,gu.shape[2]//2; at=(i-5)*w
    elif i==3:
        ref,w,at=gate,gate.shape[2],0
    else:
        q=qkv.shape[2]//4
        ref,w,at=qkv,(q,q,2*q)[i],(0,q,2*q)[i]
    return [(t*w,ref[t,:,at:at+w].astype(f32)) for t in range(n_s)]

def member(i,refs):
    a,k=((0,0),(0,1),(1,0),(1,1),(2,None),(3,0),(3,1),(4,None))[i]
    return refs[a],k

def part_of(ref,k,col,w):
    return ref[:,col:col+w] if k is None else ref[k,:,col:col+w]

def store_part(ref,k,col,v):
    if k is None: ref[:,col:col+v.shape[1]]=v
    else: ref[k,:,col:col+v.shape[1]]=v

def kinds_of(momenta,nd):
    kinds=[]
    for i in range(8):
        r,c=member(i,momenta)[0].shape[-2:]
        tall=r*nd>c
        kinds.append((tall,-(-r//16)*16 if tall else r,c))
    return tuple(kinds)

def land_shapes(kinds,nd):
    r=min(min(k[1]*nd,k[2]) for k in kinds)
    up=lambda x: -(-x//PANEL)*PANEL
    return (r,up(max(k[2] for k in kinds if not k[0]))),(up(max(k[1]*nd for k in kinds if k[0])),r)

def make_look(i,look,landed,momenta):
    ref,k=member(i,momenta)
    rows=ref.shape[-2]
    if look.shape[0]>rows: look[rows:,:]=jnp.zeros((look.shape[0]-rows,look.shape[1]),bf16)
    for col,v in grad_blocks(i,landed):
        m=MOMENTUM*part_of(ref,k,col,v.shape[1])+v
        look[0:rows,col:col+v.shape[1]]=(v+MOMENTUM*m).astype(bf16)

def slot(kind,buf,q):
    t,rows,cols=kind
    ds=pl.ds(pl.multiple_of(q*rows,rows),rows)
    return buf.at[ds] if t else buf.at[ds,pl.ds(0,cols)]

def whole(kind,buf,nd):
    t,rows,cols=kind
    return buf.at[pl.ds(0,rows*nd)] if t else buf.at[:,pl.ds(0,cols)]

class Looks:
    def __init__(self,n_dp,n_s,kinds,look,landed,momenta,wide,tall,rin,sin):
        self.d,self.s,_,_=place()
        self.n_dp=n_dp; self.nd=n_dp*n_s; self.me=self.d*n_s+self.s
        self.kinds=kinds; self.look=look; self.landed=landed; self.momenta=momenta
        self.wide=wide; self.tall=tall; self.rin=rin; self.sin=sin
    def at(self,i):
        o=muon_owner(i,self.n_dp)
        return o,jnp.logical_and(self.d==o[0],self.s==o[1])
    def buf(self,i): return self.tall if self.kinds[i][0] else self.wide
    def look_of(self,i): make_look(i,self.look[i],self.landed,self.momenta)
    def push(self,i):
        o,there=self.at(i)
        dst=slot(self.kinds[i],self.buf(i),self.me)
        @pl.when(there)
        def _():
            pltpu.make_async_copy(self.look[i],dst,self.rin.at[0]).start()
        @pl.when(jnp.logical_not(there))
        def _():
            remote(self.look[i],dst,self.sin.at[i],self.rin.at[0],o).start()
    def arrived(self,i):
        full=whole(self.kinds[i],self.buf(i),self.nd)
        pltpu.make_async_copy(full,full,self.rin.at[0]).wait()
    def left(self,i):
        _,there=self.at(i)
        @pl.when(jnp.logical_not(there))
        def _():
            pltpu.make_async_copy(self.look[i],self.look[i],self.sin.at[i]).wait()

def muon_kernel(n_dp,n_s,kinds,*refs):
    n=len(kinds)
    landed=refs[:5]; momenta=refs[5:10]; sland=refs[10]; outs=refs[11:11+n]; stot=refs[11+n]
    look=refs[12+n:20+n]
    wide,tall,tmp,acc,g,p,spart,rin,sin,rout,sout,st,rt=refs[20+n:]
    nd=n_dp*n_s
    E=Looks(n_dp,n_s,kinds,look,landed,momenta,wide,tall,rin,sin)
    order=(7,5,6,4,2,3,0,1)
    for i in order: E.look_of(i)
    greet_all(n_dp,n_s)
    spread_small(n_dp,n_s,sland,stot,spart,st,rt)
    for i in order: E.push(i)
    count=jnp.int32(0); tall_here=jnp.int32(0); here=jnp.int32(0)
    for i in range(n):
        t,rows,cols=kinds[i]
        _,there=E.at(i)
        one=there.astype(jnp.int32)
        size=rows*nd if t else cols
        count=count+one*(-(-size//PANEL)); here=here+one
        if t: tall_here=tall_here+one
        pad=-size%PANEL
        @pl.when(there)
        def _():
            if pad:
                if t: tall[size:size+pad,:]=jnp.zeros((pad,tall.shape[1]),bf16)
                else: wide[:,size:size+pad]=jnp.zeros((wide.shape[0],pad),bf16)
            E.arrived(i)
    @pl.when(here>0)
    def _():
        newton_schulz(wide,tall,tmp,acc,g,p,tall_here>0,count)
    for i in range(n):
        t,rows,cols=kinds[i]
        _,there=E.at(i)
        @pl.when(there)
        def _():
            buf=E.buf(i)
            def send(k,_):
                q=((k+E.d)%n_dp)*n_s+(E.s+k//n_dp)%n_s
                src=slot(kinds[i],buf,q)
                @pl.when(q==E.me)
                def _():
                    pltpu.make_async_copy(src,outs[i],rout.at[i]).start()
                @pl.when(q!=E.me)
                def _():
                    remote(src,outs[i],sout.at[0],rout.at[i],(q//n_s,q%n_s)).start()
                return 0
            lax.fori_loop(0,nd,send,0)
            part=buf.at[pl.ds(0,rows*(nd-1))] if t else buf.at[pl.ds(0,rows*(nd-1)),pl.ds(0,cols)]
            pltpu.make_async_copy(part,part,sout.at[0]).wait()
    for i in order: E.left(i)
    spread_done(n_dp,n_s,sland,stot,st,rt)
    for i in range(n):
        pltpu.make_async_copy(outs[i],outs[i],rout.at[i]).wait()

def muon(landed,momenta,sland,n_dp,n_s,cid):
    nd=n_dp*n_s
    kinds=kinds_of(momenta,nd)
    xw,xt=land_shapes(kinds,nd); r=xw[0]
    V=pltpu.VMEM
    return pl.pallas_call(functools.partial(muon_kernel,n_dp,n_s,kinds),
        out_shape=[jax.ShapeDtypeStruct(k[1:],bf16) for k in kinds]+[jax.ShapeDtypeStruct((SMALL_ROWS,128),f32)],in_specs=[VM]*11,out_specs=[VM]*9,
        scratch_shapes=[V(k[1:],bf16) for k in kinds]+[V(xw,bf16),V(xt,bf16),V((8,r),f32),V((r,r),f32)]+[V((r,r),bf16)]*2+[V((SLICE,128),f32)]+[D_((1,)),D_((8,)),D_((8,)),D_((1,)),D_((1,)),D_((1,))],
        compiler_params=pltpu.CompilerParams(collective_id=cid,has_side_effects=True,vmem_limit_bytes=62<<20),name="muon")(*landed,*momenta,sland)

def finish_kernel(nd,*refs):
    landed=refs[:5]; momenta=refs[5:10]; masters=refs[10:15]; orthos=refs[15:23]
    grads=refs[23:28]; steps=refs[28:33]; moms=refs[33:38]
    for i in range(8):
        ms,k=member(i,masters)
        rows,cols=ms.shape[-2:]
        scale=0.2*math.sqrt(max(rows*nd,cols))
        for col,v in grad_blocks(i,landed):
            w=v.shape[1]
            store_part(member(i,grads)[0],k,col,v)
            store_part(member(i,moms)[0],k,col,MOMENTUM*part_of(member(i,momenta)[0],k,col,w)+v)
        o=orthos[i][0:rows,:].astype(f32)
        store_part(member(i,steps)[0],k,0,-MUON_RATE*(scale*o+MUON_DECAY*part_of(ms,k,0,cols)))

def finish(landed,momenta,masters,orthos,nd):
    out=[jax.ShapeDtypeStruct(m.shape,f32) for m in masters]
    return pl.pallas_call(functools.partial(finish_kernel,nd),out_shape=out*3,in_specs=[VM]*23,out_specs=[VM]*15,
        compiler_params=pltpu.CompilerParams(vmem_limit_bytes=60<<20),name="updates")(*landed,*momenta,*masters,*orthos)


class Cube:
    def __init__(self,n_dp):
        self.d,self.s,self.hi,self.lo=place()
        self.n=n_dp; self.bits=[1<<b for b in range(n_dp.bit_length()-1)]
        self.x=self.bits[-1]
    def block(self,e):
        h=self.hi
        for b in self.bits[:-1]:
            if e&b: h=h+b-2*b*((h//b)%2)
        x=1-self.lo if e&self.x else self.lo
        return h*2+x
    def dev(self,e): return (self.block(e),self.s)

class Reducer:
    def __init__(self,n_dp,n_s,pieces,sems,W):
        self.c=c=Cube(n_dp)
        self.n_s=n_s; self.p=pieces; self.W=W
        self.sx,self.rx,self.sf,self.rf,self.lsem=sems
        self.s=c.s
        me=c.s*n_dp+c.d
        self.td=me//n_s; self.ts=me%n_s
        self.moved=jnp.logical_or(self.td!=c.d,self.ts!=c.s)
        self.grp=ring(n_s)
        self.q=[]; self.ns=0; self.nh=0; self.late=[]; self.fc={}; self.hook=None
        for p in pieces:
            dims=p["dims"]; first=dims[0]
            rest=[e for e in range(n_dp) if not e&first]
            pos=lambda e,dims=dims: next((i for i,b in enumerate(dims) if e&b),len(dims))
            p["order"]=sorted(rest,key=lambda e:(pos(e),-bin(e).count("1"),-e))
            p["pos"]=pos
    def via(self,k,e): return self.p[k]["dims"][self.p[k]["pos"](e)]
    def msg(self,k,e):
        p=self.p[k]; dims=p["dims"]; b=self.via(k,e)
        src=p["g"].at[self.c.block(e)] if b==dims[0] else p["land"].at[(e|dims[0])-1]
        return remote(src,p["land"].at[e-1],self.sx.at[k,e-1],self.rx.at[k,e-1],self.c.dev(b))
    def add(self,k): self.q+=[(k,e) for e in self.p[k]["order"]]
    def total(self,k,e):
        p=self.p[k]; dims=p["dims"]
        t=p["g"][self.c.block(e)].astype(f32)
        for b in dims[:p["pos"](e)]:
            self.msg(k,e|b).wait()
            t=t+p["land"][(e|b)-1].astype(f32)
        return t
    def handle(self,k,e):
        p=self.p[k]
        if e:
            t=self.total(k,e)
            p["land"][(e|p["dims"][0])-1]=t.astype(bf16)
            self.msg(k,e).start()
        else:
            self.late.append([k,2,self.finish])
    def finish(self,k):
        p=self.p[k]
        t=self.total(k,0).astype(bf16)
        fin,out=p["fin"],p["out"]
        if p["col"]:
            rows=t.shape[0]//self.n_s
            fin[...]=t.reshape(self.n_s,rows,t.shape[1])
            c=pltpu.make_async_copy(fin.at[self.s],out.at[self.s],self.lsem.at[k]); c.start()
            self.fc[k]=[c]
            for j,q in enumerate(self.grp):
                c=remote(fin.at[q[1]],out.at[self.s],self.sf.at[k,j],self.rf.at[k,j],q); c.start(); self.fc[k].append(c)
        else:
            fin[...]=t
            @pl.when(self.moved)
            def _():
                remote(fin,out,self.sf.at[k,0],self.rf.at[k,0],(self.td,self.ts)).start()
            @pl.when(jnp.logical_not(self.moved))
            def _():
                pltpu.make_async_copy(fin,out,self.rf.at[k,0]).start()
        self.late.append([k,2,self.landed])
    def tick(self,times=1):
        for _ in range(times):
            if self.ns<len(self.q):
                k,e=self.q[self.ns]
                self.msg(k,e|self.p[k]["dims"][0]).start(); self.ns+=1
                if self.ns-self.nh>self.W:
                    self.handle(*self.q[self.nh]); self.nh+=1
            elif self.nh<self.ns:
                self.handle(*self.q[self.nh]); self.nh+=1
            for e in list(self.late):
                e[1]-=1
                if e[1]<0:
                    self.late.remove(e); e[2](e[0])
    def landed(self,k):
        p=self.p[k]
        if p["col"]:
            for c in self.fc[k]: c.wait()
        else:
            fin,out=p["fin"],p["out"]
            pltpu.make_async_copy(fin,out,self.rf.at[k,0]).wait()
            @pl.when(self.moved)
            def _():
                remote(fin,out,self.sf.at[k,0],self.rf.at[k,0],(self.td,self.ts)).wait_send()
        if self.hook: self.hook(k)
    def drain(self):
        while self.nh<len(self.q) or self.late: self.tick()

class Gatherer:
    def __init__(self,n_dp,n_s,ins,outs,ncol,sems,order):
        self.c=c=Cube(n_dp)
        self.n_dp=n_dp; self.n_s=n_s; self.ins=ins; self.outs=outs; self.ncol=ncol; self.order=order
        self.s0,self.r0,self.s1,self.r1,self.lsem=sems
        self.d=c.d; self.s=c.s
        me=c.d*n_s+c.s
        self.td=me%n_dp; self.ts=me//n_dp
        self.moved=jnp.logical_or(self.td!=c.d,self.ts!=c.s)
        self.grp=ring(n_s)
        self.col={}; self.done=set(); self.i=0
        self.depth=len(c.bits)
    def phase0(self,k):
        src,dst=self.ins[k],self.outs[k]
        if k<self.ncol:
            c=pltpu.make_async_copy(src.at[self.s],dst.at[self.d,self.s],self.lsem.at[k]); c.start()
            self.col[k]=[c]
            for j,p in enumerate(self.grp):
                c=remote(src.at[p[1]],dst.at[self.d,self.s],self.s0.at[k,j],self.r0.at[k,j],p); c.start(); self.col[k].append(c)
        else:
            @pl.when(self.moved)
            def _():
                remote(src,dst.at[self.td],self.s0.at[k,0],self.r0.at[k,0],(self.td,self.ts)).start()
            @pl.when(jnp.logical_not(self.moved))
            def _():
                pltpu.make_async_copy(src,dst.at[self.d],self.r0.at[k,0]).start()
    def ready(self,k):
        if k in self.done: return
        self.done.add(k)
        if k<self.ncol:
            for c in self.col[k]: c.wait()
        else:
            src,dst=self.ins[k],self.outs[k]
            pltpu.make_async_copy(src,dst.at[self.d],self.r0.at[k,0]).wait()
            @pl.when(self.moved)
            def _():
                remote(src,dst.at[self.td],self.s0.at[k,0],self.r0.at[k,0],(self.td,self.ts)).wait_send()
    def blk(self,i,e):
        k,a,m,_=self.order[i]
        src=self.c.block(e)
        return self.outs[k].at[src,a:a+m] if m else self.outs[k].at[src]
    def last(self,i,e): return max((j for j,b in enumerate(self.order[i][3]) if e&b),default=-1)
    def msg(self,i,e):
        b=self.order[i][3][self.last(i,e)]
        blk=self.blk(i,e^b)
        return remote(blk,blk,self.s1.at[i,e-1],self.r1.at[i,e-1],self.c.dev(b))
    def pass_on(self,i,e):
        for b in self.order[i][3][self.last(i,e)+1:]: self.msg(i,e|b).start()
    def stage(self,i,depth):
        es=[e for e in range(1,self.n_dp) if bin(e).count("1")==depth]
        for e in sorted(es,key=lambda e:self.last(i,e)):
            self.msg(i,e).wait()
            self.pass_on(i,e)
    def tick(self,times=1):
        n=len(self.order)
        for _ in range(times):
            i=self.i; self.i+=1
            if i<n:
                self.ready(self.order[i][0])
                self.pass_on(i,0)
            for dep in range(1,self.depth+1):
                if 0<=i-dep<n: self.stage(i-dep,dep)
    def after(self,i):
        while self.i<i+self.depth+1: self.tick()
    def drain(self):
        self.after(len(self.order)-1)


def dotb(a,b,ca,cb): return lax.dot_general(a,b,(((ca,),(cb,)),((),())),preferred_element_type=f32)

def fore_kernel(n_dp,n_s,nh,P,order,last_in,last_out,*refs):
    (qk,vg,gu,ow,dw,x_ref,dyown,packed,lens,
     g_in,g_out,normed,raw,small,gated,o_ref,u_ref,s_ref,xi_ref,middle,w_sm,taps,vec,gain,gain1,gain2,info,segr,ypart,dpart,dland,part_gu,part_dn,
     c_in,c_gu,c_out,c_dn,part,land,g_gu,g_dn,dy,gath,hid,dgu)=refs[:45]
    sems=refs[45:50]; ss,rs=refs[50:52]
    E=Gatherer(n_dp,n_s,[c_in,c_gu,c_out,c_dn],[g_in,g_gu,g_out,g_dn],2,sems,order)
    s=E.s
    kq=nh*DK; kv=nh*DV; ff=c_gu.shape[2]//2
    for t in range(n_s):
        c_in[t,:,0:kq]=qk[0,:,t*kq:(t+1)*kq].astype(bf16)
        c_in[t,:,kq:2*kq]=qk[1,:,t*kq:(t+1)*kq].astype(bf16)
        c_in[t,:,2*kq:2*kq+kv]=vg[0,:,t*kv:(t+1)*kv].astype(bf16)
        c_in[t,:,2*kq+kv:]=vg[1,:,t*kv:(t+1)*kv].astype(bf16)
    greet_all(n_dp,n_s)
    E.phase0(0)
    g1=wide_row(packed,ROW_G1,gain1.shape[1])
    xv=x_ref[...].astype(f32)
    normed[s]=(xv*lax.rsqrt(jnp.mean(xv*xv,axis=-1,keepdims=True)+NORM_EPS)*g1).astype(bf16)
    c_out[...]=ow[...].astype(bf16)
    E.phase0(2)
    a=push_all(n_s,normed,ss.at[0],rs.at[0])
    E.tick(1)
    for t in range(n_s):
        c_gu[t,:,0:ff]=gu[0,:,t*ff:(t+1)*ff].astype(bf16)
        c_gu[t,:,ff:]=gu[1,:,t*ff:(t+1)*ff].astype(bf16)
    c_dn[...]=dw[...].astype(bf16)
    E.phase0(1); E.phase0(3)
    unpack_small(packed,lens,s,nh,n_s,taps,vec,gain,gain1,gain2,w_sm,info,segr)
    E.tick(1)
    dy[s]=dyown[...]
    b=push_all(n_s,dy,ss.at[1],rs.at[1])
    for c in a: c.wait()
    local,D=x_ref.shape; rows=local*n_s
    nrm=normed[...].reshape(rows,D)
    small[...]=dotb(nrm,w_sm[...],1,0)
    E.after(last_in)
    raw[...]=dotb(nrm,g_in[...].reshape(D,raw.shape[1]),1,0)
    E.tick()
    for i,_ in enumerate(mixer_fwd(raw,small,taps,vec,gain,info,segr,gated,o_ref,u_ref,s_ref,xi_ref,nh,P)):
        if i%2==0: E.tick()
    E.after(last_out)
    part[...]=dotb(gated[...],g_out[...].reshape(nh*DV,D),1,0).astype(bf16).reshape(part.shape)
    c1=push_parts(n_s,part,land,ss.at[2],rs.at[2])
    E.tick()
    for c in c1: c.wait()
    m=x_ref[...].astype(f32)+add_up(n_s,part,land)
    middle[...]=m
    r=lax.rsqrt(jnp.mean(m*m,axis=-1,keepdims=True)+NORM_EPS)
    gath[s]=(m*r*gain2[0:1]).astype(bf16)
    c2=push_all(n_s,gath,ss.at[3],rs.at[3])
    E.drain()
    for c in c2: c.wait()
    for c in b: c.wait()
    n2=gath[...].reshape(rows,D)
    w_gu=g_gu[...].reshape(D,2*ff)
    gup=dotb(n2,w_gu,1,0)
    gt=gup[:,:ff]; up=gup[:,ff:]
    sg=sigmoid(gt)
    hid[...]=(gt*sg*up).astype(bf16)
    dyv=dy[...].reshape(rows,D)
    w_dn=g_dn[...].reshape(ff,D)
    dh=dotb(dyv,w_dn,1,1)
    dgu[:,:ff]=(dh*up*sg*(1.0+gt*(1.0-sg))).astype(bf16)
    dgu[:,ff:]=(dh*(gt*sg)).astype(bf16)
    dpart[...]=dotb(dgu[...],w_gu,1,1).astype(bf16).reshape(dpart.shape)
    c3=push_parts(n_s,dpart,dland,ss.at[4],rs.at[4])
    part_dn[...]=dotb(hid[...],dyv,0,0).astype(bf16).reshape(part_dn.shape)
    part_gu[...]=dotb(n2,dgu[...],0,0).astype(bf16).reshape(part_gu.shape)
    ypart[...]=dotb(hid[...],w_dn,1,0).astype(bf16).reshape(ypart.shape)
    for c in c3: c.wait()

def fore(qk,vg,gu,ow,dw,x,dyown,packed,lens,n_dp,n_s,P,cid):
    ins=[qk,vg,gu,ow,dw,x,dyown,packed,lens]
    local,D=x.shape; rows=local*n_s; n_hi=n_dp//2
    nh=H//n_s; wid=nh*(2*DK+2*DV); nb=nh*rows//CH
    z=[1<<b for b in range(n_hi.bit_length()-1)]; xb=n_hi
    main=tuple(z[::-1]+[xb]); other=tuple(z[:0:-1]+[xb,z[0]])
    order=tuple([(0,i,1,main if i<n_s-1 else other) for i in range(n_s)]+[(2,0,0,main)]+[(1,i,1,main if i<n_s-1 else other) for i in range(n_s)]+[(3,0,0,main)])
    S_=jax.ShapeDtypeStruct; V=pltpu.VMEM
    ps=[(n_s,qk.shape[1],wid),(n_s,gu.shape[1],2*gu.shape[2]//n_s),ow.shape,dw.shape]
    outs=[S_((n_dp,)+q,bf16) for q in (ps[0],ps[2])]+[S_((n_s,local,D),bf16)]+[S_((rows,wid),f32),S_((rows,128),f32),S_((rows,nh*DV),bf16),S_((rows,nh*DV),f32),S_((rows,nh*DV),f32),
          S_((nb,DK,DV),f32),S_((nb,CH,CH),f32),S_((local,D),f32)]
    outs+=[S_((D,128),bf16),S_((8,nh*(2*DK+DV)),f32),S_((8,128),f32),S_((8,DV),f32),S_((8,D),f32),S_((8,D),f32),S_((rows,128),f32),S_((8,rows),f32)]
    outs+=[S_((n_s,local,D),bf16)]*2+[S_((n_s-1,local,D),bf16),S_((n_dp,D//n_dp,ps[1][2]),bf16),S_((n_dp,)+dw.shape,bf16)]
    sc=[V(q,bf16) for q in ps]+[V((n_s,local,D),bf16),V((n_s-1,local,D),bf16)]+[V((n_dp,)+ps[1],bf16),V((n_dp,)+ps[3],bf16)]+[V((n_s,local,D),bf16)]*2+[V((rows,ps[1][2]//2),bf16),V((rows,ps[1][2]),bf16)]
    sc+=[D_((4,n_s))]*2+[D_((len(order),n_dp))]*2+[D_((4,))]+[D_((5,n_s))]*2
    return pl.pallas_call(functools.partial(fore_kernel,n_dp,n_s,nh,P,order,n_s-1,n_s),
        out_shape=outs,in_specs=[VM]*len(ins),out_specs=[VM]*len(outs),scratch_shapes=sc,
        compiler_params=pltpu.CompilerParams(collective_id=cid,has_side_effects=True,vmem_limit_bytes=63<<20),name="forward")(*ins)


OTHER=(1,)

def back_kernel(n_dp,n_s,nh,P,W,*refs):
    (gu_ref,dn_ref,ypart,dpart,dland0,middle,dy,x_ref,gain2,gain1,w_out,w_in,w_sm,raw,small,taps,vec,gain,info,segr,normed,gated,o_ref,u_ref,s_ref,xi_ref,
     out_gu,out_dn,out_out,out_g,out_q,bout,igrad,stot,
     yland,dland,gath,dgt,draw,dsb,epart,dmid,
     p_out,p_g,p_q,sg)=refs[:46]
    rest=refs[46:]
    land=rest[0:5]; fin=rest[5:10]
    sems=rest[10:15]; ss,rs,st,rt=rest[15:19]
    gs=(gu_ref,dn_ref,p_out,p_g,p_q); outs=(out_gu,out_dn,out_out,out_g,out_q)
    z=[1<<b for b in range((n_dp//2).bit_length()-1)]; xb=n_dp//2
    main=[xb]+z; other=z[:1]+[xb]+z[1:]
    pieces=[dict(g=gs[k],land=land[k],fin=fin[k],out=outs[k],col=k in (0,3,4),dims=other if k in OTHER else main) for k in range(5)]
    E=Reducer(n_dp,n_s,pieces,sems,W)
    s=E.s
    greet_all(n_dp,n_s)
    E.add(1); E.add(0)
    E.tick(2)
    m=middle[...]
    du,dg=norm_back(m,gain2[0:1],add_up(n_s,dpart,dland0))
    dm=dy[...].astype(f32)+du
    dmid[...]=dm
    dg2=dg
    gath[s]=dm.astype(bf16)
    g=push_all(n_s,gath,ss.at[1],rs.at[1])
    E.tick(W)
    for c in g: c.wait()
    a=push_parts(n_s,ypart,yland,ss.at[2],rs.at[2])
    rows=raw.shape[0]; D=gath.shape[2]
    dbr=gath[...].reshape(rows,D)
    dgt[...]=dotb(dbr,w_out[...],1,1)
    E.tick(1)
    p_out[...]=dotb(gated[...],dbr,0,0).astype(bf16).reshape(p_out.shape)
    E.add(2)
    n=CH; off=2*nh*DK+nh*DV
    def emit(h,c,v): draw[c*n:(c+1)*n,off+h*DV:off+(h+1)*DV]=v.astype(bf16)
    dO,gg=gate_back(raw,gain[0:1],dgt,o_ref,nh,emit)
    E.tick(1)
    p_g[...]=dotb(normed[...],draw[:,off:],0,0).astype(bf16).reshape(p_g.shape)
    E.add(3)
    res=[]
    for _ in mixer_bwd(raw,small,taps,vec,info,segr,dO,u_ref,s_ref,xi_ref,nh,P,res):
        E.tick(1)
    dsmall,g_dt,g_al=res[0]
    for coff,w,dcol,tg in res[1:]:
        draw[:,coff:coff+w]=dcol.astype(bf16)
    dsb[...]=dsmall.astype(bf16)
    p_q[...]=dotb(normed[...],draw[:,:off],0,0).astype(bf16).reshape(p_q.shape)
    E.add(4)
    E.tick(4)
    epart[...]=(dotb(draw[...],w_in[...],1,1)+dotb(dsb[...],w_sm[...],1,1)).astype(bf16).reshape(epart.shape)
    e=push_parts(n_s,epart,dland,ss.at[3],rs.at[3])
    for c in a: c.wait()
    bout[...]=(middle[...]+add_up(n_s,ypart,yland)).astype(bf16)
    psm=dotb(normed[...],dsb[...],0,0)
    E.tick(2)
    for c in e: c.wait()
    du,dg=norm_back(x_ref[...].astype(f32),gain1[0:1],add_up(n_s,epart,dland))
    igrad[...]=(dmid[...]+du).astype(bf16)
    pack_small(sg,psm,res[1:],g_al,g_dt,gg,dg,dg2,s,nh,n_s)
    share_small(n_dp,n_s,sg,stot,st,rt)
    E.drain()
    shared_small(n_dp,n_s,sg,stot,st,rt)

def back(part_gu,part_dn,ypart,dpart,dland,middle,dy,x,gain2,gain1,w_out,w_in,w_sm,raw,small,taps,vec,gain,info,segr,normed,gated,O,U,S,X,n_dp,n_s,P,cid,W=4):
    ins=[part_gu,part_dn,ypart,dpart,dland,middle,dy,x,gain2,gain1,w_out,w_in,w_sm,raw,small,taps,vec,gain,info,segr,normed,gated,O,U,S,X]
    local,D=x.shape; rows=local*n_s; nh=raw.shape[1]//(2*DK+2*DV); n_hi=n_dp//2
    off=2*nh*DK+nh*DV
    shp=[part_gu.shape,part_dn.shape,(n_dp,w_out.shape[0]//n_dp,D),(n_dp,D//n_dp,nh*DV),(n_dp,D//n_dp,off)]
    col=(0,3,4)
    osh=[(n_s,q[1]//n_s,q[2]) if k in col else q[1:] for k,q in enumerate(shp)]
    S_=jax.ShapeDtypeStruct; V=pltpu.VMEM
    outs=[S_(q,bf16) for q in osh]+[S_((local,D),bf16),S_((local,D),bf16),S_((n_dp*n_s,SLICE,128),f32)]
    sc=[V((n_s-1,local,D),bf16)]*2+[V((n_s,local,D),bf16),V((rows,nh*DV),f32),V((rows,raw.shape[1]),bf16),V((rows,128),bf16),V((n_s,local,D),bf16),V((local,D),f32)]
    sc+=[V(shp[k],bf16) for k in (2,3,4)]+[V((SMALL_ROWS,128),f32)]
    sc+=[V((n_dp-1,)+q[1:],bf16) for q in shp]+[V(q,bf16) for q in osh]
    sc+=[D_((5,n_dp))]*2+[D_((5,n_s))]*2+[D_((5,))]+[D_((4,n_s))]*2+[D_((1,))]*2
    return pl.pallas_call(functools.partial(back_kernel,n_dp,n_s,nh,P,W),
        out_shape=outs,in_specs=[VM]*len(ins),out_specs=[VM]*len(outs),scratch_shapes=sc,
        compiler_params=pltpu.CompilerParams(collective_id=cid,has_side_effects=True,vmem_limit_bytes=63<<20),name="backward")(*ins)


STEP_COUNT = 10
ADAM_RATE = 0.05
BETA_ONE = 0.9
BETA_TWO = 0.95
ADAM_EPS = 1e-08
PASSES = dict(kk=3, qk=3, inv=3, u=3, s=3, o=3, g=3)


def body(
    n_dp,
    n_s,
    tokens,
    cotangent,
    query_key,
    value_gate,
    output_weight,
    gate_up,
    down_weight,
    small_params,
    momentum_query_key,
    momentum_value_gate,
    momentum_output,
    momentum_gate_up,
    momentum_down,
    moment_one,
    moment_two,
    seq_lengths,
):
    local = tokens.shape[0]
    rows = local * n_s
    packed = jnp.pad(small_params, (0, SMALL_ROWS * 128 - small_params.shape[0])).reshape(SMALL_ROWS, 128)
    (w_in, w_out, normed, raw, raw_small, gated, mixed, updates, states, inverses, middle,
     w_small, taps, vec, gain_o, gain_1, gain_2, info, segr, y_part, d_part, d_land, part_gu, part_dn) = fore(
        query_key, value_gate, gate_up, output_weight, down_weight, tokens, cotangent, packed, seq_lengths, n_dp, n_s, PASSES, 0
    )
    w_in = w_in.reshape(D, -1)
    w_out = w_out.reshape(-1, D)
    normed = normed.reshape(rows, D)
    momenta = [momentum_query_key, momentum_value_gate, momentum_output, momentum_gate_up, momentum_down]
    (g_gu, grad_dn, grad_out, g_gate, g_qkv, block_out, input_grad, small_sum) = back(
        part_gu,
        part_dn,
        y_part,
        d_part,
        d_land,
        middle,
        cotangent,
        tokens,
        gain_2,
        gain_1,
        w_out,
        w_in,
        w_small,
        raw,
        raw_small,
        taps,
        vec,
        gain_o,
        info,
        segr,
        normed,
        gated,
        mixed,
        updates,
        states,
        inverses,
        n_dp,
        n_s,
        PASSES,
        2,
    )
    landed = [g_gu, grad_dn, grad_out, g_gate, g_qkv]
    masters = [query_key, value_gate, output_weight, gate_up, down_weight]
    *orthos, small_total = muon(landed, momenta, small_sum, n_dp, n_s, 5)
    big = finish(landed, momenta, masters, orthos, n_dp * n_s)
    small_grad = small_total.reshape(-1)[: small_params.shape[0]]
    new_one = BETA_ONE * moment_one + (1.0 - BETA_ONE) * small_grad
    new_two = BETA_TWO * moment_two + (1.0 - BETA_TWO) * small_grad * small_grad
    small_step = (
        -ADAM_RATE
        * (new_one / (1.0 - BETA_ONE**STEP_COUNT))
        / (jnp.sqrt(new_two / (1.0 - BETA_TWO**STEP_COUNT)) + ADAM_EPS)
    )

    return (block_out, input_grad) + tuple(big) + (small_grad, small_step, new_one, new_two)


def solution(mesh):
    cols = P(None, ("dp", "shard"), None)
    rows = P(("dp", "shard"), None)
    weights = (cols, cols, rows, cols, rows)
    return jax.shard_map(
        functools.partial(body, mesh.shape["dp"], mesh.shape["shard"]),
        mesh=mesh,
        in_specs=(rows, rows) + weights + (P(),) + weights + (P(), P(), P("dp", None)),
        out_specs=(rows, rows) + weights * 3 + (P(),) * 4,
        check_vma=False,
    )
```

```python
import functools
import math

import jax
import jax.numpy as jnp
from jax import lax
from jax.experimental import pallas as pl
from jax.experimental.pallas import tpu as pltpu
from jax.sharding import PartitionSpec as P

DK=128; DV=256; KCONV=4; CH=128
f32=jnp.float32; bf16=jnp.bfloat16
HI=lax.Precision.HIGHEST
GATE_EPS=1e-5; UNIT_EPS=1e-6

def _split(a):
    h=a.astype(bf16)
    return h,(a-h.astype(f32)).astype(bf16)

def dot(a,b,ca,cb,passes=3):
    dn=(((ca,),(cb,)),((),()))
    if passes==6:
        return lax.dot_general(a,b,dn,precision=HI,preferred_element_type=f32)
    if passes==1:
        return lax.dot_general(a.astype(bf16),b.astype(bf16),dn,preferred_element_type=f32)
    ah,al=_split(a); bh,bl=_split(b)
    g=functools.partial(lax.dot_general,dimension_numbers=dn,preferred_element_type=f32)
    return g(ah,bh)+(g(ah,bl)+g(al,bh))

def softplus(x): return jnp.maximum(x,0.0)+jnp.log1p(jnp.exp(-jnp.abs(x)))
def sigmoid(x): return lax.logistic(x)

def iota2(n,ax): return lax.broadcasted_iota(jnp.int32,(n,n),ax)

def inverse(A,p):
    n=A[0].shape[0]
    ri=iota2(n,0); ci=iota2(n,1)
    eye=(ri==ci).astype(f32)
    same=lambda b:(ri//b)==(ci//b)
    pw=[jnp.where(same(16),a,0.0) for a in A]
    X=[eye-q for q in pw]
    for _ in range(3):
        pw=[dot(q,q,1,0,p) for q in pw]
        X=[x+dot(x,q,1,0,p) for x,q in zip(X,pw)]
    b=16
    while b<n:
        m=jnp.logical_and(same(2*b),jnp.logical_not(same(b)))
        off=[jnp.where(m,a,0.0) for a in A]
        t=[dot(o,x,1,0,p) for o,x in zip(off,X)]
        X=[x-dot(x,q,1,0,p) for x,q in zip(X,t)]
        b*=2
    return X

def conv_pre(u,taps,info):
    s=taps[3:4]*u
    for k in (1,2,3):
        s=s+taps[3-k:4-k]*(pltpu.roll(u,k,0)*info[:,k:k+1])
    return s

def l2(u):
    return lax.rsqrt(jnp.sum(u*u,axis=-1,keepdims=True)+UNIT_EPS)

def acts(raw,taps,info,nh):
    out=[]
    kq=nh*DK
    for h in range(nh):
        d={}
        for nm,off,w in (("q",h*DK,DK),("k",kq+h*DK,DK),("v",2*kq+h*DV,DV)):
            pre=conv_pre(raw[:,off:off+w],taps[:,off:off+w],info)
            act=pre*sigmoid(pre)
            d[nm+"pre"]=pre; d[nm]=act
        rq=l2(d["q"])*(DK**-0.5); rk=l2(d["k"])
        d["rq"]=rq; d["rk"]=rk
        d["qn"]=d["q"]*rq; d["kn"]=d["k"]*rk
        out.append(d)
    return out

def decays(small,vec,nh):
    z=small+vec[1:2]
    ld=-vec[0:1]*softplus(z)
    beta=sigmoid(small)
    return z,ld,beta

def chunk_terms(ld,segc,segr,R,nh):
    n=CH
    ri=iota2(n,0); ci=iota2(n,1)
    low=(ri>=ci)
    L=low.astype(f32)
    out=[]
    for c in range(R//n):
        sl=slice(c*n,(c+1)*n)
        ldc=ld[sl]
        cc=dot(L,ldc,1,0,6)
        cr=dot(ldc,L,0,1,6)
        sc=segc[sl]; sr=segr[:,sl]
        M=jnp.logical_and(low,sc==sr)
        prev=segc[c*n-1:c*n] if c else None
        last=segc[(c+1)*n-1:(c+1)*n]
        heads=[]
        for h in range(nh):
            col=cc[:,h:h+1]; row=cr[h:h+1,:]
            R_=jnp.where(M,jnp.exp(jnp.where(M,col-row,0.0)),0.0)
            end=cc[n-1:n,h:h+1]
            t=jnp.where(sc==last,jnp.exp(end-col),0.0)
            if c:
                e=jnp.where(sc==prev,jnp.exp(col),0.0)
                g=jnp.where(last==prev,jnp.exp(end),0.0)
            else:
                e=jnp.zeros_like(col); g=jnp.zeros_like(end)
            heads.append((R_,e,t,g))
        out.append(heads)
    return out

def mixer_fwd(raw_ref,small_ref,taps_ref,vec_ref,gain_ref,info_ref,segr_ref,gated_ref,o_ref,u_ref,s_ref,x_ref,nh,P):
    R=raw_ref.shape[0]; nc=R//CH; n=CH
    info=info_ref[...]; gain=gain_ref[0:1]
    segc=info[:,0:1]
    a=acts(raw_ref,taps_ref[...],info,nh)
    z,ld,beta=decays(small_ref[...],vec_ref[...],nh)
    yield
    terms=chunk_terms(ld,segc,segr_ref[0:1],R,nh)
    ri=iota2(n,0); ci=iota2(n,1)
    strict=ri>ci
    idx=[(h,c) for c in range(nc) for h in range(nh)]
    sl=lambda c:slice(c*n,(c+1)*n)
    A=[];Pm=[]
    for h,c in idx:
        K=a[h]["kn"][sl(c)]; Q=a[h]["qn"][sl(c)]
        R_=terms[c][h][0]
        b=beta[sl(c),nh+h:nh+h+1]
        A.append(jnp.where(strict,b*R_*dot(K,K,1,1,P["kk"]),0.0))
        Pm.append(dot(Q,K,1,1,P["qk"])*R_)
    yield
    X=inverse(A,P["inv"])
    for i in range(len(idx)): x_ref[i]=X[i]
    yield
    U0=[];W=[]
    for i,(h,c) in enumerate(idx):
        b=beta[sl(c),nh+h:nh+h+1]; e=terms[c][h][1]
        U0.append(dot(X[i],b*a[h]["v"][sl(c)],1,0,P["u"]))
        W.append(dot(X[i],(b*e)*a[h]["kn"][sl(c)],1,0,P["u"]) if c else None)
    yield
    S=[None]*nh
    off=2*nh*DK+nh*DV
    for i,(h,c) in enumerate(idx):
        R_,e,t,g=terms[c][h]
        K=a[h]["kn"][sl(c)]; Q=a[h]["qn"][sl(c)]
        S0=S[h]
        U=U0[i] if c==0 else U0[i]-dot(W[i],S0,1,0,P["s"])
        o=dot(Pm[i],U,1,0,P["o"])
        if c: o=o+dot(e*Q,S0,1,0,P["o"])
        up=dot(t*K,U,0,0,P["s"])
        S[h]=up if c==0 else g*S0+up
        co=slice(h*DV,(h+1)*DV)
        s_ref[i]=S0 if c else jnp.zeros((DK,DV),f32)
        u_ref[sl(c),co]=U; o_ref[sl(c),co]=o
        r=lax.rsqrt(jnp.mean(o*o,axis=-1,keepdims=True)+GATE_EPS)
        gt=raw_ref[sl(c),off+h*DV:off+(h+1)*DV]
        gated_ref[sl(c),co]=(o*r*gain*(gt*sigmoid(gt))).astype(bf16)
        if h==nh-1 and c==1: yield

def gate_back(raw_ref,gain,dgated_ref,o_ref,nh,emit):
    R=raw_ref.shape[0]; nc=R//CH; n=CH
    off=2*nh*DK+nh*DV
    dO={};ggain=None
    for c in range(nc):
        for h in range(nh):
            r_=slice(c*n,(c+1)*n); co=slice(h*DV,(h+1)*DV)
            o=o_ref[r_,co]
            r=lax.rsqrt(jnp.mean(o*o,axis=-1,keepdims=True)+GATE_EPS)
            gt=raw_ref[r_,off+h*DV:off+(h+1)*DV]
            s=sigmoid(gt); sg=gt*s
            dg=dgated_ref[r_,co]
            nrm=o*r
            emit(h,c,dg*nrm*gain*(s*(1.0+gt*(1.0-s))))
            dsn=dg*sg
            part=jnp.sum(dsn*nrm,axis=0,keepdims=True)
            ggain=part if ggain is None else ggain+part
            dn=dsn*gain
            dO[h,c]=r*dn-nrm*(r*jnp.mean(nrm*dn,axis=-1,keepdims=True))
    return dO,ggain

def mixer_bwd(raw_ref,small_ref,taps_ref,vec_ref,info_ref,segr_ref,dO,u_ref,s_ref,x_ref,nh,P,result):
    R=raw_ref.shape[0]; nc=R//CH; n=CH
    raw=raw_ref; taps=taps_ref[...]; vec=vec_ref[...]; info=info_ref[...]
    segc=info[:,0:1]
    a=acts(raw,taps,info,nh)
    z,ld,beta=decays(small_ref[...],vec,nh)
    yield
    terms=chunk_terms(ld,segc,segr_ref[0:1],R,nh)
    ri=iota2(n,0); ci=iota2(n,1)
    strict=ri>ci
    U_=(ri<=ci).astype(f32)
    idx=[(h,c) for c in reversed(range(nc)) for h in range(nh)]
    sl=lambda c:slice(c*n,(c+1)*n)
    yield
    dU0={};KK={};QK={}
    for h,c in idx:
        K=a[h]["kn"][sl(c)]; Q=a[h]["qn"][sl(c)]
        KK[h,c]=dot(K,K,1,1,P["kk"]); QK[h,c]=dot(Q,K,1,1,P["qk"])
        dU0[h,c]=dot(QK[h,c]*terms[c][h][0],dO[h,c],0,0,P["u"])
    yield
    dS=[None]*nh
    dS1s={};Ys={}
    for c in reversed(range(nc)):
        for h in range(nh):
            R_,e,t,g=terms[c][h]
            K=a[h]["kn"][sl(c)]; Q=a[h]["qn"][sl(c)]
            b=beta[sl(c),nh+h:nh+h+1]
            dS1=dS[h]
            dS1s[h,c]=dS1
            dU=dU0[h,c]
            if dS1 is not None: dU=dU+dot(t*K,dS1,1,0,P["s"])
            Y=dot(x_ref[c*nh+h],dU,0,0,P["s"])
            Ys[h,c]=Y
            if c:
                d0=dot(e*Q,dO[h,c],0,0,P["s"])-dot((b*e)*K,Y,0,0,P["s"])
                dS[h]=d0 if dS1 is None else g*dS1+d0
        yield
    dQ={};dK={};dV={};dbeta={};dld={}
    for h,c in idx:
        R_,e,t,g=terms[c][h]
        K=a[h]["kn"][sl(c)]; Q=a[h]["qn"][sl(c)]; V=a[h]["v"][sl(c)]
        b=beta[sl(c),nh+h:nh+h+1]
        Y=Ys[h,c]; U=u_ref[sl(c),h*DV:(h+1)*DV]; dS1=dS1s[h,c]
        dA=jnp.where(strict,-dot(Y,U,1,1,P["g"]),0.0)
        dP=dot(dO[h,c],U,1,1,P["g"])
        H=dP*R_
        Gr=dA*R_
        G=b*Gr
        dq=dot(H,K,1,0,P["g"])
        dk=dot(G,K,1,0,P["g"])+dot(G,K,0,0,P["g"])+dot(H,Q,0,0,P["g"])
        dV[h,c]=b*Y
        db=jnp.sum(Y*V,axis=-1,keepdims=True)+jnp.sum(Gr*KK[h,c],axis=-1,keepdims=True)
        Z=H*QK[h,c]+G*KK[h,c]
        dc=jnp.sum(Z,axis=-1,keepdims=True)-jnp.sum(Z.T,axis=-1,keepdims=True)
        last=(lax.broadcasted_iota(jnp.int32,(n,1),0)==n-1).astype(f32)
        if c:
            S0=s_ref[c*nh+h]
            YS=dot(Y,S0,1,1,P["g"]); OS=dot(dO[h,c],S0,1,1,P["g"])
            dq=dq+e*OS
            dk=dk-(b*e)*YS
            ks=jnp.sum(YS*K,axis=-1,keepdims=True)
            qs=jnp.sum(OS*Q,axis=-1,keepdims=True)
            db=db-e*ks
            dc=dc+e*(qs-b*ks)
        if dS1 is not None:
            US=dot(U,dS1,1,1,P["g"])
            dk=dk+t*US
            tt=t*jnp.sum(US*K,axis=-1,keepdims=True)
            dc=dc-tt
            tot=jnp.sum(tt,axis=0,keepdims=True)
            if c:
                tot=tot+g*jnp.sum(jnp.sum(dS1*S0,axis=-1,keepdims=True),axis=0,keepdims=True)
            dc=dc+last*tot
        dQ[h,c]=dq; dK[h,c]=dk; dbeta[h,c]=db
        dld[h,c]=dc
        if h==nh-1: yield
    lane=lax.broadcasted_iota(jnp.int32,(n,128),1)
    dsm=[]
    for c in range(nc):
        acc_d=jnp.zeros((n,128),f32); acc_b=jnp.zeros((n,128),f32)
        for h in range(nh):
            acc_d=acc_d+jnp.where(lane==h,dld[h,c],0.0)
            acc_b=acc_b+jnp.where(lane==nh+h,dbeta[h,c],0.0)
        acc_d=dot(U_,acc_d,1,0,6)
        dsm.append((acc_d,acc_b))
    dldf=jnp.concatenate([x[0] for x in dsm],axis=0)
    dbf=jnp.concatenate([x[1] for x in dsm],axis=0)
    dz=-dldf*vec[0:1]*sigmoid(z)
    dsmall=dz+dbf*beta*(1.0-beta)
    g_dt=jnp.sum(dz,axis=0,keepdims=True)
    g_al=jnp.sum(dldf*ld,axis=0,keepdims=True)
    result.append((dsmall,g_dt,g_al))
    for nm in ("q","k","v"):
        for h in range(nh):
            d=a[h]
            w=DV if nm=="v" else DK
            coff={"q":h*DK,"k":nh*DK+h*DK,"v":2*nh*DK+h*DV}[nm]
            dy=jnp.concatenate([{"q":dQ,"k":dK,"v":dV}[nm][h,c] for c in range(nc)],axis=0)
            if nm!="v":
                y=d[nm+"n"]
                if nm=="q": y=y*(DK**0.5)
                dy=d["r"+nm]*(dy-y*jnp.sum(y*dy,axis=-1,keepdims=True))
            pre=d[nm+"pre"]; s=sigmoid(pre)
            dp=dy*(s*(1.0+pre*(1.0-s)))
            u=raw[:,coff:coff+w]; tp=taps[:,coff:coff+w]
            du=tp[3:4]*dp
            tg=[None]*4
            tg[3]=jnp.sum(dp*u,axis=0,keepdims=True)
            for k in (1,2,3):
                su=pltpu.roll(dp,dp.shape[0]-k,0)*info[:,3+k:4+k]
                du=du+tp[3-k:4-k]*su
                tg[3-k]=jnp.sum(su*u,axis=0,keepdims=True)
            result.append((coff,w,du,tg))
        yield


f32=jnp.float32; bf16=jnp.bfloat16
MESH=pl.DeviceIdType.MESH
ANY=pl.BlockSpec(memory_space=pl.ANY)
VM=pl.BlockSpec(memory_space=pltpu.VMEM)

def place():
    d=lax.axis_index("dp"); s=lax.axis_index("shard")
    return d,s,d//2,d%2

def greet(peers):
    bar=pltpu.get_barrier_semaphore()
    for p in peers:
        pl.semaphore_signal(bar,inc=1,device_id=p,device_id_type=MESH)
    pl.semaphore_wait(bar,len(peers))

def greet_all(n_dp,n_s):
    d,s,_,_=place()
    me=d*n_s+s
    bar=pltpu.get_barrier_semaphore()
    def one(q,_):
        @pl.when(q!=me)
        def _():
            pl.semaphore_signal(bar,inc=1,device_id=(q//n_s,q%n_s),device_id_type=MESH)
        return 0
    lax.fori_loop(0,n_dp*n_s,one,0)

def greeted(n_dp,n_s):
    pl.semaphore_wait(pltpu.get_barrier_semaphore(),n_dp*n_s-1)

def remote(src,dst,ss,rs,dev):
    return pltpu.make_async_remote_copy(src_ref=src,dst_ref=dst,send_sem=ss,recv_sem=rs,device_id=dev,device_id_type=MESH)

NORM_EPS=1e-6
D_=pltpu.SemaphoreType.DMA
def ring(n_s):
    d,s,_,_=place()
    return [(d,(s+j)%n_s) for j in range(1,n_s)]

def push_parts(n_s,part,land,ss,rs):
    cs=[]
    for j,p in enumerate(ring(n_s)):
        c=remote(part.at[p[1]],land.at[j],ss.at[j],rs.at[j],p); c.start(); cs.append(c)
    return cs

def push_all(n_s,out,ss,rs):
    _,s,_,_=place()
    cs=[]
    for j,p in enumerate(ring(n_s)):
        c=remote(out.at[s],out.at[s],ss.at[j],rs.at[j],p); c.start(); cs.append(c)
    return cs

def add_up(n_s,part,land):
    _,s,_,_=place()
    t=part[s].astype(f32)
    for j in range(n_s-1): t=t+land[j].astype(f32)
    return t

def norm_back(u,g,dn):
    w=u.shape[-1]
    r=lax.rsqrt(jnp.mean(u*u,axis=-1,keepdims=True)+NORM_EPS)
    gd=g*dn
    du=r*gd-u*(r*r*r*(jnp.sum(u*gd,axis=-1,keepdims=True)/w))
    return du,jnp.sum(u*r*dn,axis=0,keepdims=True)


D = 1024
H = 8
ROW_CQ = 2 * D * H // 128
ROW_CK = ROW_CQ + KCONV * H * DK // 128
ROW_CV = ROW_CK + KCONV * H * DK // 128
ROW_G1 = ROW_CV + KCONV * H * DV // 128
ROW_G2 = ROW_G1 + D // 128
ROW_GO = ROW_G2 + D // 128
ROW_AL = ROW_GO + DV // 128
SMALL_ROWS = 288
SLICE = 16

def wide_row(ref,first,width):
    return jnp.concatenate([ref[first+i:first+i+1,:] for i in range(width//128)],axis=1)

def tap_rows(s,nh):
    out=[]
    for base,width,off in ((ROW_CQ,DK,0),(ROW_CK,DK,nh*DK),(ROW_CV,DV,2*nh*DK)):
        per=width//128
        for i in range(KCONV):
            for c in range(nh*per):
                out.append((base+i*H*per+s*nh*per+c,i,off+c*128))
    return out

def spread(n_d):
    per=128//H
    d=lax.broadcasted_iota(jnp.int32,(n_d,n_d//per),0); r=lax.broadcasted_iota(jnp.int32,(n_d,n_d//per),1)
    dd=lax.broadcasted_iota(jnp.int32,(n_d,128),0); l=lax.broadcasted_iota(jnp.int32,(n_d,128),1)
    return (d//per==r).astype(f32),(l//H==dd%per).astype(f32)

def pick(s,nh,first):
    l=lax.broadcasted_iota(jnp.int32,(128,128),0); j=lax.broadcasted_iota(jnp.int32,(128,128),1)-first
    return jnp.logical_and(jnp.logical_and(j>=0,j<nh),l%H==s*nh+j).astype(f32)

def unpack_small(packed,lens,s,nh,n_s,taps,vec,gain,gain1,gain2,w_sm,info,segr):
    taps[...]=jnp.zeros_like(taps)
    for row,i,off in tap_rows(s,nh): taps[i:i+1,off:off+128]=packed[pl.ds(row,1),:]
    lane=lax.broadcasted_iota(jnp.int32,(1,128),1)
    last=packed[ROW_AL:ROW_AL+1,:]
    vec[...]=jnp.zeros_like(vec)
    al=jnp.zeros((1,128),f32); dt=jnp.zeros((1,128),f32)
    for j in range(nh):
        al=al+jnp.where(lane==j,jnp.exp(jnp.sum(jnp.where(lane==s*nh+j,last,0.0),axis=1,keepdims=True)),0.0)
        dt=dt+jnp.where(lane==j,jnp.sum(jnp.where(lane==H+s*nh+j,last,0.0),axis=1,keepdims=True),0.0)
    vec[0:1]=al; vec[1:2]=dt
    gain[...]=jnp.broadcast_to(wide_row(packed,ROW_GO,gain.shape[1]),gain.shape)
    gain1[...]=jnp.broadcast_to(wide_row(packed,ROW_G1,gain1.shape[1]),gain1.shape)
    gain2[...]=jnp.broadcast_to(wide_row(packed,ROW_G2,gain2.shape[1]),gain2.shape)
    n_d=w_sm.shape[0]; per=n_d*H//128
    e1,mask=spread(n_d)
    t=jnp.zeros((n_d,128),f32)
    for k in range(2):
        a=dot(e1,packed[k*per:(k+1)*per,:],1,0,1)*mask
        t=t+dot(a,pick(s,nh,k*nh),1,0,1)
    w_sm[...]=t.astype(bf16)
    rows=info.shape[0]; count=lens.shape[1]
    lv=lens[...].astype(f32)
    ends=[];e=jnp.zeros((1,1),f32)
    for j in range(count):
        e=e+lv[:,j:j+1]; ends.append(e)
    def number(p):
        n=jnp.zeros_like(p)
        for e in ends: n=n+(p>=e).astype(f32)
        return jnp.where(p<0.0,-1.0,n)
    lanes=lax.broadcasted_iota(jnp.int32,(rows,128),1)
    pos=lax.broadcasted_iota(jnp.int32,(rows,128),0).astype(f32)
    shift=jnp.where(lanes<=3,-lanes,lanes-3).astype(f32)
    seg=number(pos)
    info[...]=jnp.where(lanes==0,seg,(number(pos+shift)==seg).astype(f32))
    segr[...]=number(lax.broadcasted_iota(jnp.int32,segr.shape,1).astype(f32))

def pack_small(sg,psm,taps,g_al,g_dt,gg,dg1,dg2,s,nh,n_s):
    sg[...]=jnp.zeros_like(sg)
    n_d=psm.shape[0]; per=n_d*H//128
    e1,mask=spread(n_d)
    for k in range(2):
        a=dot(psm,pick(s,nh,k*nh),1,1,6)*mask
        sg[k*per:(k+1)*per,:]=dot(e1,a,0,0,6)
    where={}
    for row,i,off in tap_rows(s,nh): where[i,off]=row
    for coff,w,_,tg in taps:
        for i in range(KCONV):
            for c in range(w//128):
                sg[pl.ds(where[i,coff+c*128],1),:]=tg[i][:,c*128:(c+1)*128]
    for first,v in ((ROW_G1,dg1),(ROW_G2,dg2),(ROW_GO,gg)):
        for i in range(v.shape[1]//128): sg[first+i:first+i+1,:]=v[:,i*128:(i+1)*128]
    lane=lax.broadcasted_iota(jnp.int32,(1,128),1)
    t=jnp.zeros((1,128),f32)
    for j in range(nh):
        t=t+jnp.where(lane==s*nh+j,g_al[:,j:j+1],0.0)+jnp.where(lane==H+s*nh+j,g_dt[:,j:j+1],0.0)
    sg[ROW_AL:ROW_AL+1,:]=t

def share_small(n_dp,n_s,sg,land,ss,rs):
    d,s,_,_=place()
    me=d*n_s+s
    def one(q,_):
        src=sg.at[pl.ds(pl.multiple_of(q*SLICE,SLICE),SLICE)]
        @pl.when(q==me)
        def _():
            pltpu.make_async_copy(src,land.at[me],rs.at[0]).start()
        @pl.when(q!=me)
        def _():
            remote(src,land.at[me],ss.at[0],rs.at[0],(q//n_s,q%n_s)).start()
        return 0
    lax.fori_loop(0,SMALL_ROWS//SLICE,one,0)

def shared_small(n_dp,n_s,sg,land,ss,rs):
    d,s,_,_=place()
    me=d*n_s+s
    n=SMALL_ROWS//SLICE
    @pl.when(me<n)
    def _():
        pltpu.make_async_copy(land,land,rs.at[0]).wait()
        part=sg.at[pl.ds(0,SLICE*(n-1))]
        pltpu.make_async_copy(part,part,ss.at[0]).wait()
    @pl.when(me>=n)
    def _():
        pltpu.make_async_copy(sg,sg,ss.at[0]).wait()

def spread_small(n_dp,n_s,land,total,part,ss,rs):
    d,s,_,_=place()
    me=d*n_s+s; nd=n_dp*n_s
    @pl.when(me<SMALL_ROWS//SLICE)
    def _():
        t=land[0]
        for q in range(1,nd): t=t+land[q]
        part[...]=t
        dst=total.at[pl.ds(pl.multiple_of(me*SLICE,SLICE),SLICE)]
        def one(q,_):
            @pl.when(q==me)
            def _():
                pltpu.make_async_copy(part,dst,rs.at[0]).start()
            @pl.when(q!=me)
            def _():
                remote(part,dst,ss.at[0],rs.at[0],(q//n_s,q%n_s)).start()
            return 0
        lax.fori_loop(0,nd,one,0)

def spread_done(n_dp,n_s,land,total,ss,rs):
    d,s,_,_=place()
    me=d*n_s+s; nd=n_dp*n_s
    @pl.when(me<SMALL_ROWS//SLICE)
    def _():
        sent=land.at[pl.ds(0,nd-1)]
        pltpu.make_async_copy(sent,sent,ss.at[0]).wait()
    pltpu.make_async_copy(total,total,rs.at[0]).wait()


f32=jnp.float32; bf16=jnp.bfloat16
CA,CB,CC=3.4445,-4.775,2.0315
NS_STEPS=2
PANEL=512
def dg(a,b,ca,cb): return lax.dot_general(a,b,(((ca,),(cb,)),((),())),preferred_element_type=f32)

def mirror(m,i,r,tm):
    for j in range(i+1,r//tm):
        m[j*tm:(j+1)*tm,i*tm:(i+1)*tm]=m[i*tm:(i+1)*tm,j*tm:(j+1)*tm].T

def newton_schulz(wide,tall,tmp,acc,g,p,is_tall,count,tm=256):
    r=g.shape[0]
    at=lambda c: pl.ds(pl.multiple_of(c*PANEL,PANEL),PANEL)
    def both(fw,ft):
        @pl.when(jnp.logical_not(is_tall))
        def _(): lax.fori_loop(0,count,fw,0)
        @pl.when(is_tall)
        def _(): lax.fori_loop(0,count,ft,0)
    tmp[...]=jnp.zeros_like(tmp)
    def sqw(c,_):
        def one(k,_):
            v=wide[pl.ds(pl.multiple_of(k*128,128),128),at(c)].astype(f32)
            tmp[0:1,0:PANEL]=tmp[0:1,0:PANEL]+jnp.sum(v*v,axis=0,keepdims=True)
            return 0
        return lax.fori_loop(0,r//128,one,0)
    def sqt(c,_):
        def one(k,_):
            v=tall[pl.ds(pl.multiple_of(c*PANEL+k*128,128),128),:].astype(f32)
            tmp[0:1,:]=tmp[0:1,:]+jnp.sum(v*v,axis=0,keepdims=True)
            return 0
        return lax.fori_loop(0,PANEL//128,one,0)
    both(sqw,sqt)
    inv=1.0/(jnp.sqrt(jnp.sum(tmp[0:1,:],axis=1,keepdims=True))+1e-7)
    def scw(c,_):
        def one(k,_):
            q=pl.ds(pl.multiple_of(k*128,128),128)
            wide[q,at(c)]=(wide[q,at(c)].astype(f32)*inv).astype(bf16)
            return 0
        return lax.fori_loop(0,r//128,one,0)
    def sct(c,_):
        def one(k,_):
            q=pl.ds(pl.multiple_of(c*PANEL+k*128,128),128)
            tall[q,:]=(tall[q,:].astype(f32)*inv).astype(bf16)
            return 0
        return lax.fori_loop(0,PANEL//128,one,0)
    both(scw,sct)
    def step(_,__):
        acc[...]=jnp.zeros_like(acc)
        def gw(c,_):
            for i in range(r//tm):
                ri=slice(i*tm,(i+1)*tm)
                acc[ri,i*tm:r]+=dg(wide[ri,at(c)],wide[i*tm:r,at(c)],1,1)
            return 0
        def gt(c,_):
            for i in range(r//tm):
                ri=slice(i*tm,(i+1)*tm)
                acc[ri,i*tm:r]+=dg(tall[at(c),ri],tall[at(c),i*tm:r],0,0)
            return 0
        both(gw,gt)
        for i in range(r//tm):
            ri=slice(i*tm,(i+1)*tm)
            g[ri,i*tm:r]=acc[ri,i*tm:r].astype(bf16)
            mirror(g,i,r,tm)
        for i in range(r//tm):
            ri=slice(i*tm,(i+1)*tm)
            p[ri,i*tm:r]=(CB*g[ri,i*tm:r].astype(f32)+CC*dg(g[ri,:],g[:,i*tm:r],1,0)).astype(bf16)
            mirror(p,i,r,tm)
        def nw(c,_):
            g[:,0:PANEL]=wide[:,at(c)]
            for i in range(r//PANEL):
                ri=slice(i*PANEL,(i+1)*PANEL)
                wide[ri,at(c)]=(CA*g[ri,0:PANEL].astype(f32)+dg(p[ri,:],g[:,0:PANEL],1,0)).astype(bf16)
            return 0
        def nt(c,_):
            v=tall[at(c),:]
            tall[at(c),:]=(CA*v.astype(f32)+dg(v,p[...],1,0)).astype(bf16)
            return 0
        both(nw,nt)
        return 0
    lax.fori_loop(0,NS_STEPS,step,0)


MOMENTUM = 0.95
MUON_RATE = 0.1
MUON_DECAY = 0.01

def muon_owner(i,n_dp):
    base=n_dp//2-2
    d,s=((2,0),(3,0),(1,2),(3,2),(2,2),(0,0),(1,0),(0,2))[i]
    return base+d,s

def grad_blocks(i,landed):
    gu,dn,out,gate,qkv=landed
    if i==4: return [(0,out[...].astype(f32))]
    if i==7: return [(0,dn[...].astype(f32))]
    n_s=gu.shape[0]
    if i in (5,6):
        ref,w=gu,gu.shape[2]//2; at=(i-5)*w
    elif i==3:
        ref,w,at=gate,gate.shape[2],0
    else:
        q=qkv.shape[2]//4
        ref,w,at=qkv,(q,q,2*q)[i],(0,q,2*q)[i]
    return [(t*w,ref[t,:,at:at+w].astype(f32)) for t in range(n_s)]

def member(i,refs):
    a,k=((0,0),(0,1),(1,0),(1,1),(2,None),(3,0),(3,1),(4,None))[i]
    return refs[a],k

def part_of(ref,k,col,w):
    return ref[:,col:col+w] if k is None else ref[k,:,col:col+w]

def store_part(ref,k,col,v):
    if k is None: ref[:,col:col+v.shape[1]]=v
    else: ref[k,:,col:col+v.shape[1]]=v

def kinds_of(momenta,nd):
    kinds=[]
    for i in range(8):
        r,c=member(i,momenta)[0].shape[-2:]
        tall=r*nd>c
        kinds.append((tall,-(-r//16)*16 if tall else r,c))
    return tuple(kinds)

def land_shapes(kinds,nd):
    r=min(min(k[1]*nd,k[2]) for k in kinds)
    up=lambda x: -(-x//PANEL)*PANEL
    return (r,up(max(k[2] for k in kinds if not k[0]))),(up(max(k[1]*nd for k in kinds if k[0])),r)

def make_look(i,look,landed,momenta):
    ref,k=member(i,momenta)
    rows=ref.shape[-2]
    if look.shape[0]>rows: look[rows:,:]=jnp.zeros((look.shape[0]-rows,look.shape[1]),bf16)
    for col,v in grad_blocks(i,landed):
        m=MOMENTUM*part_of(ref,k,col,v.shape[1])+v
        look[0:rows,col:col+v.shape[1]]=(v+MOMENTUM*m).astype(bf16)

def slot(kind,buf,q):
    t,rows,cols=kind
    ds=pl.ds(pl.multiple_of(q*rows,rows),rows)
    return buf.at[ds] if t else buf.at[ds,pl.ds(0,cols)]

def whole(kind,buf,nd):
    t,rows,cols=kind
    return buf.at[pl.ds(0,rows*nd)] if t else buf.at[:,pl.ds(0,cols)]

class Looks:
    def __init__(self,n_dp,n_s,kinds,look,landed,momenta,wide,tall,rin,sin):
        self.d,self.s,_,_=place()
        self.n_dp=n_dp; self.nd=n_dp*n_s; self.me=self.d*n_s+self.s
        self.kinds=kinds; self.look=look; self.landed=landed; self.momenta=momenta
        self.wide=wide; self.tall=tall; self.rin=rin; self.sin=sin
    def at(self,i):
        o=muon_owner(i,self.n_dp)
        return o,jnp.logical_and(self.d==o[0],self.s==o[1])
    def buf(self,i): return self.tall if self.kinds[i][0] else self.wide
    def look_of(self,i): make_look(i,self.look[i],self.landed,self.momenta)
    def push(self,i):
        o,there=self.at(i)
        dst=slot(self.kinds[i],self.buf(i),self.me)
        @pl.when(there)
        def _():
            pltpu.make_async_copy(self.look[i],dst,self.rin.at[0]).start()
        @pl.when(jnp.logical_not(there))
        def _():
            remote(self.look[i],dst,self.sin.at[i],self.rin.at[0],o).start()
    def arrived(self,i):
        full=whole(self.kinds[i],self.buf(i),self.nd)
        pltpu.make_async_copy(full,full,self.rin.at[0]).wait()
    def left(self,i):
        _,there=self.at(i)
        @pl.when(jnp.logical_not(there))
        def _():
            pltpu.make_async_copy(self.look[i],self.look[i],self.sin.at[i]).wait()

def muon_kernel(n_dp,n_s,kinds,*refs):
    n=len(kinds)
    landed=refs[:5]; momenta=refs[5:10]; sland=refs[10]; outs=refs[11:11+n]; stot=refs[11+n]
    look=refs[12+n:20+n]
    wide,tall,tmp,acc,g,p,spart,rin,sin,rout,sout,st,rt=refs[20+n:]
    nd=n_dp*n_s
    E=Looks(n_dp,n_s,kinds,look,landed,momenta,wide,tall,rin,sin)
    order=(7,5,6,4,2,3,0,1)
    greet_all(n_dp,n_s)
    for i in order: E.look_of(i)
    greeted(n_dp,n_s)
    spread_small(n_dp,n_s,sland,stot,spart,st,rt)
    for i in order: E.push(i)
    count=jnp.int32(0); tall_here=jnp.int32(0); here=jnp.int32(0)
    for i in range(n):
        t,rows,cols=kinds[i]
        _,there=E.at(i)
        one=there.astype(jnp.int32)
        size=rows*nd if t else cols
        count=count+one*(-(-size//PANEL)); here=here+one
        if t: tall_here=tall_here+one
        pad=-size%PANEL
        @pl.when(there)
        def _():
            if pad:
                if t: tall[size:size+pad,:]=jnp.zeros((pad,tall.shape[1]),bf16)
                else: wide[:,size:size+pad]=jnp.zeros((wide.shape[0],pad),bf16)
            E.arrived(i)
    @pl.when(here>0)
    def _():
        newton_schulz(wide,tall,tmp,acc,g,p,tall_here>0,count)
    for i in range(n):
        t,rows,cols=kinds[i]
        _,there=E.at(i)
        @pl.when(there)
        def _():
            buf=E.buf(i)
            def send(k,_):
                q=((k+E.d)%n_dp)*n_s+(E.s+k//n_dp)%n_s
                src=slot(kinds[i],buf,q)
                @pl.when(q==E.me)
                def _():
                    pltpu.make_async_copy(src,outs[i],rout.at[i]).start()
                @pl.when(q!=E.me)
                def _():
                    remote(src,outs[i],sout.at[0],rout.at[i],(q//n_s,q%n_s)).start()
                return 0
            lax.fori_loop(0,nd,send,0)
            part=buf.at[pl.ds(0,rows*(nd-1))] if t else buf.at[pl.ds(0,rows*(nd-1)),pl.ds(0,cols)]
            pltpu.make_async_copy(part,part,sout.at[0]).wait()
    for i in order: E.left(i)
    spread_done(n_dp,n_s,sland,stot,st,rt)
    for i in range(n):
        pltpu.make_async_copy(outs[i],outs[i],rout.at[i]).wait()

def muon(landed,momenta,sland,n_dp,n_s,cid):
    nd=n_dp*n_s
    kinds=kinds_of(momenta,nd)
    xw,xt=land_shapes(kinds,nd); r=xw[0]
    V=pltpu.VMEM
    return pl.pallas_call(functools.partial(muon_kernel,n_dp,n_s,kinds),
        out_shape=[jax.ShapeDtypeStruct(k[1:],bf16) for k in kinds]+[jax.ShapeDtypeStruct((SMALL_ROWS,128),f32)],in_specs=[VM]*11,out_specs=[VM]*9,
        scratch_shapes=[V(k[1:],bf16) for k in kinds]+[V(xw,bf16),V(xt,bf16),V((8,r),f32),V((r,r),f32)]+[V((r,r),bf16)]*2+[V((SLICE,128),f32)]+[D_((1,)),D_((8,)),D_((8,)),D_((1,)),D_((1,)),D_((1,))],
        compiler_params=pltpu.CompilerParams(collective_id=cid,has_side_effects=True,vmem_limit_bytes=62<<20),name="muon")(*landed,*momenta,sland)

def finish_kernel(nd,*refs):
    landed=refs[:5]; momenta=refs[5:10]; masters=refs[10:15]; orthos=refs[15:23]
    grads=refs[23:28]; steps=refs[28:33]; moms=refs[33:38]
    for i in range(8):
        ms,k=member(i,masters)
        rows,cols=ms.shape[-2:]
        scale=0.2*math.sqrt(max(rows*nd,cols))
        for col,v in grad_blocks(i,landed):
            w=v.shape[1]
            store_part(member(i,grads)[0],k,col,v)
            store_part(member(i,moms)[0],k,col,MOMENTUM*part_of(member(i,momenta)[0],k,col,w)+v)
        o=orthos[i][0:rows,:].astype(f32)
        store_part(member(i,steps)[0],k,0,-MUON_RATE*(scale*o+MUON_DECAY*part_of(ms,k,0,cols)))

def finish(landed,momenta,masters,orthos,nd):
    out=[jax.ShapeDtypeStruct(m.shape,f32) for m in masters]
    return pl.pallas_call(functools.partial(finish_kernel,nd),out_shape=out*3,in_specs=[VM]*23,out_specs=[VM]*15,
        compiler_params=pltpu.CompilerParams(vmem_limit_bytes=60<<20),name="updates")(*landed,*momenta,*masters,*orthos)


class Cube:
    def __init__(self,n_dp):
        self.d,self.s,self.hi,self.lo=place()
        self.n=n_dp; self.bits=[1<<b for b in range(n_dp.bit_length()-1)]
        self.x=self.bits[-1]
    def block(self,e):
        h=self.hi
        for b in self.bits[:-1]:
            if e&b: h=h+b-2*b*((h//b)%2)
        x=1-self.lo if e&self.x else self.lo
        return h*2+x
    def dev(self,e): return (self.block(e),self.s)

class Reducer:
    def __init__(self,n_dp,n_s,pieces,sems,W):
        self.c=c=Cube(n_dp)
        self.n_s=n_s; self.p=pieces; self.W=W
        self.sx,self.rx,self.sf,self.rf,self.lsem=sems
        self.s=c.s
        me=c.s*n_dp+c.d
        self.td=me//n_s; self.ts=me%n_s
        self.moved=jnp.logical_or(self.td!=c.d,self.ts!=c.s)
        self.grp=ring(n_s)
        self.q=[]; self.ns=0; self.nh=0; self.late=[]; self.fc={}; self.hook=None
        for p in pieces:
            dims=p["dims"]; first=dims[0]
            rest=[e for e in range(n_dp) if not e&first]
            pos=lambda e,dims=dims: next((i for i,b in enumerate(dims) if e&b),len(dims))
            p["order"]=sorted(rest,key=lambda e:(pos(e),-bin(e).count("1"),-e))
            p["pos"]=pos
    def via(self,k,e): return self.p[k]["dims"][self.p[k]["pos"](e)]
    def msg(self,k,e):
        p=self.p[k]; dims=p["dims"]; b=self.via(k,e)
        src=p["g"].at[self.c.block(e)] if b==dims[0] else p["land"].at[(e|dims[0])-1]
        return remote(src,p["land"].at[e-1],self.sx.at[k,e-1],self.rx.at[k,e-1],self.c.dev(b))
    def add(self,k): self.q+=[(k,e) for e in self.p[k]["order"]]
    def total(self,k,e):
        p=self.p[k]; dims=p["dims"]
        t=p["g"][self.c.block(e)].astype(f32)
        for b in dims[:p["pos"](e)]:
            self.msg(k,e|b).wait()
            t=t+p["land"][(e|b)-1].astype(f32)
        return t
    def handle(self,k,e):
        p=self.p[k]
        if e:
            t=self.total(k,e)
            p["land"][(e|p["dims"][0])-1]=t.astype(bf16)
            self.msg(k,e).start()
        else:
            self.late.append([k,2,self.finish])
    def finish(self,k):
        p=self.p[k]
        t=self.total(k,0).astype(bf16)
        fin,out=p["fin"],p["out"]
        if p["col"]:
            rows=t.shape[0]//self.n_s
            fin[...]=t.reshape(self.n_s,rows,t.shape[1])
            c=pltpu.make_async_copy(fin.at[self.s],out.at[self.s],self.lsem.at[k]); c.start()
            self.fc[k]=[c]
            for j,q in enumerate(self.grp):
                c=remote(fin.at[q[1]],out.at[self.s],self.sf.at[k,j],self.rf.at[k,j],q); c.start(); self.fc[k].append(c)
        else:
            fin[...]=t
            @pl.when(self.moved)
            def _():
                remote(fin,out,self.sf.at[k,0],self.rf.at[k,0],(self.td,self.ts)).start()
            @pl.when(jnp.logical_not(self.moved))
            def _():
                pltpu.make_async_copy(fin,out,self.rf.at[k,0]).start()
        self.late.append([k,2,self.landed])
    def tick(self,times=1):
        for _ in range(times):
            if self.ns<len(self.q):
                k,e=self.q[self.ns]
                self.msg(k,e|self.p[k]["dims"][0]).start(); self.ns+=1
                if self.ns-self.nh>self.W:
                    self.handle(*self.q[self.nh]); self.nh+=1
            elif self.nh<self.ns:
                self.handle(*self.q[self.nh]); self.nh+=1
            for e in list(self.late):
                e[1]-=1
                if e[1]<0:
                    self.late.remove(e); e[2](e[0])
    def landed(self,k):
        p=self.p[k]
        if p["col"]:
            for c in self.fc[k]: c.wait()
        else:
            fin,out=p["fin"],p["out"]
            pltpu.make_async_copy(fin,out,self.rf.at[k,0]).wait()
            @pl.when(self.moved)
            def _():
                remote(fin,out,self.sf.at[k,0],self.rf.at[k,0],(self.td,self.ts)).wait_send()
        if self.hook: self.hook(k)
    def drain(self):
        while self.nh<len(self.q) or self.late: self.tick()

class Gatherer:
    def __init__(self,n_dp,n_s,ins,outs,ncol,sems,order):
        self.c=c=Cube(n_dp)
        self.n_dp=n_dp; self.n_s=n_s; self.ins=ins; self.outs=outs; self.ncol=ncol; self.order=order
        self.s0,self.r0,self.s1,self.r1,self.lsem=sems
        self.d=c.d; self.s=c.s
        me=c.d*n_s+c.s
        self.td=me%n_dp; self.ts=me//n_dp
        self.moved=jnp.logical_or(self.td!=c.d,self.ts!=c.s)
        self.grp=ring(n_s)
        self.col={}; self.done=set(); self.i=0
        self.depth=len(c.bits)
    def phase0(self,k):
        src,dst=self.ins[k],self.outs[k]
        if k<self.ncol:
            c=pltpu.make_async_copy(src.at[self.s],dst.at[self.d,self.s],self.lsem.at[k]); c.start()
            self.col[k]=[c]
            for j,p in enumerate(self.grp):
                c=remote(src.at[p[1]],dst.at[self.d,self.s],self.s0.at[k,j],self.r0.at[k,j],p); c.start(); self.col[k].append(c)
        else:
            @pl.when(self.moved)
            def _():
                remote(src,dst.at[self.td],self.s0.at[k,0],self.r0.at[k,0],(self.td,self.ts)).start()
            @pl.when(jnp.logical_not(self.moved))
            def _():
                pltpu.make_async_copy(src,dst.at[self.d],self.r0.at[k,0]).start()
    def ready(self,k):
        if k in self.done: return
        self.done.add(k)
        if k<self.ncol:
            for c in self.col[k]: c.wait()
        else:
            src,dst=self.ins[k],self.outs[k]
            pltpu.make_async_copy(src,dst.at[self.d],self.r0.at[k,0]).wait()
            @pl.when(self.moved)
            def _():
                remote(src,dst.at[self.td],self.s0.at[k,0],self.r0.at[k,0],(self.td,self.ts)).wait_send()
    def blk(self,i,e):
        k,a,m,_=self.order[i]
        src=self.c.block(e)
        return self.outs[k].at[src,a:a+m] if m else self.outs[k].at[src]
    def last(self,i,e): return max((j for j,b in enumerate(self.order[i][3]) if e&b),default=-1)
    def msg(self,i,e):
        b=self.order[i][3][self.last(i,e)]
        blk=self.blk(i,e^b)
        return remote(blk,blk,self.s1.at[i,e-1],self.r1.at[i,e-1],self.c.dev(b))
    def pass_on(self,i,e):
        for b in self.order[i][3][self.last(i,e)+1:]: self.msg(i,e|b).start()
    def stage(self,i,depth):
        es=[e for e in range(1,self.n_dp) if bin(e).count("1")==depth]
        for e in sorted(es,key=lambda e:self.last(i,e)):
            self.msg(i,e).wait()
            self.pass_on(i,e)
    def tick(self,times=1):
        n=len(self.order)
        for _ in range(times):
            i=self.i; self.i+=1
            if i<n:
                self.ready(self.order[i][0])
                self.pass_on(i,0)
            for dep in range(1,self.depth+1):
                if 0<=i-dep<n: self.stage(i-dep,dep)
    def after(self,i):
        while self.i<i+self.depth+1: self.tick()
    def drain(self):
        self.after(len(self.order)-1)


def dotb(a,b,ca,cb): return lax.dot_general(a,b,(((ca,),(cb,)),((),())),preferred_element_type=f32)

def fore_kernel(n_dp,n_s,nh,P,order,last_in,last_out,*refs):
    (qk,vg,gu,ow,dw,x_ref,dyown,packed,lens,
     g_in,g_out,normed,raw,small,gated,o_ref,u_ref,s_ref,xi_ref,middle,w_sm,taps,vec,gain,gain1,gain2,info,segr,ypart,dpart,dland,part_gu,part_dn,
     c_in,c_gu,c_out,c_dn,part,land,g_gu,g_dn,dy,gath,hid,dgu)=refs[:45]
    sems=refs[45:50]; ss,rs=refs[50:52]
    E=Gatherer(n_dp,n_s,[c_in,c_gu,c_out,c_dn],[g_in,g_gu,g_out,g_dn],2,sems,order)
    s=E.s
    kq=nh*DK; kv=nh*DV; ff=c_gu.shape[2]//2
    greet_all(n_dp,n_s)
    for t in range(n_s):
        c_in[t,:,0:kq]=qk[0,:,t*kq:(t+1)*kq].astype(bf16)
        c_in[t,:,kq:2*kq]=qk[1,:,t*kq:(t+1)*kq].astype(bf16)
        c_in[t,:,2*kq:2*kq+kv]=vg[0,:,t*kv:(t+1)*kv].astype(bf16)
        c_in[t,:,2*kq+kv:]=vg[1,:,t*kv:(t+1)*kv].astype(bf16)
    greeted(n_dp,n_s)
    E.phase0(0)
    g1=wide_row(packed,ROW_G1,gain1.shape[1])
    xv=x_ref[...].astype(f32)
    normed[s]=(xv*lax.rsqrt(jnp.mean(xv*xv,axis=-1,keepdims=True)+NORM_EPS)*g1).astype(bf16)
    c_out[...]=ow[...].astype(bf16)
    E.phase0(2)
    a=push_all(n_s,normed,ss.at[0],rs.at[0])
    E.tick(1)
    for t in range(n_s):
        c_gu[t,:,0:ff]=gu[0,:,t*ff:(t+1)*ff].astype(bf16)
        c_gu[t,:,ff:]=gu[1,:,t*ff:(t+1)*ff].astype(bf16)
    c_dn[...]=dw[...].astype(bf16)
    E.phase0(1); E.phase0(3)
    unpack_small(packed,lens,s,nh,n_s,taps,vec,gain,gain1,gain2,w_sm,info,segr)
    E.tick(1)
    dy[s]=dyown[...]
    b=push_all(n_s,dy,ss.at[1],rs.at[1])
    for c in a: c.wait()
    local,D=x_ref.shape; rows=local*n_s
    nrm=normed[...].reshape(rows,D)
    small[...]=dotb(nrm,w_sm[...],1,0)
    E.after(last_in)
    raw[...]=dotb(nrm,g_in[...].reshape(D,raw.shape[1]),1,0)
    E.tick()
    for i,_ in enumerate(mixer_fwd(raw,small,taps,vec,gain,info,segr,gated,o_ref,u_ref,s_ref,xi_ref,nh,P)):
        if i%2==0: E.tick()
    E.after(last_out)
    part[...]=dotb(gated[...],g_out[...].reshape(nh*DV,D),1,0).astype(bf16).reshape(part.shape)
    c1=push_parts(n_s,part,land,ss.at[2],rs.at[2])
    E.tick()
    for c in c1: c.wait()
    m=x_ref[...].astype(f32)+add_up(n_s,part,land)
    middle[...]=m
    r=lax.rsqrt(jnp.mean(m*m,axis=-1,keepdims=True)+NORM_EPS)
    gath[s]=(m*r*gain2[0:1]).astype(bf16)
    c2=push_all(n_s,gath,ss.at[3],rs.at[3])
    E.drain()
    for c in c2: c.wait()
    for c in b: c.wait()
    n2=gath[...].reshape(rows,D)
    w_gu=g_gu[...].reshape(D,2*ff)
    gup=dotb(n2,w_gu,1,0)
    gt=gup[:,:ff]; up=gup[:,ff:]
    sg=sigmoid(gt)
    hid[...]=(gt*sg*up).astype(bf16)
    dyv=dy[...].reshape(rows,D)
    w_dn=g_dn[...].reshape(ff,D)
    dh=dotb(dyv,w_dn,1,1)
    dgu[:,:ff]=(dh*up*sg*(1.0+gt*(1.0-sg))).astype(bf16)
    dgu[:,ff:]=(dh*(gt*sg)).astype(bf16)
    dpart[...]=dotb(dgu[...],w_gu,1,1).astype(bf16).reshape(dpart.shape)
    c3=push_parts(n_s,dpart,dland,ss.at[4],rs.at[4])
    part_dn[...]=dotb(hid[...],dyv,0,0).astype(bf16).reshape(part_dn.shape)
    part_gu[...]=dotb(n2,dgu[...],0,0).astype(bf16).reshape(part_gu.shape)
    ypart[...]=dotb(hid[...],w_dn,1,0).astype(bf16).reshape(ypart.shape)
    for c in c3: c.wait()

def fore(qk,vg,gu,ow,dw,x,dyown,packed,lens,n_dp,n_s,P,cid):
    ins=[qk,vg,gu,ow,dw,x,dyown,packed,lens]
    local,D=x.shape; rows=local*n_s; n_hi=n_dp//2
    nh=H//n_s; wid=nh*(2*DK+2*DV); nb=nh*rows//CH
    z=[1<<b for b in range(n_hi.bit_length()-1)]; xb=n_hi
    main=tuple(z[::-1]+[xb]); other=tuple(z[:0:-1]+[xb,z[0]])
    order=tuple([(0,i,1,main if i<n_s-1 else other) for i in range(n_s)]+[(2,0,0,main)]+[(1,i,1,main if i<n_s-1 else other) for i in range(n_s)]+[(3,0,0,main)])
    S_=jax.ShapeDtypeStruct; V=pltpu.VMEM
    ps=[(n_s,qk.shape[1],wid),(n_s,gu.shape[1],2*gu.shape[2]//n_s),ow.shape,dw.shape]
    outs=[S_((n_dp,)+q,bf16) for q in (ps[0],ps[2])]+[S_((n_s,local,D),bf16)]+[S_((rows,wid),f32),S_((rows,128),f32),S_((rows,nh*DV),bf16),S_((rows,nh*DV),f32),S_((rows,nh*DV),f32),
          S_((nb,DK,DV),f32),S_((nb,CH,CH),f32),S_((local,D),f32)]
    outs+=[S_((D,128),bf16),S_((8,nh*(2*DK+DV)),f32),S_((8,128),f32),S_((8,DV),f32),S_((8,D),f32),S_((8,D),f32),S_((rows,128),f32),S_((8,rows),f32)]
    outs+=[S_((n_s,local,D),bf16)]*2+[S_((n_s-1,local,D),bf16),S_((n_dp,D//n_dp,ps[1][2]),bf16),S_((n_dp,)+dw.shape,bf16)]
    sc=[V(q,bf16) for q in ps]+[V((n_s,local,D),bf16),V((n_s-1,local,D),bf16)]+[V((n_dp,)+ps[1],bf16),V((n_dp,)+ps[3],bf16)]+[V((n_s,local,D),bf16)]*2+[V((rows,ps[1][2]//2),bf16),V((rows,ps[1][2]),bf16)]
    sc+=[D_((4,n_s))]*2+[D_((len(order),n_dp))]*2+[D_((4,))]+[D_((5,n_s))]*2
    return pl.pallas_call(functools.partial(fore_kernel,n_dp,n_s,nh,P,order,n_s-1,n_s),
        out_shape=outs,in_specs=[VM]*len(ins),out_specs=[VM]*len(outs),scratch_shapes=sc,
        compiler_params=pltpu.CompilerParams(collective_id=cid,has_side_effects=True,vmem_limit_bytes=63<<20),name="forward")(*ins)


OTHER=(1,)
TAIL=3

def back_kernel(n_dp,n_s,nh,P,W,*refs):
    (gu_ref,dn_ref,ypart,dpart,dland0,middle,dy,x_ref,gain2,gain1,w_out,w_in,w_sm,raw,small,taps,vec,gain,info,segr,normed,gated,o_ref,u_ref,s_ref,xi_ref,
     out_gu,out_dn,out_out,out_g,out_q,bout,igrad,stot,
     yland,dland,gath,dgt,draw,dsb,epart,dmid,
     p_out,p_g,p_q,sg)=refs[:46]
    rest=refs[46:]
    land=rest[0:5]; fin=rest[5:10]
    sems=rest[10:15]; ss,rs,st,rt=rest[15:19]
    gs=(gu_ref,dn_ref,p_out,p_g,p_q); outs=(out_gu,out_dn,out_out,out_g,out_q)
    z=[1<<b for b in range((n_dp//2).bit_length()-1)]; xb=n_dp//2
    main=[xb]+z; other=z[:1]+[xb]+z[1:]
    pieces=[dict(g=gs[k],land=land[k],fin=fin[k],out=outs[k],col=k in (0,3,4),dims=other if k in OTHER else main) for k in range(5)]
    E=Reducer(n_dp,n_s,pieces,sems,W)
    s=E.s
    greet_all(n_dp,n_s)
    greeted(n_dp,n_s)
    E.add(1); E.add(0)
    E.tick(2)
    m=middle[...]
    du,dg=norm_back(m,gain2[0:1],add_up(n_s,dpart,dland0))
    dm=dy[...].astype(f32)+du
    dmid[...]=dm
    dg2=dg
    gath[s]=dm.astype(bf16)
    g=push_all(n_s,gath,ss.at[1],rs.at[1])
    E.tick(W)
    for c in g: c.wait()
    a=push_parts(n_s,ypart,yland,ss.at[2],rs.at[2])
    rows=raw.shape[0]; D=gath.shape[2]
    dbr=gath[...].reshape(rows,D)
    dgt[...]=dotb(dbr,w_out[...],1,1)
    E.tick(1)
    p_out[...]=dotb(gated[...],dbr,0,0).astype(bf16).reshape(p_out.shape)
    E.add(2)
    n=CH; off=2*nh*DK+nh*DV
    def emit(h,c,v): draw[c*n:(c+1)*n,off+h*DV:off+(h+1)*DV]=v.astype(bf16)
    dO,gg=gate_back(raw,gain[0:1],dgt,o_ref,nh,emit)
    E.tick(1)
    p_g[...]=dotb(normed[...],draw[:,off:],0,0).astype(bf16).reshape(p_g.shape)
    E.add(3)
    res=[]
    for _ in mixer_bwd(raw,small,taps,vec,info,segr,dO,u_ref,s_ref,xi_ref,nh,P,res):
        E.tick(1)
    dsmall,g_dt,g_al=res[0]
    for coff,w,dcol,tg in res[1:]:
        draw[:,coff:coff+w]=dcol.astype(bf16)
    dsb[...]=dsmall.astype(bf16)
    p_q[...]=dotb(normed[...],draw[:,:off],0,0).astype(bf16).reshape(p_q.shape)
    E.add(4)
    E.tick(4)
    epart[...]=(dotb(draw[...],w_in[...],1,1)+dotb(dsb[...],w_sm[...],1,1)).astype(bf16).reshape(epart.shape)
    e=push_parts(n_s,epart,dland,ss.at[3],rs.at[3])
    for c in a: c.wait()
    bout[...]=(middle[...]+add_up(n_s,ypart,yland)).astype(bf16)
    psm=dotb(normed[...],dsb[...],0,0)
    E.tick(TAIL)
    for c in e: c.wait()
    du,dg=norm_back(x_ref[...].astype(f32),gain1[0:1],add_up(n_s,epart,dland))
    igrad[...]=(dmid[...]+du).astype(bf16)
    pack_small(sg,psm,res[1:],g_al,g_dt,gg,dg,dg2,s,nh,n_s)
    share_small(n_dp,n_s,sg,stot,st,rt)
    E.drain()
    shared_small(n_dp,n_s,sg,stot,st,rt)

def back(part_gu,part_dn,ypart,dpart,dland,middle,dy,x,gain2,gain1,w_out,w_in,w_sm,raw,small,taps,vec,gain,info,segr,normed,gated,O,U,S,X,n_dp,n_s,P,cid,W=4):
    ins=[part_gu,part_dn,ypart,dpart,dland,middle,dy,x,gain2,gain1,w_out,w_in,w_sm,raw,small,taps,vec,gain,info,segr,normed,gated,O,U,S,X]
    local,D=x.shape; rows=local*n_s; nh=raw.shape[1]//(2*DK+2*DV); n_hi=n_dp//2
    off=2*nh*DK+nh*DV
    shp=[part_gu.shape,part_dn.shape,(n_dp,w_out.shape[0]//n_dp,D),(n_dp,D//n_dp,nh*DV),(n_dp,D//n_dp,off)]
    col=(0,3,4)
    osh=[(n_s,q[1]//n_s,q[2]) if k in col else q[1:] for k,q in enumerate(shp)]
    S_=jax.ShapeDtypeStruct; V=pltpu.VMEM
    outs=[S_(q,bf16) for q in osh]+[S_((local,D),bf16),S_((local,D),bf16),S_((n_dp*n_s,SLICE,128),f32)]
    sc=[V((n_s-1,local,D),bf16)]*2+[V((n_s,local,D),bf16),V((rows,nh*DV),f32),V((rows,raw.shape[1]),bf16),V((rows,128),bf16),V((n_s,local,D),bf16),V((local,D),f32)]
    sc+=[V(shp[k],bf16) for k in (2,3,4)]+[V((SMALL_ROWS,128),f32)]
    sc+=[V((n_dp-1,)+q[1:],bf16) for q in shp]+[V(q,bf16) for q in osh]
    sc+=[D_((5,n_dp))]*2+[D_((5,n_s))]*2+[D_((5,))]+[D_((4,n_s))]*2+[D_((1,))]*2
    return pl.pallas_call(functools.partial(back_kernel,n_dp,n_s,nh,P,W),
        out_shape=outs,in_specs=[VM]*len(ins),out_specs=[VM]*len(outs),scratch_shapes=sc,
        compiler_params=pltpu.CompilerParams(collective_id=cid,has_side_effects=True,vmem_limit_bytes=63<<20),name="backward")(*ins)


STEP_COUNT = 10
ADAM_RATE = 0.05
BETA_ONE = 0.9
BETA_TWO = 0.95
ADAM_EPS = 1e-08
PASSES = dict(kk=3, qk=3, inv=3, u=3, s=3, o=3, g=3)


def body(
    n_dp,
    n_s,
    tokens,
    cotangent,
    query_key,
    value_gate,
    output_weight,
    gate_up,
    down_weight,
    small_params,
    momentum_query_key,
    momentum_value_gate,
    momentum_output,
    momentum_gate_up,
    momentum_down,
    moment_one,
    moment_two,
    seq_lengths,
):
    local = tokens.shape[0]
    rows = local * n_s
    packed = jnp.pad(small_params, (0, SMALL_ROWS * 128 - small_params.shape[0])).reshape(SMALL_ROWS, 128)
    (w_in, w_out, normed, raw, raw_small, gated, mixed, updates, states, inverses, middle,
     w_small, taps, vec, gain_o, gain_1, gain_2, info, segr, y_part, d_part, d_land, part_gu, part_dn) = fore(
        query_key, value_gate, gate_up, output_weight, down_weight, tokens, cotangent, packed, seq_lengths, n_dp, n_s, PASSES, 0
    )
    w_in = w_in.reshape(D, -1)
    w_out = w_out.reshape(-1, D)
    normed = normed.reshape(rows, D)
    momenta = [momentum_query_key, momentum_value_gate, momentum_output, momentum_gate_up, momentum_down]
    (g_gu, grad_dn, grad_out, g_gate, g_qkv, block_out, input_grad, small_sum) = back(
        part_gu,
        part_dn,
        y_part,
        d_part,
        d_land,
        middle,
        cotangent,
        tokens,
        gain_2,
        gain_1,
        w_out,
        w_in,
        w_small,
        raw,
        raw_small,
        taps,
        vec,
        gain_o,
        info,
        segr,
        normed,
        gated,
        mixed,
        updates,
        states,
        inverses,
        n_dp,
        n_s,
        PASSES,
        2,
    )
    landed = [g_gu, grad_dn, grad_out, g_gate, g_qkv]
    masters = [query_key, value_gate, output_weight, gate_up, down_weight]
    *orthos, small_total = muon(landed, momenta, small_sum, n_dp, n_s, 5)
    big = finish(landed, momenta, masters, orthos, n_dp * n_s)
    small_grad = small_total.reshape(-1)[: small_params.shape[0]]
    new_one = BETA_ONE * moment_one + (1.0 - BETA_ONE) * small_grad
    new_two = BETA_TWO * moment_two + (1.0 - BETA_TWO) * small_grad * small_grad
    small_step = (
        -ADAM_RATE
        * (new_one / (1.0 - BETA_ONE**STEP_COUNT))
        / (jnp.sqrt(new_two / (1.0 - BETA_TWO**STEP_COUNT)) + ADAM_EPS)
    )

    return (block_out, input_grad) + tuple(big) + (small_grad, small_step, new_one, new_two)


def solution(mesh):
    cols = P(None, ("dp", "shard"), None)
    rows = P(("dp", "shard"), None)
    weights = (cols, cols, rows, cols, rows)
    return jax.shard_map(
        functools.partial(body, mesh.shape["dp"], mesh.shape["shard"]),
        mesh=mesh,
        in_specs=(rows, rows) + weights + (P(),) + weights + (P(), P(), P("dp", None)),
        out_specs=(rows, rows) + weights * 3 + (P(),) * 4,
        check_vma=False,
    )
```
